128 devices in a mesh: slab: 32 (over x, z, core), depth: 4 (over y).
Axes of the slice: x: 4, y: 4, z: 4, core: 2. Of those that a mesh axis runs over, the one named last changes fastest.
Arguments:
- generating_displacement: float32 [3, 128, 16, 512], P(None, 'slab', 'depth'), may hold values from -0.6 to 0.6
- generating_velocity: float32 [3, 128, 16, 512], P(None, 'slab', 'depth'), may hold values from -6 to 6
- generating_memory: float32 [3, 5, 5, 5, 5, 32, 4, 128], P(None, None, None, None, None, 'slab', 'depth'), may hold values from -1.8 to 1.8
- correlation_displacement: float32 [3, 128, 16, 512], P(None, 'slab', 'depth'), may hold values from -0.6 to 0.6
- correlation_velocity: float32 [3, 128, 16, 512], P(None, 'slab', 'depth'), may hold values from -6 to 6
- correlation_memory: float32 [3, 5, 5, 5, 5, 32, 4, 128], P(None, None, None, None, None, 'slab', 'depth'), may hold values from -1.8 to 1.8
- first_lame: float32 [5, 5, 5, 32, 4, 128], P(None, None, None, 'slab', 'depth'), may hold values from 0.5 to 1.5
- shear_modulus: float32 [5, 5, 5, 32, 4, 128], P(None, None, None, 'slab', 'depth'), may hold values from 0.5 to 1
- modulus_defect: float32 [5, 5, 5, 32, 4, 128], P(None, None, None, 'slab', 'depth'), may hold values from 0.05 to 0.3
- relaxation_keep: float32 [3], replicated, may hold values from 0.5 to 0.98
- density: float32 [128, 16, 512], P('slab', 'depth'), may hold values from 0.8 to 1.6
- surface_history: float32 [64, 128, 512], P(None, 'slab', 'depth'), may hold values from -0.6 to 0.6
- node_cell: int32 [128, 512], P('slab', 'depth'), may hold values from 0 to 255
- cell_filters: float32 [256, 64], replicated, may hold values from -0.75 to 0.75
Outputs:
- generating_displacement_next: float32 [3, 128, 16, 512], P(None, 'slab', 'depth')
- generating_velocity_next: float32 [3, 128, 16, 512], P(None, 'slab', 'depth')
- generating_memory_next: float32 [3, 5, 5, 5, 5, 32, 4, 128], P(None, None, None, None, None, 'slab', 'depth')
- correlation_displacement_next: float32 [3, 128, 16, 512], P(None, 'slab', 'depth')
- correlation_velocity_next: float32 [3, 128, 16, 512], P(None, 'slab', 'depth')
- correlation_memory_next: float32 [3, 5, 5, 5, 5, 32, 4, 128], P(None, None, None, None, None, 'slab', 'depth')
The draws below stay inside these ranges and needn't reach their ends.
Inputs may be any that keep to these rules, and one draw needn't show every extreme that they name: node_cell gives each surface node's source cell.
All inputs are finite; a program needn't handle non-finite values.
Results may differ from the reference program's by a relative error of at most 0.0001.
Values sent between devices are 32-bit elements; how exact they have to be, the bound alone decides.
A program may use at most 128 MiB of HBM per device.

```python
import math
import jax
import jax.numpy as jnp
import numpy as np
from jax import lax

GLL = 5
N_SLS = 3
STEPS = 4
TAPS = 64
CELLS = 256
EZ = 128
NEX = 32
NEY = 4
NX = 128
NY = 16
NZ = 512


def touch_ends(result, rng, least, high):
    place = [jax.random.randint(jax.random.fold_in(rng, axis), (), 0, length) for axis, length in enumerate(result.shape)]
    longest = result.shape.index(max(result.shape))
    beside = place[:longest] + [(place[longest] + 1) % result.shape[longest]] + place[longest + 1:]
    return result.at[tuple(place)].set(least).at[tuple(beside)].set(high)


def shard_levels(rng, extent, shards, least, largest):
    factor_of, own = 1.0, jax.random.fold_in(rng, 6)
    for dim, shards_of in shards:
        steps = jnp.exp(jax.random.uniform(jax.random.fold_in(own, dim), (shards_of,), jnp.float32, least / len(shards), largest / len(shards)))
        factor_of = factor_of * jnp.repeat(steps, extent[dim] // shards_of).reshape([-1 if axis == dim else 1 for axis in range(len(extent))])
    return factor_of


def scatter_about(stream_key, dims, deviation, reach, split=(), held_as=jnp.bfloat16):
    gain = shard_levels(stream_key, dims, split, -0.22, 0.18) if split else 1.0
    values = jax.random.normal(stream_key, dims, jnp.float32) * deviation * gain
    return jnp.minimum(jnp.maximum(values, -reach), reach).astype(held_as)


def setup_inputs(seed: int = 0) -> dict:
    keys = jax.random.split(jax.random.key(seed), 15)
    return {
        "generating_displacement": scatter_about(keys[0], (3, NX, NY, NZ), 0.1, 0.6, ((1, 32), (2, 4)), jnp.float32),
        "generating_velocity": scatter_about(keys[1], (3, NX, NY, NZ), 1.0, 6.0, ((1, 32), (2, 4)), jnp.float32),
        "generating_memory": scatter_about(keys[2], (N_SLS, 5, GLL, GLL, GLL, NEX, NEY, EZ), 0.3, 1.8, ((5, 32), (6, 4)), jnp.float32),
        "correlation_displacement": scatter_about(keys[3], (3, NX, NY, NZ), 0.1, 0.6, ((1, 32), (2, 4)), jnp.float32),
        "correlation_velocity": scatter_about(keys[4], (3, NX, NY, NZ), 1.0, 6.0, ((1, 32), (2, 4)), jnp.float32),
        "correlation_memory": scatter_about(keys[5], (N_SLS, 5, GLL, GLL, GLL, NEX, NEY, EZ), 0.3, 1.8, ((5, 32), (6, 4)), jnp.float32),
        "first_lame": jnp.clip(0.5 + 1.0 * jax.random.uniform(keys[6], (GLL, GLL, GLL, NEX, NEY, EZ), jnp.float32) ** shard_levels(keys[6], (GLL, GLL, GLL, NEX, NEY, EZ), ((3, 32), (4, 4)), -0.2, 0.2), 0.5, 1.5),
        "shear_modulus": jnp.clip(0.5 + 0.5 * jax.random.uniform(keys[7], (GLL, GLL, GLL, NEX, NEY, EZ), jnp.float32) ** shard_levels(keys[7], (GLL, GLL, GLL, NEX, NEY, EZ), ((3, 32), (4, 4)), -0.2, 0.2), 0.5, 1.0),
        "modulus_defect": jnp.clip(jnp.exp(math.log(0.3) - 1.7917595 * jax.random.uniform(keys[8], (GLL, GLL, GLL, NEX, NEY, EZ), jnp.float32) ** shard_levels(keys[8], (GLL, GLL, GLL, NEX, NEY, EZ), ((3, 32), (4, 4)), -0.2, 0.2)), 0.05, 0.3),
        "relaxation_keep": jnp.clip(jax.random.uniform(keys[9], (N_SLS,), jnp.float32, 0.5, 0.98), 0.5, 0.98),
        "density": jnp.clip(0.8 + 0.8 * jax.random.uniform(keys[10], (NX, NY, NZ), jnp.float32) ** shard_levels(keys[10], (NX, NY, NZ), ((0, 32), (1, 4)), -0.2, 0.2), 0.8, 1.6),
        "surface_history": scatter_about(keys[11], (TAPS, NX, NZ), 0.1, 0.6, ((1, 32), (2, 4)), jnp.float32),
        "node_cell": touch_ends(jax.random.randint(keys[12], (NX, NZ), 0, CELLS), jax.random.fold_in(keys[12], 1), 0, CELLS - 1).astype(jnp.int32),
        "cell_filters": scatter_about(keys[13], (CELLS, TAPS), TAPS ** -0.5, 0.75, (), jnp.float32),
    }


time_step = 0.04
highest = lax.Precision.HIGHEST

def gll_tables():
    points = np.array([-1.0, -np.sqrt(3.0 / 7.0), 0.0, np.sqrt(3.0 / 7.0), 1.0])
    weights = np.array([0.1, 49.0 / 90.0, 32.0 / 45.0, 49.0 / 90.0, 0.1])
    number = points.shape[0]
    products = np.array([np.prod([points[target] - points[others] for others in range(number) if others != target]) for target in range(number)])
    derivative = np.zeros((number, number))
    for target in range(number):
        for source in range(number):
            if target == source:
                derivative[target, source] = np.sum([1.0 / (points[target] - points[others]) for others in range(number) if others != target])
            else:
                derivative[target, source] = products[target] / products[source] / (points[target] - points[source])
    return (derivative, weights)

def weight_table(weights_np):
    return weights_np[:, None, None] * weights_np[None, :, None] * weights_np[None, None, :]

def expand_axis(array, position, elements):
    return jnp.stack([lax.slice_in_dim(array, offset, offset + 4 * (elements - 1) + 1, stride=4, axis=position) for offset in range(5)], axis=0)

def to_local(extended):
    count_x = (extended.shape[1] - 1) // 4
    count_y = (extended.shape[2] - 1) // 4
    count_z = (extended.shape[3] - 1) // 4
    section = expand_axis(extended, 1, count_x)
    section = expand_axis(section, 3, count_y)
    section = expand_axis(section, 5, count_z)
    return jnp.transpose(section, (3, 2, 1, 0, 4, 5, 6))

def fold_axis(local, local_axis, element_axis):
    moved = jnp.moveaxis(local, (local_axis, element_axis), (0, -1))
    rest_shape = moved.shape[1:-1]
    elements = moved.shape[-1]
    blank = jnp.zeros_like(moved[0])
    leading = jnp.stack([moved[0], moved[1], moved[2], moved[3]], axis=-1).reshape(rest_shape + (4 * elements,))
    trailing = jnp.stack([moved[4], blank, blank, blank], axis=-1).reshape(rest_shape + (4 * elements,))
    pad_one = jnp.zeros(rest_shape + (1,), jnp.float32)
    pad_four = jnp.zeros(rest_shape + (4,), jnp.float32)
    return jnp.concatenate([leading, pad_one], axis=-1) + jnp.concatenate([pad_four, trailing[..., :4 * elements - 3]], axis=-1)

def from_local(local_force):
    section = fold_axis(local_force, 3, 6)
    section = fold_axis(section, 2, 4)
    section = fold_axis(section, 1, 2)
    return jnp.transpose(section, (0, 3, 2, 1))

def element_force(local_disp, memory, first_lame, shear_modulus, modulus_defect, relaxation_keep, derivative, weight_cube):
    grad_x = jnp.einsum('pq,iqbcxyz->ipbcxyz', derivative, local_disp, precision=highest)
    grad_y = jnp.einsum('pq,iaqcxyz->iapcxyz', derivative, local_disp, precision=highest)
    grad_z = jnp.einsum('pq,iabqxyz->iabpxyz', derivative, local_disp, precision=highest)
    strain_xx = grad_x[0]
    strain_yy = grad_y[1]
    strain_zz = grad_z[2]
    strain_xy = 0.5 * (grad_y[0] + grad_x[1])
    strain_xz = 0.5 * (grad_z[0] + grad_x[2])
    strain_yz = 0.5 * (grad_z[1] + grad_y[2])
    volume_strain = strain_xx + strain_yy + strain_zz
    deviator = jnp.stack([strain_xx - volume_strain / 3.0, strain_yy - volume_strain / 3.0, strain_xy, strain_xz, strain_yz])
    relaxed = lax.optimization_barrier(jnp.sum(memory, axis=0))
    double_shear = 2.0 * shear_modulus
    pressure = first_lame * volume_strain
    stress_xx = pressure + double_shear * strain_xx - relaxed[0]
    stress_yy = pressure + double_shear * strain_yy - relaxed[1]
    stress_zz = pressure + double_shear * strain_zz + relaxed[0] + relaxed[1]
    stress_xy = double_shear * strain_xy - relaxed[2]
    stress_xz = double_shear * strain_xz - relaxed[3]
    stress_yz = double_shear * strain_yz - relaxed[4]
    flux_x = weight_cube * jnp.stack([stress_xx, stress_xy, stress_xz])
    flux_y = weight_cube * jnp.stack([stress_xy, stress_yy, stress_yz])
    flux_z = weight_cube * jnp.stack([stress_xz, stress_yz, stress_zz])
    local_force = jnp.einsum('pq,ipbcxyz->iqbcxyz', derivative, flux_x, precision=highest)
    local_force = local_force + jnp.einsum('pq,iapcxyz->iaqcxyz', derivative, flux_y, precision=highest)
    local_force = local_force + jnp.einsum('pq,iabpxyz->iabqxyz', derivative, flux_z, precision=highest)
    retention = relaxation_keep.reshape((-1, 1, 1, 1, 1, 1, 1, 1))
    memory_next = retention * memory + (1.0 - retention) * (modulus_defect * double_shear * deviator)[None]
    return (local_force, memory_next)

def node_weights(length, first_index, free_top):
    global_index = first_index + jnp.arange(length, dtype=jnp.int32)
    residue = global_index % 4
    values = jnp.where(residue == 0, 0.2, jnp.where(residue == 2, 32.0 / 45.0, 49.0 / 90.0))
    if free_top:
        values = jnp.where(global_index == 0, 0.1, values)
    return values.astype(jnp.float32)

def stiffness(displacement, memory, material):
    nodes_x, nodes_y, nodes_z = displacement.shape[1:]
    extended = jnp.concatenate([displacement, displacement[:, :1]], axis=1)
    extended = jnp.concatenate([extended, jnp.zeros_like(extended[:, :, :1])], axis=2)
    extended = jnp.concatenate([extended, extended[:, :, :, :1]], axis=3)
    local_force, memory_next = element_force(to_local(extended), memory, *material)
    assembled = from_local(local_force)
    assembled = assembled[:, :, :nodes_y]
    assembled = assembled[:, :nodes_x].at[:, 0].add(assembled[:, nodes_x])
    assembled = assembled[..., :nodes_z].at[..., 0].add(assembled[..., nodes_z])
    return (assembled, memory_next)

def reference(generating_displacement, generating_velocity, generating_memory, correlation_displacement, correlation_velocity, correlation_memory, first_lame, shear_modulus, modulus_defect, relaxation_keep, density, surface_history, node_cell, cell_filters):
    derivative_np, weights_np = gll_tables()
    derivative = jnp.asarray(derivative_np, jnp.float32)
    weight_cube = jnp.asarray(weight_table(weights_np)[:, :, :, None, None, None], jnp.float32)
    material = (first_lame, shear_modulus, modulus_defect, relaxation_keep, derivative, weight_cube)
    nodes_x, nodes_y, nodes_z = density.shape
    nodal_mass = density * node_weights(nodes_x, 0, False)[:, None, None] * node_weights(nodes_y, 0, True)[None, :, None] * node_weights(nodes_z, 0, False)[None, None, :]

    def advance(displacement, velocity, memory, surface_force):
        internal, memory = stiffness(displacement, memory, material)
        external = jnp.zeros_like(displacement).at[1, :, 0, :].set(surface_force)
        velocity = velocity + time_step * (external - internal) / nodal_mass
        displacement = displacement + time_step * velocity
        return (displacement, velocity, memory)
    displacement, velocity, memory = (generating_displacement, generating_velocity, generating_memory)
    silent = jnp.zeros((nodes_x, nodes_z), jnp.float32)
    samples = []
    for step_index in range(STEPS):
        displacement, velocity, memory = advance(displacement, velocity, memory, silent)
        samples.append(displacement[1, :, 0, :])
    generated = (displacement, velocity, memory)
    window = jnp.concatenate([surface_history, jnp.stack(samples)], axis=0)
    taps = jnp.moveaxis(jnp.take(cell_filters, node_cell, axis=0), 2, 0)
    forcing = [lax.optimization_barrier(jnp.sum(taps * window[lag + 1:lag + 1 + TAPS], axis=0)) for lag in range(STEPS)]
    displacement, velocity, memory = (correlation_displacement, correlation_velocity, correlation_memory)
    for step_index in range(STEPS):
        displacement, velocity, memory = advance(displacement, velocity, memory, forcing[step_index])
    return (generated[0], generated[1], generated[2], displacement, velocity, memory)
```

```python
import functools

import jax
import jax.numpy as jnp
import ml_dtypes
import numpy as np
from jax import lax
from jax.experimental import pallas as pl
from jax.experimental.pallas import tpu as pltpu
from jax.sharding import PartitionSpec as P

STEPS = 4
TAPS = 64
DT = 0.04
F32 = jnp.float32
BF16 = jnp.bfloat16
MESH = pl.DeviceIdType.MESH

DISP = (0, 3)
VEL = (6, 9)
RHO = 12
SLOTS = 13


def gll_tables():
    points = np.array([-1.0, -np.sqrt(3.0 / 7.0), 0.0, np.sqrt(3.0 / 7.0), 1.0])
    weights = np.array([0.1, 49.0 / 90.0, 32.0 / 45.0, 49.0 / 90.0, 0.1])
    products = np.array([np.prod([points[t] - points[o] for o in range(5) if o != t]) for t in range(5)])
    derivative = np.zeros((5, 5))
    for t in range(5):
        for s in range(5):
            if t == s:
                derivative[t, s] = np.sum([1.0 / (points[t] - points[o]) for o in range(5) if o != t])
            else:
                derivative[t, s] = products[t] / products[s] / (points[t] - points[s])
    return derivative, weights


DMAT, WGLL = gll_tables()


def node_row(b, c):
    return c * 5 + b if c < 4 else 24 + b


def halves(matrix):
    high = matrix.astype(ml_dtypes.bfloat16)
    low = (matrix - high.astype(np.float64)).astype(ml_dtypes.bfloat16)
    return high, low


def operators():
    same = np.zeros((32, 32))
    along_y = np.zeros((32, 32))
    along_z = np.zeros((32, 32))
    for b in range(5):
        for c in range(5):
            row = b * 5 + c
            same[row, node_row(b, c)] = 1.0
            for q in range(5):
                along_y[row, node_row(q, c)] = DMAT[b, q]
                along_z[row, node_row(b, q)] = DMAT[c, q]
    high, low = halves(np.concatenate([same, along_y, along_z], axis=0))
    gradient = np.concatenate([high, high, low], axis=1)
    y_high, y_low = halves(along_y.T)
    z_high, z_low = halves(along_z.T)
    back = same.T.astype(ml_dtypes.bfloat16)
    force = np.concatenate([y_high, z_high, y_high, z_high, y_low, z_low, back, back], axis=1)
    return gradient, force


def tables():
    table = np.zeros((5, 32, 128), np.float32)
    wn = np.array([0.2, 49.0 / 90.0, 32.0 / 45.0, 49.0 / 90.0, 0.2])
    for b in range(5):
        for c in range(5):
            table[0, b * 5 + c] = WGLL[b] * WGLL[c]
        for c in range(4):
            row = node_row(b, c)
            table[1, row] = 1.0 / (wn[b] * wn[c])
            table[2, row] = float(b == 0)
            table[3, row] = float(b == 4)
    table[4, 20:] = 1.0
    return table


def interleave():
    table = np.zeros((512, 512), np.float32)
    for c in range(4):
        for e in range(128):
            table[4 * e + c, c * 128 + e] = 1.0
    return table.astype(ml_dtypes.bfloat16)


def split2(x):
    high = x.astype(BF16)
    return high, (x - high.astype(F32)).astype(BF16)


def split3(x):
    high = x.astype(BF16)
    rest = x - high.astype(F32)
    middle = rest.astype(BF16)
    return high, middle, (rest - middle.astype(F32)).astype(BF16)


def derive(x, matrix):
    even = [x[0] + x[4], x[1] + x[3]]
    odd = [x[0] - x[4], x[1] - x[3]]
    out = [None] * 5
    for p in range(2):
        s = sum(float(0.5 * (matrix[p, q] - matrix[p, 4 - q])) * odd[q] for q in range(2))
        t = sum(float(0.5 * (matrix[p, q] + matrix[p, 4 - q])) * even[q] for q in range(2))
        t = t + float(matrix[p, 2]) * x[2]
        out[p] = s + t
        out[4 - p] = s - t
    out[2] = sum(float(matrix[2, q]) * odd[q] for q in range(2))
    return out


def kernel(
    ug, vg, rg, uc, vc, rc, lam, mu, defect, keep, rho, hist, cells, filt, perm, opg, opf, table,
    ug_o, vg_o, rg_o, uc_o, vc_o, rc_o,
    pair_u, pair_v, pair_r, perm_v, opg_v, opf_v, tab_v,
    mem, sw, qs, lam_v, mu_v, def_v, inv_mass,
    nd, ft, fs, yp, ym, rxm, rxp, rym, ryp, rdg,
    hy1, hy2, ry1, ry2, rc1, rc2,
    hist_v, cells_v, filt_v, fg_own, fgb, fgn, sj, frc,
    xr, out_v,
    lsem, osem, h_send, h_recv, f_send, f_recv, g_send, g_recv,
):
    s = lax.axis_index("slab")
    d = lax.axis_index("depth")
    ns = lax.axis_size("slab")
    nd_ = lax.axis_size("depth")
    sp, sm = lax.rem(s + 1, ns), lax.rem(s + ns - 1, ns)
    dp, dm = lax.rem(d + 1, nd_), lax.rem(d + nd_ - 1, nd_)

    barrier = pltpu.get_barrier_semaphore()
    peers = 0
    for ps in (s, sm, sp):
        for k in range(4):
            if ps is s and k == 0:
                continue
            pl.semaphore_signal(
                barrier, inc=1, device_id=(ps, lax.rem(d + k, nd_)), device_id_type=MESH
            )
            peers += 1

    loads = []

    def load(src, dst):
        copy = pltpu.make_async_copy(src, dst, lsem.at[len(loads)])
        copy.start()
        loads.append(copy)
        return copy

    l_ug = load(ug, pair_u.at[:, 0:4])
    l_uc = load(uc, pair_u.at[:, 4:8])
    l_perm = load(perm, perm_v)
    l_opg = load(opg, opg_v)
    l_tab = load(table, tab_v)
    l_vg = load(vg, pair_v.at[:, 0:4])
    l_vc = load(vc, pair_v.at[:, 4:8])
    l_rho = load(rho, pair_r.at[:, 0:4])
    l_opf = load(opf, opf_v)
    zero7 = jnp.zeros((7, 128), F32)
    for w in range(2):
        for k in range(75):
            mem[w, k, 25:32, :] = zero7
    for a in range(5):
        lam_v[a, 25:32, :] = zero7
        mu_v[a, 25:32, :] = zero7
        def_v[a, 25:32, :] = zero7
    for x in range(4):
        hist_v[x, 64:72, :] = jnp.zeros((8, 128), F32)
    l_lam = load(lam.at[:, :, 0], lam_v.at[:, 0:25])
    l_mu = load(mu.at[:, :, 0], mu_v.at[:, 0:25])
    l_rg = load(rg.at[:, :, 0], mem.at[0, :, 0:25])
    l_def = load(defect.at[:, :, 0], def_v.at[:, 0:25])
    l_cells = load(cells, cells_v)
    l_filt = load(filt, filt_v)
    l_hist = [load(hist.at[:, x], hist_v.at[x, 0:64]) for x in range(4)]
    l_rc = load(rc.at[:, :, 0], mem.at[1, :, 0:25])

    zero24 = jnp.zeros((24, 128), F32)
    for a in range(4):
        for k in range(SLOTS):
            nd[a, k] = zero24
    for q in range(8):
        fgn[pl.ds(q * 24, 24), :] = zero24

    def deinterleave(ref, blocks):
        rows = blocks * 8
        x = ref[...].reshape(rows, 512)
        y = jnp.dot(jnp.concatenate(split3(x), axis=0), perm_v[...], preferred_element_type=F32)
        return y[0:rows] + y[rows : 2 * rows] + y[2 * rows : 3 * rows]

    l_perm.wait()
    l_ug.wait()
    l_uc.wait()
    y = deinterleave(pair_u, 12)
    for k in range(12):
        for c in range(4):
            lanes = slice(c * 128, c * 128 + 128)
            nd[k % 4, DISP[0] + k // 4, c * 5 : c * 5 + 4, :] = y[k * 8 : k * 8 + 4, lanes]
            nd[k % 4, DISP[1] + k // 4, c * 5 : c * 5 + 4, :] = y[k * 8 + 4 : k * 8 + 8, lanes]
    for a in range(4):
        for k in range(3):
            hy1[a * 12 + k * 4 : a * 12 + k * 4 + 4, :] = nd[a, k, pl.ds(0, 4, stride=5), :]

    pl.semaphore_wait(barrier, peers)

    def remote(src, dst, send, recv, target):
        return pltpu.make_async_remote_copy(
            src_ref=src, dst_ref=dst, send_sem=send, recv_sem=recv, device_id=target, device_id_type=MESH
        )

    h1 = [
        remote(hy1, ry1, h_send.at[0], h_recv.at[0], (s, dm)),
        remote(nd.at[0, 0:3], nd.at[4, 0:3], h_send.at[1], h_recv.at[1], (sm, d)),
        remote(hy1.at[0:16], rc1, h_send.at[2], h_recv.at[2], (sm, dm)),
    ]
    for copy in h1:
        copy.start()

    l_vg.wait()
    l_vc.wait()
    l_rho.wait()
    y = deinterleave(pair_v, 12)
    for k in range(12):
        for c in range(4):
            lanes = slice(c * 128, c * 128 + 128)
            nd[k % 4, VEL[0] + k // 4, c * 5 : c * 5 + 4, :] = y[k * 8 : k * 8 + 4, lanes]
            nd[k % 4, VEL[1] + k // 4, c * 5 : c * 5 + 4, :] = y[k * 8 + 4 : k * 8 + 8, lanes]
    y = deinterleave(pair_r, 4)
    for k in range(4):
        for c in range(4):
            nd[k, RHO, c * 5 : c * 5 + 4, :] = y[k * 8 : k * 8 + 4, c * 128 : c * 128 + 128]
    for a in range(4):
        for k in range(10):
            row = a * 40 + k * 4
            hy2[row : row + 4, :] = nd[a, 3 + k, pl.ds(0, 4, stride=5), :]
    h2 = [
        remote(hy2, ry2, h_send.at[3], h_recv.at[3], (s, dm)),
        remote(nd.at[0, 3:13], nd.at[4, 3:13], h_send.at[4], h_recv.at[4], (sm, d)),
        remote(hy2.at[0:40], rc2, h_send.at[5], h_recv.at[5], (sm, dm)),
    ]
    for copy in h2:
        copy.start()

    l_tab.wait()
    l_lam.wait()
    l_mu.wait()
    l_def.wait()
    weight_bc = tab_v[0]
    for a in range(5):
        weight = weight_bc * float(WGLL[a])
        two_mu = 2.0 * mu_v[a]
        lam_v[a] = weight * lam_v[a]
        mu_v[a] = weight * two_mu
        def_v[a] = two_mu * def_v[a]

    def relaxed(w):
        for a in range(5):
            weight = weight_bc * float(WGLL[a])
            for k in range(5):
                j = k * 5 + a
                sw[w, j] = weight * (mem[w, j] + mem[w, 25 + j] + mem[w, 50 + j])

    l_rg.wait()
    relaxed(0)

    l_cells.wait()
    l_filt.wait()
    for copy in l_hist:
        copy.wait()
    filt3 = jnp.concatenate(split3(filt_v[...]), axis=0)
    ids = lax.broadcasted_iota(jnp.int32, (256, 128), 0)
    for x in range(4):
        one_hot = jnp.where(ids == cells_v[x : x + 1, :], 1.0, 0.0).astype(BF16)
        g = jnp.dot(filt3, one_hot, preferred_element_type=F32)
        g = g[0:64] + g[64:128] + g[128:192]
        for t in range(4):
            fg_own[x * 8 + t : x * 8 + t + 1, :] = jnp.sum(
                g * hist_v[x, t + 1 : t + 65, :], axis=0, keepdims=True
            )
            fg_own[x * 8 + 4 + t : x * 8 + 5 + t, :] = g[63 - t : 64 - t]
    far = remote(fg_own.at[0:8], fgb.at[d, 32:40], g_send.at[0], g_recv.at[4 + d], (sm, 0))
    far.start()

    @pl.when(d != 0)
    def _():
        remote(fg_own, fgb.at[d, 0:32], g_send.at[1], g_recv.at[d], (s, 0)).start()

    def strain_stress_force(w, t):
        opg_m = opg_v[...]
        comps = []
        for i in range(3):
            columns = []
            for a in range(5):
                u = nd[a, DISP[w] + i]
                u = jnp.concatenate([u, pltpu.roll(u[0:8], 127, 1)], axis=0)
                high, low = split2(u)
                columns.append(jnp.concatenate([high, low, high], axis=0))
            g = jnp.dot(opg_m, jnp.concatenate(columns, axis=1), preferred_element_type=F32)
            lanes = [slice(a * 128, a * 128 + 128) for a in range(5)]
            gx = derive([g[0:32, l] for l in lanes], DMAT)
            comps.append((gx, [g[32:64, l] for l in lanes], [g[64:96, l] for l in lanes]))
        fluxes = []
        for a in range(5):
            gx = [comps[i][0][a] for i in range(3)]
            gy = [comps[i][1][a] for i in range(3)]
            gz = [comps[i][2][a] for i in range(3)]
            xy = 0.5 * (gy[0] + gx[1])
            xz = 0.5 * (gz[0] + gx[2])
            yz = 0.5 * (gz[1] + gy[2])
            trace = gx[0] + gy[1] + gz[2]
            third = trace * (1.0 / 3.0)
            m, q = mu_v[a], def_v[a]
            for k, e in enumerate((gx[0] - third, gy[1] - third, xy, xz, yz)):
                qs[w, k * 5 + a] = q * e
            pressure = lam_v[a] * trace
            r = [sw[w, k * 5 + a] for k in range(5)]
            sxx = pressure + m * gx[0] - r[0]
            syy = pressure + m * gy[1] - r[1]
            szz = pressure + m * gz[2] + (r[0] + r[1])
            sxy = m * xy - r[2]
            sxz = m * xz - r[3]
            syz = m * yz - r[4]
            fluxes.append(((sxx, sxy, sxz), (sxy, syy, syz), (sxz, syz, szz)))
        opf_m = opf_v[...]
        for i in range(3):
            fx = derive([fluxes[a][0][i] for a in range(5)], DMAT.T)
            columns = []
            for a in range(5):
                y_high, y_low = split2(fluxes[a][1][i])
                z_high, z_low = split2(fluxes[a][2][i])
                x_high, x_low = split2(fx[a])
                columns.append(
                    jnp.concatenate([y_high, z_high, y_low, z_low, y_high, z_high, x_high, x_low], axis=0)
                )
            f = jnp.dot(opf_m, jnp.concatenate(columns, axis=1), preferred_element_type=F32)
            for a in range(5):
                fa = f[:, a * 128 : a * 128 + 128]
                fs[w, t, a, i, 0:8, :] = fa[0:8] + pltpu.roll(fa[24:32], 1, 1)
                fs[w, t, a, i, 8:24, :] = fa[8:24]

    below = (d < nd_ - 1).astype(F32)

    def messages(w, t):
        n = w * STEPS + t
        sends = [
            (ym.at[n], rym.at[n], (s, dm)),
            (yp.at[n], ryp.at[n], (s, dp)),
            (ym.at[n, 0:16], rdg.at[n, 0], (sm, dm)),
            (yp.at[n, 0:16], rdg.at[n, 1], (sm, dp)),
            (ym.at[n, 48:64], rdg.at[n, 2], (sp, dm)),
            (yp.at[n, 48:64], rdg.at[n, 3], (sp, dp)),
            (fs.at[w, t, 0], rxm.at[n], (sm, d)),
            (fs.at[w, t, 4], rxp.at[n], (sp, d)),
        ]
        return [
            remote(src, dst, f_send.at[n, j], f_recv.at[n, j], target)
            for j, (src, dst, target) in enumerate(sends)
        ]

    def send(w, t):
        n = w * STEPS + t
        for a in range(5):
            for i in range(3):
                row = a * 12 + i * 4
                ym[n, row : row + 4, :] = fs[w, t, a, i, pl.ds(0, 4, stride=5), :]
                yp[n, row : row + 4, :] = below * fs[w, t, a, i, pl.ds(4, 4, stride=5), :]
        ym[n, 60:64, :] = jnp.zeros((4, 128), F32)
        yp[n, 60:64, :] = jnp.zeros((4, 128), F32)
        for copy in messages(w, t):
            copy.start()

    kept = [keep[l] for l in range(3)]

    def memory(w, last):
        for a in range(5):
            weight = weight_bc * float(WGLL[a])
            for k in range(5):
                j = k * 5 + a
                q = qs[w, j]
                new = []
                for l in range(3):
                    value = kept[l] * mem[w, 25 * l + j] + (1.0 - kept[l]) * q
                    mem[w, 25 * l + j] = value
                    new.append(value)
                if not last:
                    sw[w, j] = weight * (new[0] + new[1] + new[2])

    def receive(w, t):
        n = w * STEPS + t
        for copy in messages(w, t):
            copy.wait_recv()
        for a in range(5):
            for i in range(3):
                f = fs[w, t, a, i]
                if a == 0:
                    f = f + rxp[n, i]
                if a == 4:
                    f = f + rxm[n, i]
                ft[a, i] = f
        for a in range(5):
            for i in range(3):
                row = a * 12 + i * 4
                low = ryp[n, row : row + 4, :]
                top = rym[n, row : row + 4, :]
                if a == 4:
                    low = low + rdg[n, 1, i * 4 : i * 4 + 4, :]
                    top = top + rdg[n, 0, i * 4 : i * 4 + 4, :]
                if a == 0:
                    low = low + rdg[n, 3, i * 4 : i * 4 + 4, :]
                    top = top + rdg[n, 2, i * 4 : i * 4 + 4, :]
                if w == 1 and i == 1:
                    low = low - frc[a * 4 : a * 4 + 4, :]
                at_low = (a, i, pl.ds(0, 4, stride=5), slice(None))
                at_top = (a, i, pl.ds(4, 4, stride=5), slice(None))
                ft[at_low] = ft[at_low] + low
                ft[at_top] = ft[at_top] + top

    def update(w):
        for a in range(5):
            scale = inv_mass[a]
            for i in range(3):
                v = nd[a, VEL[w] + i] - scale * ft[a, i]
                nd[a, VEL[w] + i] = v
                nd[a, DISP[w] + i] = nd[a, DISP[w] + i] + DT * v

    def sample(t):
        for a in range(5):
            sj[t, a * 4 : a * 4 + 4, :] = nd[a, DISP[0] + 1, pl.ds(0, 4, stride=5), :]

    def forcing(t):
        f = fgn[t * 24 : t * 24 + 24, :]
        for m in range(t + 1):
            f = f + fgn[(4 + m) * 24 : (5 + m) * 24, :] * sj[t - m]
        frc[...] = f

    for copy in h1:
        copy.wait()
    for a in range(4):
        for k in range(3):
            row = a * 12 + k * 4
            nd[a, k, pl.ds(4, 4, stride=5), :] = below * ry1[row : row + 4, :]
    for k in range(3):
        nd[4, k, pl.ds(4, 4, stride=5), :] = below * rc1[k * 4 : k * 4 + 4, :]
    l_opg.wait()
    l_opf.wait()
    strain_stress_force(0, 0)
    send(0, 0)

    l_rc.wait()
    relaxed(1)
    for copy in h2:
        copy.wait()
    for a in range(4):
        for k in range(10):
            row = a * 40 + k * 4
            top = ry2[row : row + 4, :]
            nd[a, 3 + k, pl.ds(4, 4, stride=5), :] = top if k == 9 else below * top
    for k in range(10):
        top = rc2[k * 4 : k * 4 + 4, :]
        nd[4, 3 + k, pl.ds(4, 4, stride=5), :] = top if k == 9 else below * top
    strain_stress_force(1, 0)
    send(1, 0)
    memory(0, False)
    first = (d == 0).astype(F32)
    row_factor = tab_v[1, 0:24] * (1.0 + first * tab_v[2, 0:24] - (1.0 - below) * tab_v[3, 0:24])
    for a in range(5):
        wx = float([0.2, 49.0 / 90.0, 32.0 / 45.0, 49.0 / 90.0, 0.2][a])
        inv_mass[a] = (DT / wx) * row_factor / (nd[a, RHO] + tab_v[4, 0:24])

    @pl.when(d == 0)
    def _():
        for j in range(1, 4):
            remote(fg_own, fgb.at[j, 0:32], g_send.at[1], g_recv.at[j], (s, 0)).wait_recv()
        for j in range(4):
            remote(fg_own.at[0:8], fgb.at[j, 32:40], g_send.at[0], g_recv.at[4 + j], (sm, 0)).wait_recv()
        fgb[0, 0:32, :] = fg_own[...]
        x = jnp.concatenate([fgb[j] for j in range(4)], axis=1)
        y = jnp.dot(jnp.concatenate(split3(x), axis=0), perm_v[...], preferred_element_type=F32)
        y = y[0:40] + y[40:80] + y[80:120]
        for a in range(5):
            for c in range(4):
                fgn[pl.ds(a * 4 + c, 8, stride=24), :] = y[a * 8 : a * 8 + 8, c * 128 : c * 128 + 128]

    far.wait_send()

    @pl.when(d != 0)
    def _():
        remote(fg_own, fgb.at[d, 0:32], g_send.at[1], g_recv.at[d], (s, 0)).wait_send()

    memory(1, False)

    stores = []

    def store(src, dst):
        copy = pltpu.make_async_copy(src, dst, osem.at[len(stores)])
        copy.start()
        stores.append(copy)

    def finish(w, u_out, v_out):
        for i in range(3):
            for x in range(4):
                row = (i * 4 + x) * 8
                for c in range(4):
                    xr[c, row : row + 4, :] = nd[x, DISP[w] + i, c * 5 : c * 5 + 4, :]
                    xr[c, row + 4 : row + 8, :] = nd[x, VEL[w] + i, c * 5 : c * 5 + 4, :]
        x = jnp.concatenate([xr[c] for c in range(4)], axis=1)
        y = lax.dot_general(
            jnp.concatenate(split3(x), axis=0), perm_v[...], (((1,), (1,)), ((), ())),
            preferred_element_type=F32,
        )
        out_v[w] = (y[0:96] + y[96:192] + y[192:288]).reshape(12, 8, 512)
        store(out_v.at[w, :, 0:4], u_out)
        store(out_v.at[w, :, 4:8], v_out)

    for t in range(STEPS):
        receive(0, t)
        update(0)
        sample(t)
        forcing(t)
        if t < STEPS - 1:
            strain_stress_force(0, t + 1)
            send(0, t + 1)
            if t > 0:
                memory(1, False)
        else:
            memory(1, True)
            store(mem.at[1, :, 0:25], rc_o.at[:, :, 0])
            finish(0, ug_o, vg_o)
        receive(1, t)
        update(1)
        if t < STEPS - 1:
            strain_stress_force(1, t + 1)
            send(1, t + 1)
            memory(0, t == STEPS - 2)
            if t == STEPS - 2:
                store(mem.at[0, :, 0:25], rg_o.at[:, :, 0])
        else:
            finish(1, uc_o, vc_o)
    for w in range(2):
        for t in range(STEPS):
            for copy in messages(w, t):
                copy.wait_send()
    for copy in stores:
        copy.wait()


def body(*args):
    (ug, vg, rg, uc, vc, rc, lam, mu, defect, keep, rho, hist, cells, filt) = args
    gradient, force = operators()
    operands = (
        ug.reshape(12, 4, 512), vg.reshape(12, 4, 512), rg.reshape(75, 25, 1, 128),
        uc.reshape(12, 4, 512), vc.reshape(12, 4, 512), rc.reshape(75, 25, 1, 128),
        lam.reshape(5, 25, 1, 128), mu.reshape(5, 25, 1, 128), defect.reshape(5, 25, 1, 128),
        keep, rho, hist, cells, filt.T,
        jnp.asarray(interleave()), jnp.asarray(gradient), jnp.asarray(force), jnp.asarray(tables()),
    )
    anywhere = pl.BlockSpec(memory_space=pl.ANY)
    in_specs = [anywhere] * len(operands)
    in_specs[9] = pl.BlockSpec(memory_space=pltpu.SMEM)
    nodal = jax.ShapeDtypeStruct((12, 4, 512), F32)
    points = jax.ShapeDtypeStruct((75, 25, 1, 128), F32)
    dma = pltpu.SemaphoreType.DMA
    vm = lambda *shape: pltpu.VMEM(shape, F32)
    waves = 2 * STEPS
    outs = pl.pallas_call(
        kernel,
        out_shape=(nodal, nodal, points, nodal, nodal, points),
        in_specs=in_specs,
        out_specs=(anywhere,) * 6,
        scratch_shapes=[
            vm(12, 8, 512), vm(12, 8, 512), vm(4, 8, 512),
            pltpu.VMEM((512, 512), BF16), pltpu.VMEM((96, 96), BF16), pltpu.VMEM((32, 256), BF16),
            vm(5, 32, 128),
            vm(2, 75, 32, 128), vm(2, 25, 32, 128), vm(2, 25, 32, 128),
            vm(5, 32, 128), vm(5, 32, 128), vm(5, 32, 128), vm(5, 24, 128),
            vm(5, SLOTS, 24, 128), vm(5, 3, 24, 128), vm(2, STEPS, 5, 3, 24, 128),
            vm(waves, 64, 128), vm(waves, 64, 128),
            vm(waves, 3, 24, 128), vm(waves, 3, 24, 128),
            vm(waves, 64, 128), vm(waves, 64, 128), vm(waves, 4, 16, 128),
            vm(48, 128), vm(160, 128), vm(48, 128), vm(160, 128), vm(16, 128), vm(40, 128),
            vm(4, 72, 128), pltpu.VMEM((4, 128), jnp.int32), vm(64, 256),
            vm(32, 128), vm(4, 40, 128), vm(192, 128), vm(STEPS, 24, 128), vm(24, 128),
            vm(4, 96, 128), vm(2, 12, 8, 512),
            dma((24,)), dma((6,)), dma((6,)), dma((6,)), dma((waves, 8)), dma((waves, 8)),
            dma((2,)), dma((8,)),
        ],
        compiler_params=pltpu.CompilerParams(
            collective_id=0, has_side_effects=True, vmem_limit_bytes=40 * 1024 * 1024
        ),
    )(*operands)
    full = (3, 5, 5, 5, 5, 1, 1, 128)
    u = (3, 4, 4, 512)
    return (
        outs[0].reshape(u), outs[1].reshape(u), outs[2].reshape(full),
        outs[3].reshape(u), outs[4].reshape(u), outs[5].reshape(full),
    )


def solution(mesh):
    nodal = P(None, "slab", "depth", None)
    points = P(None, None, None, None, None, "slab", "depth", None)
    material = P(None, None, None, "slab", "depth", None)
    return jax.shard_map(
        body,
        mesh=mesh,
        in_specs=(
            nodal, nodal, points, nodal, nodal, points, material, material, material, P(),
            P("slab", "depth", None), P(None, "slab", "depth"), P("slab", "depth"), P(),
        ),
        out_specs=(nodal, nodal, points, nodal, nodal, points),
        check_vma=False,
    )
```

```python
import functools

import jax
import jax.numpy as jnp
import ml_dtypes
import numpy as np
from jax import lax
from jax.experimental import pallas as pl
from jax.experimental.pallas import tpu as pltpu
from jax.sharding import PartitionSpec as P

STEPS = 4
TAPS = 64
DT = 0.04
F32 = jnp.float32
BF16 = jnp.bfloat16
MESH = pl.DeviceIdType.MESH

DISP = (0, 3)
VEL = (6, 9)
RHO = 12
SLOTS = 13


def gll_tables():
    points = np.array([-1.0, -np.sqrt(3.0 / 7.0), 0.0, np.sqrt(3.0 / 7.0), 1.0])
    weights = np.array([0.1, 49.0 / 90.0, 32.0 / 45.0, 49.0 / 90.0, 0.1])
    products = np.array([np.prod([points[t] - points[o] for o in range(5) if o != t]) for t in range(5)])
    derivative = np.zeros((5, 5))
    for t in range(5):
        for s in range(5):
            if t == s:
                derivative[t, s] = np.sum([1.0 / (points[t] - points[o]) for o in range(5) if o != t])
            else:
                derivative[t, s] = products[t] / products[s] / (points[t] - points[s])
    return derivative, weights


DMAT, WGLL = gll_tables()


def node_row(b, c):
    return c * 5 + b if c < 4 else 24 + b


def halves(matrix):
    high = matrix.astype(ml_dtypes.bfloat16)
    low = (matrix - high.astype(np.float64)).astype(ml_dtypes.bfloat16)
    return high, low


def operators():
    same = np.zeros((32, 32))
    along_y = np.zeros((32, 32))
    along_z = np.zeros((32, 32))
    for b in range(5):
        for c in range(5):
            row = b * 5 + c
            same[row, node_row(b, c)] = 1.0
            for q in range(5):
                along_y[row, node_row(q, c)] = DMAT[b, q]
                along_z[row, node_row(b, q)] = DMAT[c, q]
    high, low = halves(np.concatenate([same, along_y, along_z], axis=0))
    gradient = np.concatenate([high, high, low], axis=1)
    y_high, y_low = halves(along_y.T)
    z_high, z_low = halves(along_z.T)
    back = same.T.astype(ml_dtypes.bfloat16)
    force = np.concatenate([y_high, z_high, y_high, z_high, y_low, z_low, back, back], axis=1)
    return gradient, force


def tables():
    table = np.zeros((5, 32, 128), np.float32)
    wn = np.array([0.2, 49.0 / 90.0, 32.0 / 45.0, 49.0 / 90.0, 0.2])
    for b in range(5):
        for c in range(5):
            table[0, b * 5 + c] = WGLL[b] * WGLL[c]
        for c in range(4):
            row = node_row(b, c)
            table[1, row] = 1.0 / (wn[b] * wn[c])
            table[2, row] = float(b == 0)
            table[3, row] = float(b == 4)
    table[4, 20:] = 1.0
    return table


def interleave():
    table = np.zeros((512, 512), np.float32)
    for c in range(4):
        for e in range(128):
            table[4 * e + c, c * 128 + e] = 1.0
    return table.astype(ml_dtypes.bfloat16)


def split2(x):
    high = x.astype(BF16)
    return high, (x - high.astype(F32)).astype(BF16)


def split3(x):
    high = x.astype(BF16)
    rest = x - high.astype(F32)
    middle = rest.astype(BF16)
    return high, middle, (rest - middle.astype(F32)).astype(BF16)


def derive(x, matrix):
    even = [x[0] + x[4], x[1] + x[3]]
    odd = [x[0] - x[4], x[1] - x[3]]
    out = [None] * 5
    for p in range(2):
        s = sum(float(0.5 * (matrix[p, q] - matrix[p, 4 - q])) * odd[q] for q in range(2))
        t = sum(float(0.5 * (matrix[p, q] + matrix[p, 4 - q])) * even[q] for q in range(2))
        t = t + float(matrix[p, 2]) * x[2]
        out[p] = s + t
        out[4 - p] = s - t
    out[2] = sum(float(matrix[2, q]) * odd[q] for q in range(2))
    return out


def kernel(
    ug, vg, rg, uc, vc, rc, lam, mu, defect, keep, rho, hist, cells, filt, perm, opg, opf, table,
    mem, out_v,
    pair_u, pair_v, pair_r, perm_v, opg_v, opf_v, tab_v,
    sw, qs, lam_v, mu_v, def_v, inv_mass,
    nd, ft, fs, yp, ym, rxm, rxp, rym, ryp, rdg,
    hy1, hy2, ry1, ry2, rc1, rc2,
    hist_v, cells_v, filt_v, fg_own, fgb, fgn, sj, frc,
    xr,
    keep_s, lsem, h_send, h_recv, f_send, f_recv, g_send, g_recv,
):
    s = lax.axis_index("slab")
    d = lax.axis_index("depth")
    ns = lax.axis_size("slab")
    nd_ = lax.axis_size("depth")
    sp, sm = lax.rem(s + 1, ns), lax.rem(s + ns - 1, ns)
    dp, dm = lax.rem(d + 1, nd_), lax.rem(d + nd_ - 1, nd_)

    barrier = pltpu.get_barrier_semaphore()
    peers = 0
    for ps in (s, sm, sp):
        for k in range(4):
            if ps is s and k == 0:
                continue
            pl.semaphore_signal(
                barrier, inc=1, device_id=(ps, lax.rem(d + k, nd_)), device_id_type=MESH
            )
            peers += 1

    loads = []

    def load(src, dst):
        copy = pltpu.make_async_copy(src, dst, lsem.at[len(loads)])
        copy.start()
        loads.append(copy)
        return copy

    l_ug = load(ug, pair_u.at[:, 0:4])
    l_uc = load(uc, pair_u.at[:, 4:8])
    l_perm = load(perm, perm_v)
    l_opg = load(opg, opg_v)
    l_tab = load(table, tab_v)
    l_vg = load(vg, pair_v.at[:, 0:4])
    l_vc = load(vc, pair_v.at[:, 4:8])
    l_rho = load(rho, pair_r.at[:, 0:4])
    l_opf = load(opf, opf_v)
    zero7 = jnp.zeros((7, 128), F32)
    for w in range(2):
        for k in range(75):
            mem[w, k, 25:32, :] = zero7
    for a in range(5):
        lam_v[a, 25:32, :] = zero7
        mu_v[a, 25:32, :] = zero7
        def_v[a, 25:32, :] = zero7
    for x in range(4):
        hist_v[x, 64:72, :] = jnp.zeros((8, 128), F32)
    l_lam = load(lam.at[:, :, 0], lam_v.at[:, 0:25])
    l_mu = load(mu.at[:, :, 0], mu_v.at[:, 0:25])
    l_rg = load(rg.at[:, :, 0], mem.at[0, :, 0:25])
    l_def = load(defect.at[:, :, 0], def_v.at[:, 0:25])
    l_keep = load(keep, keep_s)
    l_cells = load(cells, cells_v)
    l_filt = load(filt, filt_v)
    l_hist = [load(hist.at[:, x], hist_v.at[x, 0:64]) for x in range(4)]
    l_rc = load(rc.at[:, :, 0], mem.at[1, :, 0:25])

    zero24 = jnp.zeros((24, 128), F32)
    for a in range(4):
        for k in range(SLOTS):
            nd[a, k] = zero24
    for q in range(8):
        fgn[pl.ds(q * 24, 24), :] = zero24

    def deinterleave(ref, blocks):
        rows = blocks * 8
        x = ref[...].reshape(rows, 512)
        y = jnp.dot(jnp.concatenate(split3(x), axis=0), perm_v[...], preferred_element_type=F32)
        return y[0:rows] + y[rows : 2 * rows] + y[2 * rows : 3 * rows]

    l_perm.wait()
    l_ug.wait()
    l_uc.wait()
    y = deinterleave(pair_u, 12)
    for k in range(12):
        for c in range(4):
            lanes = slice(c * 128, c * 128 + 128)
            nd[k % 4, DISP[0] + k // 4, c * 5 : c * 5 + 4, :] = y[k * 8 : k * 8 + 4, lanes]
            nd[k % 4, DISP[1] + k // 4, c * 5 : c * 5 + 4, :] = y[k * 8 + 4 : k * 8 + 8, lanes]
    for a in range(4):
        for k in range(3):
            hy1[a * 12 + k * 4 : a * 12 + k * 4 + 4, :] = nd[a, k, pl.ds(0, 4, stride=5), :]

    pl.semaphore_wait(barrier, peers)

    def remote(src, dst, send, recv, target):
        return pltpu.make_async_remote_copy(
            src_ref=src, dst_ref=dst, send_sem=send, recv_sem=recv, device_id=target, device_id_type=MESH
        )

    h1 = [
        remote(hy1, ry1, h_send.at[0], h_recv.at[0], (s, dm)),
        remote(nd.at[0, 0:3], nd.at[4, 0:3], h_send.at[1], h_recv.at[1], (sm, d)),
        remote(hy1.at[0:16], rc1, h_send.at[2], h_recv.at[2], (sm, dm)),
    ]
    for copy in h1:
        copy.start()

    l_vg.wait()
    l_vc.wait()
    l_rho.wait()
    y = deinterleave(pair_v, 12)
    for k in range(12):
        for c in range(4):
            lanes = slice(c * 128, c * 128 + 128)
            nd[k % 4, VEL[0] + k // 4, c * 5 : c * 5 + 4, :] = y[k * 8 : k * 8 + 4, lanes]
            nd[k % 4, VEL[1] + k // 4, c * 5 : c * 5 + 4, :] = y[k * 8 + 4 : k * 8 + 8, lanes]
    y = deinterleave(pair_r, 4)
    for k in range(4):
        for c in range(4):
            nd[k, RHO, c * 5 : c * 5 + 4, :] = y[k * 8 : k * 8 + 4, c * 128 : c * 128 + 128]
    for a in range(4):
        for k in range(10):
            row = a * 40 + k * 4
            hy2[row : row + 4, :] = nd[a, 3 + k, pl.ds(0, 4, stride=5), :]
    h2 = [
        remote(hy2, ry2, h_send.at[3], h_recv.at[3], (s, dm)),
        remote(nd.at[0, 3:13], nd.at[4, 3:13], h_send.at[4], h_recv.at[4], (sm, d)),
        remote(hy2.at[0:40], rc2, h_send.at[5], h_recv.at[5], (sm, dm)),
    ]
    for copy in h2:
        copy.start()

    l_tab.wait()
    l_lam.wait()
    l_mu.wait()
    l_def.wait()
    weight_bc = tab_v[0]
    for a in range(5):
        weight = weight_bc * float(WGLL[a])
        two_mu = 2.0 * mu_v[a]
        lam_v[a] = weight * lam_v[a]
        mu_v[a] = weight * two_mu
        def_v[a] = two_mu * def_v[a]

    def relaxed(w):
        for a in range(5):
            weight = weight_bc * float(WGLL[a])
            for k in range(5):
                j = k * 5 + a
                sw[w, j] = weight * (mem[w, j] + mem[w, 25 + j] + mem[w, 50 + j])

    l_rg.wait()
    relaxed(0)

    l_cells.wait()
    l_filt.wait()
    for copy in l_hist:
        copy.wait()
    filt3 = jnp.concatenate(split3(filt_v[...]), axis=0)
    ids = lax.broadcasted_iota(jnp.int32, (256, 128), 0)
    for x in range(4):
        one_hot = jnp.where(ids == cells_v[x : x + 1, :], 1.0, 0.0).astype(BF16)
        g = jnp.dot(filt3, one_hot, preferred_element_type=F32)
        g = g[0:64] + g[64:128] + g[128:192]
        for t in range(4):
            fg_own[x * 8 + t : x * 8 + t + 1, :] = jnp.sum(
                g * hist_v[x, t + 1 : t + 65, :], axis=0, keepdims=True
            )
            fg_own[x * 8 + 4 + t : x * 8 + 5 + t, :] = g[63 - t : 64 - t]
    far = remote(fg_own.at[0:8], fgb.at[d, 32:40], g_send.at[0], g_recv.at[4 + d], (sm, 0))
    far.start()

    @pl.when(d != 0)
    def _():
        remote(fg_own, fgb.at[d, 0:32], g_send.at[1], g_recv.at[d], (s, 0)).start()

    def strain_stress_force(w, t):
        opg_m = opg_v[...]
        comps = []
        for i in range(3):
            columns = []
            for a in range(5):
                u = nd[a, DISP[w] + i]
                u = jnp.concatenate([u, pltpu.roll(u[0:8], 127, 1)], axis=0)
                high, low = split2(u)
                columns.append(jnp.concatenate([high, low, high], axis=0))
            g = jnp.dot(opg_m, jnp.concatenate(columns, axis=1), preferred_element_type=F32)
            lanes = [slice(a * 128, a * 128 + 128) for a in range(5)]
            gx = derive([g[0:32, l] for l in lanes], DMAT)
            comps.append((gx, [g[32:64, l] for l in lanes], [g[64:96, l] for l in lanes]))
        fluxes = []
        for a in range(5):
            gx = [comps[i][0][a] for i in range(3)]
            gy = [comps[i][1][a] for i in range(3)]
            gz = [comps[i][2][a] for i in range(3)]
            xy = 0.5 * (gy[0] + gx[1])
            xz = 0.5 * (gz[0] + gx[2])
            yz = 0.5 * (gz[1] + gy[2])
            trace = gx[0] + gy[1] + gz[2]
            third = trace * (1.0 / 3.0)
            m, q = mu_v[a], def_v[a]
            for k, e in enumerate((gx[0] - third, gy[1] - third, xy, xz, yz)):
                qs[w, k * 5 + a] = q * e
            pressure = lam_v[a] * trace
            r = [sw[w, k * 5 + a] for k in range(5)]
            sxx = pressure + m * gx[0] - r[0]
            syy = pressure + m * gy[1] - r[1]
            szz = pressure + m * gz[2] + (r[0] + r[1])
            sxy = m * xy - r[2]
            sxz = m * xz - r[3]
            syz = m * yz - r[4]
            fluxes.append(((sxx, sxy, sxz), (sxy, syy, syz), (sxz, syz, szz)))
        opf_m = opf_v[...]
        for i in range(3):
            fx = derive([fluxes[a][0][i] for a in range(5)], DMAT.T)
            columns = []
            for a in range(5):
                y_high, y_low = split2(fluxes[a][1][i])
                z_high, z_low = split2(fluxes[a][2][i])
                x_high, x_low = split2(fx[a])
                columns.append(
                    jnp.concatenate([y_high, z_high, y_low, z_low, y_high, z_high, x_high, x_low], axis=0)
                )
            f = jnp.dot(opf_m, jnp.concatenate(columns, axis=1), preferred_element_type=F32)
            for a in range(5):
                fa = f[:, a * 128 : a * 128 + 128]
                fs[w, t, a, i, 0:8, :] = fa[0:8] + pltpu.roll(fa[24:32], 1, 1)
                fs[w, t, a, i, 8:24, :] = fa[8:24]

    below = (d < nd_ - 1).astype(F32)

    def messages(w, t):
        n = w * STEPS + t
        sends = [
            (ym.at[n], rym.at[n], (s, dm)),
            (yp.at[n], ryp.at[n], (s, dp)),
            (ym.at[n, 0:16], rdg.at[n, 0], (sm, dm)),
            (yp.at[n, 0:16], rdg.at[n, 1], (sm, dp)),
            (ym.at[n, 48:64], rdg.at[n, 2], (sp, dm)),
            (yp.at[n, 48:64], rdg.at[n, 3], (sp, dp)),
            (fs.at[w, t, 0], rxm.at[n], (sm, d)),
            (fs.at[w, t, 4], rxp.at[n], (sp, d)),
        ]
        return [
            remote(src, dst, f_send.at[n, j], f_recv.at[n, j], target)
            for j, (src, dst, target) in enumerate(sends)
        ]

    def send(w, t):
        n = w * STEPS + t
        for a in range(5):
            for i in range(3):
                row = a * 12 + i * 4
                ym[n, row : row + 4, :] = fs[w, t, a, i, pl.ds(0, 4, stride=5), :]
                yp[n, row : row + 4, :] = below * fs[w, t, a, i, pl.ds(4, 4, stride=5), :]
        ym[n, 60:64, :] = jnp.zeros((4, 128), F32)
        yp[n, 60:64, :] = jnp.zeros((4, 128), F32)
        for copy in messages(w, t):
            copy.start()

    l_keep.wait()
    kept = [keep_s[l] for l in range(3)]

    def memory(w, last):
        for a in range(5):
            weight = weight_bc * float(WGLL[a])
            for k in range(5):
                j = k * 5 + a
                q = qs[w, j]
                new = []
                for l in range(3):
                    value = kept[l] * mem[w, 25 * l + j] + (1.0 - kept[l]) * q
                    mem[w, 25 * l + j] = value
                    new.append(value)
                if not last:
                    sw[w, j] = weight * (new[0] + new[1] + new[2])

    def receive(w, t):
        n = w * STEPS + t
        for copy in messages(w, t):
            copy.wait_recv()
        for a in range(5):
            for i in range(3):
                f = fs[w, t, a, i]
                if a == 0:
                    f = f + rxp[n, i]
                if a == 4:
                    f = f + rxm[n, i]
                ft[a, i] = f
        for a in range(5):
            for i in range(3):
                row = a * 12 + i * 4
                low = ryp[n, row : row + 4, :]
                top = rym[n, row : row + 4, :]
                if a == 4:
                    low = low + rdg[n, 1, i * 4 : i * 4 + 4, :]
                    top = top + rdg[n, 0, i * 4 : i * 4 + 4, :]
                if a == 0:
                    low = low + rdg[n, 3, i * 4 : i * 4 + 4, :]
                    top = top + rdg[n, 2, i * 4 : i * 4 + 4, :]
                if w == 1 and i == 1:
                    low = low - frc[a * 4 : a * 4 + 4, :]
                at_low = (a, i, pl.ds(0, 4, stride=5), slice(None))
                at_top = (a, i, pl.ds(4, 4, stride=5), slice(None))
                ft[at_low] = ft[at_low] + low
                ft[at_top] = ft[at_top] + top

    def update(w):
        for a in range(5):
            scale = inv_mass[a]
            for i in range(3):
                v = nd[a, VEL[w] + i] - scale * ft[a, i]
                nd[a, VEL[w] + i] = v
                nd[a, DISP[w] + i] = nd[a, DISP[w] + i] + DT * v

    def sample(t):
        for a in range(5):
            sj[t, a * 4 : a * 4 + 4, :] = nd[a, DISP[0] + 1, pl.ds(0, 4, stride=5), :]

    def forcing(t):
        f = fgn[t * 24 : t * 24 + 24, :]
        for m in range(t + 1):
            f = f + fgn[(4 + m) * 24 : (5 + m) * 24, :] * sj[t - m]
        frc[...] = f

    for copy in h1:
        copy.wait()
    for a in range(4):
        for k in range(3):
            row = a * 12 + k * 4
            nd[a, k, pl.ds(4, 4, stride=5), :] = below * ry1[row : row + 4, :]
    for k in range(3):
        nd[4, k, pl.ds(4, 4, stride=5), :] = below * rc1[k * 4 : k * 4 + 4, :]
    l_opg.wait()
    l_opf.wait()
    strain_stress_force(0, 0)
    send(0, 0)

    l_rc.wait()
    relaxed(1)
    for copy in h2:
        copy.wait()
    for a in range(4):
        for k in range(10):
            row = a * 40 + k * 4
            top = ry2[row : row + 4, :]
            nd[a, 3 + k, pl.ds(4, 4, stride=5), :] = top if k == 9 else below * top
    for k in range(10):
        top = rc2[k * 4 : k * 4 + 4, :]
        nd[4, 3 + k, pl.ds(4, 4, stride=5), :] = top if k == 9 else below * top
    strain_stress_force(1, 0)
    send(1, 0)
    memory(0, False)
    first = (d == 0).astype(F32)
    row_factor = tab_v[1, 0:24] * (1.0 + first * tab_v[2, 0:24] - (1.0 - below) * tab_v[3, 0:24])
    for a in range(5):
        wx = float([0.2, 49.0 / 90.0, 32.0 / 45.0, 49.0 / 90.0, 0.2][a])
        inv_mass[a] = (DT / wx) * row_factor / (nd[a, RHO] + tab_v[4, 0:24])

    @pl.when(d == 0)
    def _():
        for j in range(1, 4):
            remote(fg_own, fgb.at[j, 0:32], g_send.at[1], g_recv.at[j], (s, 0)).wait_recv()
        for j in range(4):
            remote(fg_own.at[0:8], fgb.at[j, 32:40], g_send.at[0], g_recv.at[4 + j], (sm, 0)).wait_recv()
        fgb[0, 0:32, :] = fg_own[...]
        x = jnp.concatenate([fgb[j] for j in range(4)], axis=1)
        y = jnp.dot(jnp.concatenate(split3(x), axis=0), perm_v[...], preferred_element_type=F32)
        y = y[0:40] + y[40:80] + y[80:120]
        for a in range(5):
            for c in range(4):
                fgn[pl.ds(a * 4 + c, 8, stride=24), :] = y[a * 8 : a * 8 + 8, c * 128 : c * 128 + 128]

    far.wait_send()

    @pl.when(d != 0)
    def _():
        remote(fg_own, fgb.at[d, 0:32], g_send.at[1], g_recv.at[d], (s, 0)).wait_send()

    memory(1, False)

    def finish(w):
        for i in range(3):
            for x in range(4):
                row = (i * 4 + x) * 8
                for c in range(4):
                    xr[c, row : row + 4, :] = nd[x, DISP[w] + i, c * 5 : c * 5 + 4, :]
                    xr[c, row + 4 : row + 8, :] = nd[x, VEL[w] + i, c * 5 : c * 5 + 4, :]
        x = jnp.concatenate([xr[c] for c in range(4)], axis=1)
        y = lax.dot_general(
            jnp.concatenate(split3(x), axis=0), perm_v[...], (((1,), (1,)), ((), ())),
            preferred_element_type=F32,
        )
        out_v[w] = (y[0:96] + y[96:192] + y[192:288]).reshape(12, 8, 512)

    for t in range(STEPS):
        receive(0, t)
        update(0)
        sample(t)
        forcing(t)
        if t < STEPS - 1:
            strain_stress_force(0, t + 1)
            send(0, t + 1)
            if t > 0:
                memory(1, False)
        else:
            memory(1, True)
            finish(0)
        receive(1, t)
        update(1)
        if t < STEPS - 1:
            strain_stress_force(1, t + 1)
            send(1, t + 1)
            memory(0, t == STEPS - 2)
        else:
            finish(1)
    for w in range(2):
        for t in range(STEPS):
            for copy in messages(w, t):
                copy.wait_send()


def write_kernel(mem, out_v, ug_o, vg_o, rg_o, uc_o, vc_o, rc_o, sem):
    pairs = [
        (mem.at[0, :, 0:25], rg_o.at[:, :, 0]),
        (mem.at[1, :, 0:25], rc_o.at[:, :, 0]),
        (out_v.at[0, :, 0:4], ug_o),
        (out_v.at[0, :, 4:8], vg_o),
        (out_v.at[1, :, 0:4], uc_o),
        (out_v.at[1, :, 4:8], vc_o),
    ]
    copies = [pltpu.make_async_copy(src, dst, sem.at[j]) for j, (src, dst) in enumerate(pairs)]
    for copy in copies:
        copy.start()
    for copy in copies:
        copy.wait()


def body(*args):
    (ug, vg, rg, uc, vc, rc, lam, mu, defect, keep, rho, hist, cells, filt) = args
    gradient, force = operators()
    operands = (
        ug.reshape(12, 4, 512), vg.reshape(12, 4, 512), rg.reshape(75, 25, 1, 128),
        uc.reshape(12, 4, 512), vc.reshape(12, 4, 512), rc.reshape(75, 25, 1, 128),
        lam.reshape(5, 25, 1, 128), mu.reshape(5, 25, 1, 128), defect.reshape(5, 25, 1, 128),
        keep, rho, hist, cells, filt.T,
        jnp.asarray(interleave()), jnp.asarray(gradient), jnp.asarray(force), jnp.asarray(tables()),
    )
    operands = tuple(
        pltpu.with_memory_space_constraint(x, pltpu.HBM) for x in operands
    )
    in_hbm = pl.BlockSpec(memory_space=pltpu.HBM)
    in_vmem = pl.BlockSpec(memory_space=pltpu.VMEM)
    in_specs = [in_hbm] * len(operands)
    nodal = pltpu.HBM((12, 4, 512), F32)
    points = pltpu.HBM((75, 25, 1, 128), F32)
    dma = pltpu.SemaphoreType.DMA
    vm = lambda *shape: pltpu.VMEM(shape, F32)
    waves = 2 * STEPS
    results = pl.pallas_call(
        kernel,
        out_shape=(vm(2, 75, 32, 128), vm(2, 12, 8, 512)),
        in_specs=in_specs,
        out_specs=(in_vmem,) * 2,
        scratch_shapes=[
            vm(12, 8, 512), vm(12, 8, 512), vm(4, 8, 512),
            pltpu.VMEM((512, 512), BF16), pltpu.VMEM((96, 96), BF16), pltpu.VMEM((32, 256), BF16),
            vm(5, 32, 128),
            vm(2, 25, 32, 128), vm(2, 25, 32, 128),
            vm(5, 32, 128), vm(5, 32, 128), vm(5, 32, 128), vm(5, 24, 128),
            vm(5, SLOTS, 24, 128), vm(5, 3, 24, 128), vm(2, STEPS, 5, 3, 24, 128),
            vm(waves, 64, 128), vm(waves, 64, 128),
            vm(waves, 3, 24, 128), vm(waves, 3, 24, 128),
            vm(waves, 64, 128), vm(waves, 64, 128), vm(waves, 4, 16, 128),
            vm(48, 128), vm(160, 128), vm(48, 128), vm(160, 128), vm(16, 128), vm(40, 128),
            vm(4, 72, 128), pltpu.VMEM((4, 128), jnp.int32), vm(64, 256),
            vm(32, 128), vm(4, 40, 128), vm(192, 128), vm(STEPS, 24, 128), vm(24, 128),
            vm(4, 96, 128),
            pltpu.SMEM((3,), F32), dma((24,)), dma((6,)), dma((6,)), dma((waves, 8)), dma((waves, 8)),
            dma((2,)), dma((8,)),
        ],
        compiler_params=pltpu.CompilerParams(
            collective_id=0, has_side_effects=True, vmem_limit_bytes=40 * 1024 * 1024
        ),
    )(*operands)
    outs = pl.pallas_call(
        write_kernel,
        out_shape=(nodal, nodal, points, nodal, nodal, points),
        in_specs=(in_vmem,) * 2,
        out_specs=(in_hbm,) * 6,
        scratch_shapes=[dma((6,))],
        compiler_params=pltpu.CompilerParams(vmem_limit_bytes=1024 * 1024),
    )(*(pltpu.with_memory_space_constraint(x, pltpu.VMEM) for x in results))
    full = (3, 5, 5, 5, 5, 1, 1, 128)
    u = (3, 4, 4, 512)
    return (
        outs[0].reshape(u), outs[1].reshape(u), outs[2].reshape(full),
        outs[3].reshape(u), outs[4].reshape(u), outs[5].reshape(full),
    )


def solution(mesh):
    nodal = P(None, "slab", "depth", None)
    points = P(None, None, None, None, None, "slab", "depth", None)
    material = P(None, None, None, "slab", "depth", None)
    return jax.shard_map(
        body,
        mesh=mesh,
        in_specs=(
            nodal, nodal, points, nodal, nodal, points, material, material, material, P(),
            P("slab", "depth", None), P(None, "slab", "depth"), P("slab", "depth"), P(),
        ),
        out_specs=(nodal, nodal, points, nodal, nodal, points),
        check_vma=False,
    )
```

```python
import functools

import jax
import jax.numpy as jnp
import ml_dtypes
import numpy as np
from jax import lax
from jax.experimental import pallas as pl
from jax.experimental.pallas import tpu as pltpu
from jax.sharding import PartitionSpec as P

STEPS = 4
TAPS = 64
DT = 0.04
F32 = jnp.float32
BF16 = jnp.bfloat16
MESH = pl.DeviceIdType.MESH

DISP = (0, 3)
VEL = (6, 9)
RHO = 12
SLOTS = 13


def gll_tables():
    points = np.array([-1.0, -np.sqrt(3.0 / 7.0), 0.0, np.sqrt(3.0 / 7.0), 1.0])
    weights = np.array([0.1, 49.0 / 90.0, 32.0 / 45.0, 49.0 / 90.0, 0.1])
    products = np.array([np.prod([points[t] - points[o] for o in range(5) if o != t]) for t in range(5)])
    derivative = np.zeros((5, 5))
    for t in range(5):
        for s in range(5):
            if t == s:
                derivative[t, s] = np.sum([1.0 / (points[t] - points[o]) for o in range(5) if o != t])
            else:
                derivative[t, s] = products[t] / products[s] / (points[t] - points[s])
    return derivative, weights


DMAT, WGLL = gll_tables()


def node_row(b, c):
    return c * 5 + b if c < 4 else 24 + b


def halves(matrix):
    high = matrix.astype(ml_dtypes.bfloat16)
    low = (matrix - high.astype(np.float64)).astype(ml_dtypes.bfloat16)
    return high, low


def operators():
    same = np.zeros((32, 32))
    along_y = np.zeros((32, 32))
    along_z = np.zeros((32, 32))
    for b in range(5):
        for c in range(5):
            row = b * 5 + c
            same[row, node_row(b, c)] = 1.0
            for q in range(5):
                along_y[row, node_row(q, c)] = DMAT[b, q]
                along_z[row, node_row(b, q)] = DMAT[c, q]
    high, low = halves(np.concatenate([same, along_y, along_z], axis=0))
    gradient = np.concatenate([high, high, low], axis=1)
    y_high, y_low = halves(along_y.T)
    z_high, z_low = halves(along_z.T)
    back = same.T.astype(ml_dtypes.bfloat16)
    force = np.concatenate([y_high, z_high, y_high, z_high, y_low, z_low, back, back], axis=1)
    return gradient, force


def tables():
    table = np.zeros((5, 32, 128), np.float32)
    wn = np.array([0.2, 49.0 / 90.0, 32.0 / 45.0, 49.0 / 90.0, 0.2])
    for b in range(5):
        for c in range(5):
            table[0, b * 5 + c] = WGLL[b] * WGLL[c]
        for c in range(4):
            row = node_row(b, c)
            table[1, row] = 1.0 / (wn[b] * wn[c])
            table[2, row] = float(b == 0)
            table[3, row] = float(b == 4)
    table[4, 20:] = 1.0
    return table


def interleave():
    table = np.zeros((512, 512), np.float32)
    for c in range(4):
        for e in range(128):
            table[4 * e + c, c * 128 + e] = 1.0
    return table.astype(ml_dtypes.bfloat16)


def split2(x):
    high = x.astype(BF16)
    return high, (x - high.astype(F32)).astype(BF16)


def split3(x):
    high = x.astype(BF16)
    rest = x - high.astype(F32)
    middle = rest.astype(BF16)
    return high, middle, (rest - middle.astype(F32)).astype(BF16)


def derive(x, matrix):
    even = [x[0] + x[4], x[1] + x[3]]
    odd = [x[0] - x[4], x[1] - x[3]]
    out = [None] * 5
    for p in range(2):
        s = sum(float(0.5 * (matrix[p, q] - matrix[p, 4 - q])) * odd[q] for q in range(2))
        t = sum(float(0.5 * (matrix[p, q] + matrix[p, 4 - q])) * even[q] for q in range(2))
        t = t + float(matrix[p, 2]) * x[2]
        out[p] = s + t
        out[4 - p] = s - t
    out[2] = sum(float(matrix[2, q]) * odd[q] for q in range(2))
    return out


def kernel(
    ug, vg, rg, uc, vc, rc, lam, mu, defect, keep, rho, hist, cells, filt, perm, opg, opf, table,
    mem, out_v,
    pair_u, pair_v, pair_r, perm_v, opg_v, opf_v, tab_v,
    sw, qs, lam_v, mu_v, def_v, inv_mass,
    nd, ft, fs, yp, ym, rxm, rxp, rym, ryp, rdg,
    hy1, hy2, ry1, ry2, rc1, rc2,
    hist_v, cells_v, filt_v, fg_own, fgb, fgn, sj, frc,
    xr,
    keep_s, lsem, h_send, h_recv, f_send, f_recv, g_send, g_recv,
):
    s = lax.axis_index("slab")
    d = lax.axis_index("depth")
    ns = lax.axis_size("slab")
    nd_ = lax.axis_size("depth")
    sp, sm = lax.rem(s + 1, ns), lax.rem(s + ns - 1, ns)
    dp, dm = d + 1, d - 1

    barrier = pltpu.get_barrier_semaphore()

    def greet(*target):
        pl.semaphore_signal(barrier, inc=1, device_id=target, device_id_type=MESH)

    has_low, has_top = d > 0, d < nd_ - 1

    @pl.when(d == 0)
    def _():
        for k in (3, 2):
            greet(sp, k)
            greet(s, k)

    @pl.when(has_low)
    def _():
        for x in (sm, sp, s):
            greet(x, dm)

    @pl.when(has_top)
    def _():
        for x in (sm, sp, s):
            greet(x, dp)

    greet(sm, d)
    greet(sp, d)
    peers = 2 + 3 * has_low.astype(jnp.int32) + 3 * has_top.astype(jnp.int32) + 2 * (d >= 2).astype(jnp.int32)

    loads = []

    def load(src, dst):
        copy = pltpu.make_async_copy(src, dst, lsem.at[len(loads)])
        copy.start()
        loads.append(copy)
        return copy

    l_ug = load(ug, pair_u.at[:, 0:4])
    l_uc = load(uc, pair_u.at[:, 4:8])
    l_perm = load(perm, perm_v)
    l_opg = load(opg, opg_v)
    l_tab = load(table, tab_v)
    l_vg = load(vg, pair_v.at[:, 0:4])
    l_vc = load(vc, pair_v.at[:, 4:8])
    l_rho = load(rho, pair_r.at[:, 0:4])
    l_opf = load(opf, opf_v)
    zero7 = jnp.zeros((7, 128), F32)
    for w in range(2):
        for k in range(75):
            mem[w, k, 25:32, :] = zero7
    for a in range(5):
        lam_v[a, 25:32, :] = zero7
        mu_v[a, 25:32, :] = zero7
        def_v[a, 25:32, :] = zero7
    for x in range(4):
        hist_v[x, 64:72, :] = jnp.zeros((8, 128), F32)
    l_lam = load(lam.at[:, :, 0], lam_v.at[:, 0:25])
    l_mu = load(mu.at[:, :, 0], mu_v.at[:, 0:25])
    l_rg = load(rg.at[:, :, 0], mem.at[0, :, 0:25])
    l_def = load(defect.at[:, :, 0], def_v.at[:, 0:25])
    l_keep = load(keep, keep_s)
    l_cells = load(cells, cells_v)
    l_filt = load(filt, filt_v)
    l_hist = [load(hist.at[:, x], hist_v.at[x, 0:64]) for x in range(4)]
    l_rc = load(rc.at[:, :, 0], mem.at[1, :, 0:25])

    zero24 = jnp.zeros((24, 128), F32)
    for a in range(4):
        for k in range(SLOTS):
            nd[a, k] = zero24
    for q in range(8):
        fgn[pl.ds(q * 24, 24), :] = zero24

    def deinterleave(ref, blocks):
        rows = blocks * 8
        x = ref[...].reshape(rows, 512)
        y = jnp.dot(jnp.concatenate(split3(x), axis=0), perm_v[...], preferred_element_type=F32)
        return y[0:rows] + y[rows : 2 * rows] + y[2 * rows : 3 * rows]

    l_perm.wait()
    l_ug.wait()
    l_uc.wait()
    y = deinterleave(pair_u, 12)
    for k in range(12):
        for c in range(4):
            lanes = slice(c * 128, c * 128 + 128)
            nd[k % 4, DISP[0] + k // 4, c * 5 : c * 5 + 4, :] = y[k * 8 : k * 8 + 4, lanes]
            nd[k % 4, DISP[1] + k // 4, c * 5 : c * 5 + 4, :] = y[k * 8 + 4 : k * 8 + 8, lanes]
    for a in range(4):
        for k in range(3):
            hy1[a * 12 + k * 4 : a * 12 + k * 4 + 4, :] = nd[a, k, pl.ds(0, 4, stride=5), :]

    pl.semaphore_wait(barrier, peers)

    def remote(src, dst, send, recv, target):
        return pltpu.make_async_remote_copy(
            src_ref=src, dst_ref=dst, send_sem=send, recv_sem=recv, device_id=target, device_id_type=MESH
        )

    def halo(first, slots, rows, recv_rows, corner):
        h = 0 if first else 3
        size = corner.shape[0]
        low = [
            remote(rows.at[0:size], corner, h_send.at[h + 2], h_recv.at[h + 2], (sm, dm)),
            remote(rows, recv_rows, h_send.at[h], h_recv.at[h], (s, dm)),
        ]
        side = remote(nd.at[0, slots], nd.at[4, slots], h_send.at[h + 1], h_recv.at[h + 1], (sm, d))
        return low, side

    def halo_start(*args):
        low, side = halo(*args)

        @pl.when(has_low)
        def _():
            for copy in low:
                copy.start()

        side.start()

    def halo_wait(*args):
        low, side = halo(*args)
        side.wait()

        @pl.when(has_low)
        def _():
            for copy in low:
                copy.wait_send()

        @pl.when(has_top)
        def _():
            for copy in low:
                copy.wait_recv()

    h1 = (True, slice(0, 3), hy1, ry1, rc1)
    h2 = (False, slice(3, 13), hy2, ry2, rc2)
    halo_start(*h1)

    l_vg.wait()
    l_vc.wait()
    l_rho.wait()
    y = deinterleave(pair_v, 12)
    for k in range(12):
        for c in range(4):
            lanes = slice(c * 128, c * 128 + 128)
            nd[k % 4, VEL[0] + k // 4, c * 5 : c * 5 + 4, :] = y[k * 8 : k * 8 + 4, lanes]
            nd[k % 4, VEL[1] + k // 4, c * 5 : c * 5 + 4, :] = y[k * 8 + 4 : k * 8 + 8, lanes]
    y = deinterleave(pair_r, 4)
    for k in range(4):
        for c in range(4):
            nd[k, RHO, c * 5 : c * 5 + 4, :] = y[k * 8 : k * 8 + 4, c * 128 : c * 128 + 128]
    for a in range(4):
        for k in range(10):
            row = a * 40 + k * 4
            hy2[row : row + 4, :] = nd[a, 3 + k, pl.ds(0, 4, stride=5), :]
    halo_start(*h2)

    @pl.when(d == nd_ - 1)
    def _():
        for ref in (ry1, ry2, rc1, rc2):
            ref[...] = jnp.ones(ref.shape, F32)
        for n in range(2 * STEPS):
            rym[n] = jnp.zeros((64, 128), F32)
            rdg[n, 0] = jnp.zeros((16, 128), F32)
            rdg[n, 2] = jnp.zeros((16, 128), F32)

    @pl.when(d == 0)
    def _():
        for n in range(2 * STEPS):
            ryp[n] = jnp.zeros((64, 128), F32)
            rdg[n, 1] = jnp.zeros((16, 128), F32)
            rdg[n, 3] = jnp.zeros((16, 128), F32)

    l_tab.wait()
    l_lam.wait()
    l_mu.wait()
    l_def.wait()
    weight_bc = tab_v[0]
    for a in range(5):
        weight = weight_bc * float(WGLL[a])
        two_mu = 2.0 * mu_v[a]
        lam_v[a] = weight * lam_v[a]
        mu_v[a] = weight * two_mu
        def_v[a] = two_mu * def_v[a]

    def relaxed(w):
        for a in range(5):
            weight = weight_bc * float(WGLL[a])
            for k in range(5):
                j = k * 5 + a
                sw[w, j] = weight * (mem[w, j] + mem[w, 25 + j] + mem[w, 50 + j])

    l_rg.wait()
    relaxed(0)

    l_cells.wait()
    l_filt.wait()
    for copy in l_hist:
        copy.wait()
    filt3 = jnp.concatenate(split3(filt_v[...]), axis=0)
    ids = lax.broadcasted_iota(jnp.int32, (256, 128), 0)
    for x in range(4):
        one_hot = jnp.where(ids == cells_v[x : x + 1, :], 1.0, 0.0).astype(BF16)
        g = jnp.dot(filt3, one_hot, preferred_element_type=F32)
        g = g[0:64] + g[64:128] + g[128:192]
        for t in range(4):
            fg_own[x * 8 + t : x * 8 + t + 1, :] = jnp.sum(
                g * hist_v[x, t + 1 : t + 65, :], axis=0, keepdims=True
            )
            fg_own[x * 8 + 4 + t : x * 8 + 5 + t, :] = g[63 - t : 64 - t]
    far = remote(fg_own.at[0:8], fgb.at[d, 32:40], g_send.at[0], g_recv.at[4 + d], (sm, 0))
    far.start()

    @pl.when(d != 0)
    def _():
        remote(fg_own, fgb.at[d, 0:32], g_send.at[1], g_recv.at[d], (s, 0)).start()

    def strain_stress_force(w, t):
        opg_m = opg_v[...]
        comps = []
        for i in range(3):
            columns = []
            for a in range(5):
                u = nd[a, DISP[w] + i]
                u = jnp.concatenate([u, pltpu.roll(u[0:8], 127, 1)], axis=0)
                high, low = split2(u)
                columns.append(jnp.concatenate([high, low, high], axis=0))
            g = jnp.dot(opg_m, jnp.concatenate(columns, axis=1), preferred_element_type=F32)
            lanes = [slice(a * 128, a * 128 + 128) for a in range(5)]
            gx = derive([g[0:32, l] for l in lanes], DMAT)
            comps.append((gx, [g[32:64, l] for l in lanes], [g[64:96, l] for l in lanes]))
        fluxes = []
        for a in range(5):
            gx = [comps[i][0][a] for i in range(3)]
            gy = [comps[i][1][a] for i in range(3)]
            gz = [comps[i][2][a] for i in range(3)]
            xy = 0.5 * (gy[0] + gx[1])
            xz = 0.5 * (gz[0] + gx[2])
            yz = 0.5 * (gz[1] + gy[2])
            trace = gx[0] + gy[1] + gz[2]
            third = trace * (1.0 / 3.0)
            m, q = mu_v[a], def_v[a]
            for k, e in enumerate((gx[0] - third, gy[1] - third, xy, xz, yz)):
                qs[w, k * 5 + a] = q * e
            pressure = lam_v[a] * trace
            r = [sw[w, k * 5 + a] for k in range(5)]
            sxx = pressure + m * gx[0] - r[0]
            syy = pressure + m * gy[1] - r[1]
            szz = pressure + m * gz[2] + (r[0] + r[1])
            sxy = m * xy - r[2]
            sxz = m * xz - r[3]
            syz = m * yz - r[4]
            fluxes.append(((sxx, sxy, sxz), (sxy, syy, syz), (sxz, syz, szz)))
        opf_m = opf_v[...]
        for i in range(3):
            fx = derive([fluxes[a][0][i] for a in range(5)], DMAT.T)
            columns = []
            for a in range(5):
                y_high, y_low = split2(fluxes[a][1][i])
                z_high, z_low = split2(fluxes[a][2][i])
                x_high, x_low = split2(fx[a])
                columns.append(
                    jnp.concatenate([y_high, z_high, y_low, z_low, y_high, z_high, x_high, x_low], axis=0)
                )
            f = jnp.dot(opf_m, jnp.concatenate(columns, axis=1), preferred_element_type=F32)
            for a in range(5):
                fa = f[:, a * 128 : a * 128 + 128]
                fs[w, t, a, i, 0:8, :] = fa[0:8] + pltpu.roll(fa[24:32], 1, 1)
                fs[w, t, a, i, 8:24, :] = fa[8:24]

    below = (d < nd_ - 1).astype(F32)

    def messages(w, t):
        n = w * STEPS + t
        low = [
            (ym.at[n, 0:16], rdg.at[n, 0], (sm, dm)),
            (ym.at[n, 48:64], rdg.at[n, 2], (sp, dm)),
            (ym.at[n], rym.at[n], (s, dm)),
        ]
        top = [
            (yp.at[n, 0:16], rdg.at[n, 1], (sm, dp)),
            (yp.at[n, 48:64], rdg.at[n, 3], (sp, dp)),
            (yp.at[n], ryp.at[n], (s, dp)),
        ]
        side = [
            (fs.at[w, t, 0], rxm.at[n], (sm, d)),
            (fs.at[w, t, 4], rxp.at[n], (sp, d)),
        ]
        made = []
        for base, group in ((0, low), (3, top), (6, side)):
            made.append(
                [
                    remote(src, dst, f_send.at[n, base + j], f_recv.at[n, base + j], target)
                    for j, (src, dst, target) in enumerate(group)
                ]
            )
        return made

    def start_all(w, t):
        low, top, side = messages(w, t)

        @pl.when(has_low)
        def _():
            for copy in low:
                copy.start()

        @pl.when(has_top)
        def _():
            for copy in top:
                copy.start()

        for copy in side:
            copy.start()

    def wait_all(w, t, name):
        low, top, side = messages(w, t)
        for copy in side:
            getattr(copy, name)()
        sent = name == "wait_send"

        @pl.when(has_low if sent else has_top)
        def _():
            for copy in low:
                getattr(copy, name)()

        @pl.when(has_top if sent else has_low)
        def _():
            for copy in top:
                getattr(copy, name)()

    def send(w, t):
        n = w * STEPS + t
        for a in range(5):
            for i in range(3):
                row = a * 12 + i * 4
                ym[n, row : row + 4, :] = fs[w, t, a, i, pl.ds(0, 4, stride=5), :]
                yp[n, row : row + 4, :] = fs[w, t, a, i, pl.ds(4, 4, stride=5), :]
        ym[n, 60:64, :] = jnp.zeros((4, 128), F32)
        yp[n, 60:64, :] = jnp.zeros((4, 128), F32)
        start_all(w, t)

    l_keep.wait()
    kept = [keep_s[l] for l in range(3)]

    def memory(w, last):
        for a in range(5):
            weight = weight_bc * float(WGLL[a])
            for k in range(5):
                j = k * 5 + a
                q = qs[w, j]
                new = []
                for l in range(3):
                    value = kept[l] * mem[w, 25 * l + j] + (1.0 - kept[l]) * q
                    mem[w, 25 * l + j] = value
                    new.append(value)
                if not last:
                    sw[w, j] = weight * (new[0] + new[1] + new[2])

    def receive(w, t):
        n = w * STEPS + t
        wait_all(w, t, "wait_recv")
        for a in range(5):
            for i in range(3):
                f = fs[w, t, a, i]
                if a == 0:
                    f = f + rxp[n, i]
                if a == 4:
                    f = f + rxm[n, i]
                ft[a, i] = f
        for a in range(5):
            for i in range(3):
                row = a * 12 + i * 4
                low = ryp[n, row : row + 4, :]
                top = rym[n, row : row + 4, :]
                if a == 4:
                    low = low + rdg[n, 1, i * 4 : i * 4 + 4, :]
                    top = top + rdg[n, 0, i * 4 : i * 4 + 4, :]
                if a == 0:
                    low = low + rdg[n, 3, i * 4 : i * 4 + 4, :]
                    top = top + rdg[n, 2, i * 4 : i * 4 + 4, :]
                if w == 1 and i == 1:
                    low = low - frc[a * 4 : a * 4 + 4, :]
                at_low = (a, i, pl.ds(0, 4, stride=5), slice(None))
                at_top = (a, i, pl.ds(4, 4, stride=5), slice(None))
                ft[at_low] = ft[at_low] + low
                ft[at_top] = ft[at_top] + top

    def update(w):
        for a in range(5):
            scale = inv_mass[a]
            for i in range(3):
                v = nd[a, VEL[w] + i] - scale * ft[a, i]
                nd[a, VEL[w] + i] = v
                nd[a, DISP[w] + i] = nd[a, DISP[w] + i] + DT * v

    def sample(t):
        for a in range(5):
            sj[t, a * 4 : a * 4 + 4, :] = nd[a, DISP[0] + 1, pl.ds(0, 4, stride=5), :]

    def forcing(t):
        f = fgn[t * 24 : t * 24 + 24, :]
        for m in range(t + 1):
            f = f + fgn[(4 + m) * 24 : (5 + m) * 24, :] * sj[t - m]
        frc[...] = f

    halo_wait(*h1)
    for a in range(4):
        for k in range(3):
            row = a * 12 + k * 4
            nd[a, k, pl.ds(4, 4, stride=5), :] = below * ry1[row : row + 4, :]
    for k in range(3):
        nd[4, k, pl.ds(4, 4, stride=5), :] = below * rc1[k * 4 : k * 4 + 4, :]
    l_opg.wait()
    l_opf.wait()
    strain_stress_force(0, 0)
    send(0, 0)

    l_rc.wait()
    relaxed(1)
    halo_wait(*h2)
    for a in range(4):
        for k in range(10):
            row = a * 40 + k * 4
            top = ry2[row : row + 4, :]
            nd[a, 3 + k, pl.ds(4, 4, stride=5), :] = top if k == 9 else below * top
    for k in range(10):
        top = rc2[k * 4 : k * 4 + 4, :]
        nd[4, 3 + k, pl.ds(4, 4, stride=5), :] = top if k == 9 else below * top
    strain_stress_force(1, 0)
    send(1, 0)
    memory(0, False)
    first = (d == 0).astype(F32)
    row_factor = tab_v[1, 0:24] * (1.0 + first * tab_v[2, 0:24] - (1.0 - below) * tab_v[3, 0:24])
    for a in range(5):
        wx = float([0.2, 49.0 / 90.0, 32.0 / 45.0, 49.0 / 90.0, 0.2][a])
        inv_mass[a] = (DT / wx) * row_factor / (nd[a, RHO] + tab_v[4, 0:24])

    @pl.when(d == 0)
    def _():
        for j in range(1, 4):
            remote(fg_own, fgb.at[j, 0:32], g_send.at[1], g_recv.at[j], (s, 0)).wait_recv()
        for j in range(4):
            remote(fg_own.at[0:8], fgb.at[j, 32:40], g_send.at[0], g_recv.at[4 + j], (sm, 0)).wait_recv()
        fgb[0, 0:32, :] = fg_own[...]
        x = jnp.concatenate([fgb[j] for j in range(4)], axis=1)
        y = jnp.dot(jnp.concatenate(split3(x), axis=0), perm_v[...], preferred_element_type=F32)
        y = y[0:40] + y[40:80] + y[80:120]
        for a in range(5):
            for c in range(4):
                fgn[pl.ds(a * 4 + c, 8, stride=24), :] = y[a * 8 : a * 8 + 8, c * 128 : c * 128 + 128]

    far.wait_send()

    @pl.when(d != 0)
    def _():
        remote(fg_own, fgb.at[d, 0:32], g_send.at[1], g_recv.at[d], (s, 0)).wait_send()

    memory(1, False)

    def finish(w):
        for i in range(3):
            for x in range(4):
                row = (i * 4 + x) * 8
                for c in range(4):
                    xr[c, row : row + 4, :] = nd[x, DISP[w] + i, c * 5 : c * 5 + 4, :]
                    xr[c, row + 4 : row + 8, :] = nd[x, VEL[w] + i, c * 5 : c * 5 + 4, :]
        x = jnp.concatenate([xr[c] for c in range(4)], axis=1)
        y = lax.dot_general(
            jnp.concatenate(split3(x), axis=0), perm_v[...], (((1,), (1,)), ((), ())),
            preferred_element_type=F32,
        )
        out_v[w] = (y[0:96] + y[96:192] + y[192:288]).reshape(12, 8, 512)

    for t in range(STEPS):
        receive(0, t)
        update(0)
        sample(t)
        forcing(t)
        if t < STEPS - 1:
            strain_stress_force(0, t + 1)
            send(0, t + 1)
            if t > 0:
                memory(1, False)
        else:
            memory(1, True)
            finish(0)
        receive(1, t)
        update(1)
        if t < STEPS - 1:
            strain_stress_force(1, t + 1)
            send(1, t + 1)
            memory(0, t == STEPS - 2)
        else:
            finish(1)
    for w in range(2):
        for t in range(STEPS):
            wait_all(w, t, "wait_send")


def write_kernel(mem, out_v, ug_o, vg_o, rg_o, uc_o, vc_o, rc_o, sem):
    pairs = [
        (mem.at[0, :, 0:25], rg_o.at[:, :, 0]),
        (mem.at[1, :, 0:25], rc_o.at[:, :, 0]),
        (out_v.at[0, :, 0:4], ug_o),
        (out_v.at[0, :, 4:8], vg_o),
        (out_v.at[1, :, 0:4], uc_o),
        (out_v.at[1, :, 4:8], vc_o),
    ]
    copies = [pltpu.make_async_copy(src, dst, sem.at[j]) for j, (src, dst) in enumerate(pairs)]
    for copy in copies:
        copy.start()
    for copy in copies:
        copy.wait()


def body(*args):
    (ug, vg, rg, uc, vc, rc, lam, mu, defect, keep, rho, hist, cells, filt) = args
    gradient, force = operators()
    operands = (
        ug.reshape(12, 4, 512), vg.reshape(12, 4, 512), rg.reshape(75, 25, 1, 128),
        uc.reshape(12, 4, 512), vc.reshape(12, 4, 512), rc.reshape(75, 25, 1, 128),
        lam.reshape(5, 25, 1, 128), mu.reshape(5, 25, 1, 128), defect.reshape(5, 25, 1, 128),
        keep, rho, hist, cells, filt.T,
        jnp.asarray(interleave()), jnp.asarray(gradient), jnp.asarray(force), jnp.asarray(tables()),
    )
    operands = tuple(
        pltpu.with_memory_space_constraint(x, pltpu.HBM) for x in operands
    )
    in_hbm = pl.BlockSpec(memory_space=pltpu.HBM)
    in_vmem = pl.BlockSpec(memory_space=pltpu.VMEM)
    in_specs = [in_hbm] * len(operands)
    nodal = pltpu.HBM((12, 4, 512), F32)
    points = pltpu.HBM((75, 25, 1, 128), F32)
    dma = pltpu.SemaphoreType.DMA
    vm = lambda *shape: pltpu.VMEM(shape, F32)
    waves = 2 * STEPS
    results = pl.pallas_call(
        kernel,
        out_shape=(vm(2, 75, 32, 128), vm(2, 12, 8, 512)),
        in_specs=in_specs,
        out_specs=(in_vmem,) * 2,
        scratch_shapes=[
            vm(12, 8, 512), vm(12, 8, 512), vm(4, 8, 512),
            pltpu.VMEM((512, 512), BF16), pltpu.VMEM((96, 96), BF16), pltpu.VMEM((32, 256), BF16),
            vm(5, 32, 128),
            vm(2, 25, 32, 128), vm(2, 25, 32, 128),
            vm(5, 32, 128), vm(5, 32, 128), vm(5, 32, 128), vm(5, 24, 128),
            vm(5, SLOTS, 24, 128), vm(5, 3, 24, 128), vm(2, STEPS, 5, 3, 24, 128),
            vm(waves, 64, 128), vm(waves, 64, 128),
            vm(waves, 3, 24, 128), vm(waves, 3, 24, 128),
            vm(waves, 64, 128), vm(waves, 64, 128), vm(waves, 4, 16, 128),
            vm(48, 128), vm(160, 128), vm(48, 128), vm(160, 128), vm(16, 128), vm(40, 128),
            vm(4, 72, 128), pltpu.VMEM((4, 128), jnp.int32), vm(64, 256),
            vm(32, 128), vm(4, 40, 128), vm(192, 128), vm(STEPS, 24, 128), vm(24, 128),
            vm(4, 96, 128),
            pltpu.SMEM((3,), F32), dma((24,)), dma((6,)), dma((6,)), dma((waves, 8)), dma((waves, 8)),
            dma((2,)), dma((8,)),
        ],
        compiler_params=pltpu.CompilerParams(
            collective_id=0, has_side_effects=True, vmem_limit_bytes=40 * 1024 * 1024
        ),
    )(*operands)
    outs = pl.pallas_call(
        write_kernel,
        out_shape=(nodal, nodal, points, nodal, nodal, points),
        in_specs=(in_vmem,) * 2,
        out_specs=(in_hbm,) * 6,
        scratch_shapes=[dma((6,))],
        compiler_params=pltpu.CompilerParams(vmem_limit_bytes=1024 * 1024),
    )(*(pltpu.with_memory_space_constraint(x, pltpu.VMEM) for x in results))
    full = (3, 5, 5, 5, 5, 1, 1, 128)
    u = (3, 4, 4, 512)
    return (
        outs[0].reshape(u), outs[1].reshape(u), outs[2].reshape(full),
        outs[3].reshape(u), outs[4].reshape(u), outs[5].reshape(full),
    )


def solution(mesh):
    nodal = P(None, "slab", "depth", None)
    points = P(None, None, None, None, None, "slab", "depth", None)
    material = P(None, None, None, "slab", "depth", None)
    return jax.shard_map(
        body,
        mesh=mesh,
        in_specs=(
            nodal, nodal, points, nodal, nodal, points, material, material, material, P(),
            P("slab", "depth", None), P(None, "slab", "depth"), P("slab", "depth"), P(),
        ),
        out_specs=(nodal, nodal, points, nodal, nodal, points),
        check_vma=False,
    )
```

```python
import functools

import jax
import jax.numpy as jnp
import ml_dtypes
import numpy as np
from jax import lax
from jax.experimental import pallas as pl
from jax.experimental.pallas import tpu as pltpu
from jax.sharding import PartitionSpec as P

STEPS = 4
TAPS = 64
DT = 0.04
F32 = jnp.float32
BF16 = jnp.bfloat16
MESH = pl.DeviceIdType.MESH
ROW = 8

DISP = (0, 3)
VEL = (6, 9)
RHO = 12
SLOTS = 13


def gll_tables():
    points = np.array([-1.0, -np.sqrt(3.0 / 7.0), 0.0, np.sqrt(3.0 / 7.0), 1.0])
    weights = np.array([0.1, 49.0 / 90.0, 32.0 / 45.0, 49.0 / 90.0, 0.1])
    products = np.array([np.prod([points[t] - points[o] for o in range(5) if o != t]) for t in range(5)])
    derivative = np.zeros((5, 5))
    for t in range(5):
        for s in range(5):
            if t == s:
                derivative[t, s] = np.sum([1.0 / (points[t] - points[o]) for o in range(5) if o != t])
            else:
                derivative[t, s] = products[t] / products[s] / (points[t] - points[s])
    return derivative, weights


DMAT, WGLL = gll_tables()


def node_row(b, c):
    return c * 5 + b if c < 4 else 24 + b


def halves(matrix):
    high = matrix.astype(ml_dtypes.bfloat16)
    low = (matrix - high.astype(np.float64)).astype(ml_dtypes.bfloat16)
    return high, low


def operators():
    same = np.zeros((32, 32))
    along_y = np.zeros((32, 32))
    along_z = np.zeros((32, 32))
    for b in range(5):
        for c in range(5):
            row = b * 5 + c
            same[row, node_row(b, c)] = 1.0
            for q in range(5):
                along_y[row, node_row(q, c)] = DMAT[b, q]
                along_z[row, node_row(b, q)] = DMAT[c, q]
    high, low = halves(np.concatenate([same, along_y, along_z], axis=0))
    gradient = np.concatenate([high, high, low], axis=1)
    y_high, y_low = halves(along_y.T)
    z_high, z_low = halves(along_z.T)
    back = same.T.astype(ml_dtypes.bfloat16)
    force = np.concatenate([y_high, z_high, y_high, z_high, y_low, z_low, back, back], axis=1)
    return gradient, force


def tables():
    table = np.zeros((5, 32, 128), np.float32)
    wn = np.array([0.2, 49.0 / 90.0, 32.0 / 45.0, 49.0 / 90.0, 0.2])
    for b in range(5):
        for c in range(5):
            table[0, b * 5 + c] = WGLL[b] * WGLL[c]
        for c in range(4):
            row = node_row(b, c)
            table[1, row] = 1.0 / (wn[b] * wn[c])
            table[2, row] = float(b == 0)
            table[3, row] = float(b == 4)
    table[4, 20:] = 1.0
    return table


def interleave():
    table = np.zeros((512, 512), np.float32)
    for c in range(4):
        for e in range(128):
            table[4 * e + c, c * 128 + e] = 1.0
    return table.astype(ml_dtypes.bfloat16)


def split2(x):
    high = x.astype(BF16)
    return high, (x - high.astype(F32)).astype(BF16)


def split3(x):
    high = x.astype(BF16)
    rest = x - high.astype(F32)
    middle = rest.astype(BF16)
    return high, middle, (rest - middle.astype(F32)).astype(BF16)


def derive(x, matrix):
    even = [x[0] + x[4], x[1] + x[3]]
    odd = [x[0] - x[4], x[1] - x[3]]
    out = [None] * 5
    for p in range(2):
        s = sum(float(0.5 * (matrix[p, q] - matrix[p, 4 - q])) * odd[q] for q in range(2))
        t = sum(float(0.5 * (matrix[p, q] + matrix[p, 4 - q])) * even[q] for q in range(2))
        t = t + float(matrix[p, 2]) * x[2]
        out[p] = s + t
        out[4 - p] = s - t
    out[2] = sum(float(matrix[2, q]) * odd[q] for q in range(2))
    return out


def kernel(
    ug, vg, rg, uc, vc, rc, lam, mu, defect, keep, rho, hist, cells, filt, perm, opg, opf, table,
    mem, out_v,
    pair_u, pair_v, pair_r, perm_v, opg_v, opf_v, tab_v,
    sw, qs, lam_v, mu_v, def_v, inv_mass,
    nd, ft, fs, yp, ym, rxm, rxp, rym, ryp, rdg,
    hy0, hy1, hy2, ry0, ry1, ry2, rc0, rc1, rc2, rlp, rl0, rl1, rl2,
    hist_v, cells_v, filt_v, fg_own, fgb, fgn, sj, frc,
    xr,
    keep_s, lsem, ready, h_send, h_recv, l_send, l_recv, f_send, f_recv, g_send, g_recv,
):
    s = lax.axis_index("slab")
    d = lax.axis_index("depth")
    ns = lax.axis_size("slab")
    nd_ = lax.axis_size("depth")
    sp, sm = lax.rem(s + 1, ns), lax.rem(s + ns - 1, ns)
    dp, dm = d + 1, d - 1

    barrier = pltpu.get_barrier_semaphore()

    def greet(*target):
        pl.semaphore_signal(barrier, inc=1, device_id=target, device_id_type=MESH)

    has_low, has_top = d > 0, d < nd_ - 1

    head, relay, tail = (lax.rem(s, ROW) == k for k in (0, 1, ROW - 1))
    not_head, not_tail = jnp.logical_not(head), jnp.logical_not(tail)
    row_before, row_after = lax.rem(s + ns - ROW + 1, ns), lax.rem(s + ROW - 1, ns)

    @pl.when(relay)
    def _():
        greet(row_after, d)

        @pl.when(has_top)
        def _():
            greet(row_after, dp)

    @pl.when(tail)
    def _():
        greet(s - (ROW - 2), d)

    @pl.when(jnp.logical_and(head, d >= 2))
    def _():
        greet(sm, 0)

    @pl.when(not_tail)
    def _():
        @pl.when(d == 0)
        def _():
            for k in (3, 2):
                greet(sp, k)

        @pl.when(has_low)
        def _():
            greet(sp, dm)

        @pl.when(has_top)
        def _():
            greet(sp, dp)

        greet(sp, d)

    @pl.when(d == 0)
    def _():
        for k in (3, 2):
            greet(s, k)

    @pl.when(has_low)
    def _():
        greet(sm, dm)
        greet(s, dm)

    @pl.when(has_top)
    def _():
        greet(sm, dp)
        greet(s, dp)

    greet(sm, d)
    low_n, top_n, far_n = (flag.astype(jnp.int32) for flag in (has_low, has_top, d >= 2))
    usual = 2 + 3 * low_n + 3 * top_n + 2 * far_n
    peers = jnp.where(
        head, 2 + 3 * low_n + 2 * top_n + far_n, usual + relay.astype(jnp.int32)
        + 2 * jnp.logical_and(tail, d == 0).astype(jnp.int32),
    )

    loads = []

    def load(src, dst):
        copy = pltpu.make_async_copy(src, dst, lsem.at[len(loads)])
        copy.start()
        loads.append(copy)
        return copy

    l_ug = load(ug, pair_u.at[:, 0:4])
    l_uc = load(uc, pair_u.at[:, 4:8])
    l_perm = load(perm, perm_v)
    l_opg = load(opg, opg_v)
    l_tab = load(table, tab_v)
    l_vg = load(vg, pair_v.at[:, 0:4])
    l_vc = load(vc, pair_v.at[:, 4:8])
    l_rho = load(rho, pair_r.at[:, 0:4])
    l_opf = load(opf, opf_v)
    zero7 = jnp.zeros((7, 128), F32)
    for w in range(2):
        for k in range(75):
            mem[w, k, 25:32, :] = zero7
    for a in range(5):
        lam_v[a, 25:32, :] = zero7
        mu_v[a, 25:32, :] = zero7
        def_v[a, 25:32, :] = zero7
    for x in range(4):
        hist_v[x, 64:72, :] = jnp.zeros((8, 128), F32)
    l_lam = load(lam.at[:, :, 0], lam_v.at[:, 0:25])
    l_mu = load(mu.at[:, :, 0], mu_v.at[:, 0:25])
    l_rg = load(rg.at[:, :, 0], mem.at[0, :, 0:25])
    l_def = load(defect.at[:, :, 0], def_v.at[:, 0:25])
    l_keep = load(keep, keep_s)
    l_cells = load(cells, cells_v)
    l_filt = load(filt, filt_v)
    l_hist = [load(hist.at[:, x], hist_v.at[x, 0:64]) for x in range(4)]
    l_rc = load(rc.at[:, :, 0], mem.at[1, :, 0:25])

    zero24 = jnp.zeros((24, 128), F32)
    for a in range(4):
        for k in range(SLOTS):
            nd[a, k] = zero24
    for q in range(8):
        fgn[pl.ds(q * 24, 24), :] = zero24

    def deinterleave(ref, blocks):
        rows = blocks * 8
        x = ref[...].reshape(rows, 512)
        y = jnp.dot(jnp.concatenate(split3(x), axis=0), perm_v[...], preferred_element_type=F32)
        return y[0:rows] + y[rows : 2 * rows] + y[2 * rows : 3 * rows]

    l_perm.wait()
    l_ug.wait()
    l_uc.wait()
    y = deinterleave(pair_u, 12)
    for k in range(12):
        for c in range(4):
            lanes = slice(c * 128, c * 128 + 128)
            nd[k % 4, DISP[0] + k // 4, c * 5 : c * 5 + 4, :] = y[k * 8 : k * 8 + 4, lanes]
            nd[k % 4, DISP[1] + k // 4, c * 5 : c * 5 + 4, :] = y[k * 8 + 4 : k * 8 + 8, lanes]
    for a in range(4):
        for k in range(3):
            row = a * 12 + k * 4
            hy0[row : row + 4, :] = nd[a, k, pl.ds(0, 4, stride=5), :]
            hy1[row : row + 4, :] = nd[a, 3 + k, pl.ds(0, 4, stride=5), :]

    pl.semaphore_wait(barrier, peers)

    @pl.when(tail)
    def _():
        def announce(*target):
            pl.semaphore_signal(ready, inc=1, device_id=target, device_id_type=MESH)

        announce(sp, d)

        @pl.when(has_low)
        def _():
            announce(sp, dm)

        @pl.when(has_top)
        def _():
            announce(sp, dp)

        @pl.when(d == 0)
        def _():
            for k in (2, 3):
                announce(sp, k)

    def remote(src, dst, send, recv, target):
        return pltpu.make_async_remote_copy(
            src_ref=src, dst_ref=dst, send_sem=send, recv_sem=recv, device_id=target, device_id_type=MESH
        )

    groups = [
        (slice(0, 3), hy0, ry0, rc0, rl0),
        (slice(3, 6), hy1, ry1, rc1, rl1),
        (slice(6, 13), hy2, ry2, rc2, rl2),
    ]

    def halo(g):
        slots, rows, recv_rows, corner, relay_corner = groups[g]
        size = corner.shape[0]
        side_src, corner_src = nd.at[0, slots], rows.at[0:size]
        below = remote(rows, recv_rows, h_send.at[g, 0], h_recv.at[g, 0], (s, dm))
        side = remote(side_src, nd.at[4, slots], h_send.at[g, 1], h_recv.at[g, 1], (sm, d))
        edge = remote(corner_src, corner, h_send.at[g, 2], h_recv.at[g, 2], (sm, dm))
        to_relay = (
            remote(side_src, rlp.at[slots], h_send.at[g, 1], l_recv.at[g, 0], (row_before, d)),
            remote(corner_src, relay_corner, h_send.at[g, 2], l_recv.at[g, 1], (row_before, dm)),
        )
        end = s + (ROW - 2)
        from_relay = (
            remote(rlp.at[slots], nd.at[4, slots], l_send.at[g, 0], h_recv.at[g, 1], (end, d)),
            remote(relay_corner, corner, l_send.at[g, 1], h_recv.at[g, 2], (end, d)),
        )
        return below, side, edge, to_relay, from_relay

    def halo_start(g):
        below, side, edge, to_relay, _ = halo(g)

        @pl.when(head)
        def _():
            to_relay[0].start()

            @pl.when(has_low)
            def _():
                to_relay[1].start()

        @pl.when(not_head)
        def _():
            side.start()

            @pl.when(has_low)
            def _():
                edge.start()

        @pl.when(has_low)
        def _():
            below.start()

    def forward(gs):
        @pl.when(relay)
        def _():
            for g in gs:
                _, _, _, to_relay, from_relay = halo(g)
                to_relay[0].wait_recv()
                from_relay[0].start()

                @pl.when(has_top)
                def _():
                    to_relay[1].wait_recv()
                    from_relay[1].start()

    def forward_wait(gs):
        @pl.when(relay)
        def _():
            for g in gs:
                from_relay = halo(g)[4]
                from_relay[0].wait_send()

                @pl.when(has_top)
                def _():
                    from_relay[1].wait_send()

    def halo_wait(g):
        below, side, edge, _, _ = halo(g)
        side.wait()

        @pl.when(has_low)
        def _():
            below.wait_send()
            edge.wait_send()

        @pl.when(has_top)
        def _():
            below.wait_recv()
            edge.wait_recv()

    halo_start(0)
    halo_start(1)
    forward((0, 1))

    l_vg.wait()
    l_vc.wait()
    l_rho.wait()
    y = deinterleave(pair_v, 12)
    for k in range(12):
        for c in range(4):
            lanes = slice(c * 128, c * 128 + 128)
            nd[k % 4, VEL[0] + k // 4, c * 5 : c * 5 + 4, :] = y[k * 8 : k * 8 + 4, lanes]
            nd[k % 4, VEL[1] + k // 4, c * 5 : c * 5 + 4, :] = y[k * 8 + 4 : k * 8 + 8, lanes]
    y = deinterleave(pair_r, 4)
    for k in range(4):
        for c in range(4):
            nd[k, RHO, c * 5 : c * 5 + 4, :] = y[k * 8 : k * 8 + 4, c * 128 : c * 128 + 128]
    for a in range(4):
        for k in range(7):
            row = a * 28 + k * 4
            hy2[row : row + 4, :] = nd[a, 6 + k, pl.ds(0, 4, stride=5), :]
    halo_start(2)

    @pl.when(d == nd_ - 1)
    def _():
        for ref in (ry0, ry1, ry2, rc0, rc1, rc2):
            ref[...] = jnp.ones(ref.shape, F32)
        for n in range(2 * STEPS):
            rym[n] = jnp.zeros((64, 128), F32)
            rdg[n, 0] = jnp.zeros((16, 128), F32)
            rdg[n, 2] = jnp.zeros((16, 128), F32)

    @pl.when(d == 0)
    def _():
        for n in range(2 * STEPS):
            ryp[n] = jnp.zeros((64, 128), F32)
            rdg[n, 1] = jnp.zeros((16, 128), F32)
            rdg[n, 3] = jnp.zeros((16, 128), F32)

    l_tab.wait()
    l_lam.wait()
    l_mu.wait()
    l_def.wait()
    weight_bc = tab_v[0]
    for a in range(5):
        weight = weight_bc * float(WGLL[a])
        two_mu = 2.0 * mu_v[a]
        lam_v[a] = weight * lam_v[a]
        mu_v[a] = weight * two_mu
        def_v[a] = two_mu * def_v[a]

    def relaxed(w):
        for a in range(5):
            weight = weight_bc * float(WGLL[a])
            for k in range(5):
                j = k * 5 + a
                sw[w, j] = weight * (mem[w, j] + mem[w, 25 + j] + mem[w, 50 + j])

    l_rg.wait()
    relaxed(0)

    l_cells.wait()
    l_filt.wait()
    for copy in l_hist:
        copy.wait()
    filt3 = jnp.concatenate(split3(filt_v[...]), axis=0)
    ids = lax.broadcasted_iota(jnp.int32, (256, 128), 0)
    for x in range(4):
        one_hot = jnp.where(ids == cells_v[x : x + 1, :], 1.0, 0.0).astype(BF16)
        g = jnp.dot(filt3, one_hot, preferred_element_type=F32)
        g = g[0:64] + g[64:128] + g[128:192]
        for t in range(4):
            fg_own[x * 8 + t : x * 8 + t + 1, :] = jnp.sum(
                g * hist_v[x, t + 1 : t + 65, :], axis=0, keepdims=True
            )
            fg_own[x * 8 + 4 + t : x * 8 + 5 + t, :] = g[63 - t : 64 - t]
    far = remote(fg_own.at[0:8], fgb.at[d, 32:40], g_send.at[0], g_recv.at[4 + d], (sm, 0))
    @pl.when(not_head)
    def _():
        far.start()

    @pl.when(d != 0)
    def _():
        remote(fg_own, fgb.at[d, 0:32], g_send.at[1], g_recv.at[d], (s, 0)).start()

    def strain_stress_force(w, t):
        opg_m = opg_v[...]
        comps = []
        for i in range(3):
            columns = []
            for a in range(5):
                u = nd[a, DISP[w] + i]
                u = jnp.concatenate([u, pltpu.roll(u[0:8], 127, 1)], axis=0)
                high, low = split2(u)
                columns.append(jnp.concatenate([high, low, high], axis=0))
            g = jnp.dot(opg_m, jnp.concatenate(columns, axis=1), preferred_element_type=F32)
            lanes = [slice(a * 128, a * 128 + 128) for a in range(5)]
            gx = derive([g[0:32, l] for l in lanes], DMAT)
            comps.append((gx, [g[32:64, l] for l in lanes], [g[64:96, l] for l in lanes]))
        fluxes = []
        for a in range(5):
            gx = [comps[i][0][a] for i in range(3)]
            gy = [comps[i][1][a] for i in range(3)]
            gz = [comps[i][2][a] for i in range(3)]
            xy = 0.5 * (gy[0] + gx[1])
            xz = 0.5 * (gz[0] + gx[2])
            yz = 0.5 * (gz[1] + gy[2])
            trace = gx[0] + gy[1] + gz[2]
            third = trace * (1.0 / 3.0)
            m, q = mu_v[a], def_v[a]
            for k, e in enumerate((gx[0] - third, gy[1] - third, xy, xz, yz)):
                qs[w, k * 5 + a] = q * e
            pressure = lam_v[a] * trace
            r = [sw[w, k * 5 + a] for k in range(5)]
            sxx = pressure + m * gx[0] - r[0]
            syy = pressure + m * gy[1] - r[1]
            szz = pressure + m * gz[2] + (r[0] + r[1])
            sxy = m * xy - r[2]
            sxz = m * xz - r[3]
            syz = m * yz - r[4]
            fluxes.append(((sxx, sxy, sxz), (sxy, syy, syz), (sxz, syz, szz)))
        opf_m = opf_v[...]
        for i in range(3):
            fx = derive([fluxes[a][0][i] for a in range(5)], DMAT.T)
            columns = []
            for a in range(5):
                y_high, y_low = split2(fluxes[a][1][i])
                z_high, z_low = split2(fluxes[a][2][i])
                x_high, x_low = split2(fx[a])
                columns.append(
                    jnp.concatenate([y_high, z_high, y_low, z_low, y_high, z_high, x_high, x_low], axis=0)
                )
            f = jnp.dot(opf_m, jnp.concatenate(columns, axis=1), preferred_element_type=F32)
            for a in range(5):
                fa = f[:, a * 128 : a * 128 + 128]
                fs[w, t, a, i, 0:8, :] = fa[0:8] + pltpu.roll(fa[24:32], 1, 1)
                fs[w, t, a, i, 8:24, :] = fa[8:24]

    below = (d < nd_ - 1).astype(F32)

    def messages(w, t):
        n = w * STEPS + t
        low = [
            (ym.at[n, 0:16], rdg.at[n, 0], (sm, dm)),
            (ym.at[n, 48:64], rdg.at[n, 2], (sp, dm)),
            (ym.at[n], rym.at[n], (s, dm)),
        ]
        top = [
            (yp.at[n, 0:16], rdg.at[n, 1], (sm, dp)),
            (yp.at[n, 48:64], rdg.at[n, 3], (sp, dp)),
            (yp.at[n], ryp.at[n], (s, dp)),
        ]
        side = [
            (fs.at[w, t, 0], rxm.at[n], (sm, d)),
            (fs.at[w, t, 4], rxp.at[n], (sp, d)),
        ]
        made = []
        for base, group in ((0, low), (3, top), (6, side)):
            made.append(
                [
                    remote(src, dst, f_send.at[n, base + j], f_recv.at[n, base + j], target)
                    for j, (src, dst, target) in enumerate(group)
                ]
            )
        return made

    def start_all(w, t):
        low, top, side = messages(w, t)

        @pl.when(has_low)
        def _():
            for copy in low[:2]:
                copy.start()

        @pl.when(has_top)
        def _():
            for copy in top[:2]:
                copy.start()

        for copy in side:
            copy.start()

        @pl.when(has_low)
        def _():
            low[2].start()

        @pl.when(has_top)
        def _():
            top[2].start()

    def wait_all(w, t, name):
        low, top, side = messages(w, t)
        for copy in side:
            getattr(copy, name)()
        sent = name == "wait_send"

        @pl.when(has_low if sent else has_top)
        def _():
            for copy in low:
                getattr(copy, name)()

        @pl.when(has_top if sent else has_low)
        def _():
            for copy in top:
                getattr(copy, name)()

    def send(w, t):
        n = w * STEPS + t
        for a in range(5):
            for i in range(3):
                row = a * 12 + i * 4
                ym[n, row : row + 4, :] = fs[w, t, a, i, pl.ds(0, 4, stride=5), :]
                yp[n, row : row + 4, :] = fs[w, t, a, i, pl.ds(4, 4, stride=5), :]
        ym[n, 60:64, :] = jnp.zeros((4, 128), F32)
        yp[n, 60:64, :] = jnp.zeros((4, 128), F32)
        start_all(w, t)

    l_keep.wait()
    kept = [keep_s[l] for l in range(3)]

    def memory(w, last):
        for a in range(5):
            weight = weight_bc * float(WGLL[a])
            for k in range(5):
                j = k * 5 + a
                q = qs[w, j]
                new = []
                for l in range(3):
                    value = kept[l] * mem[w, 25 * l + j] + (1.0 - kept[l]) * q
                    mem[w, 25 * l + j] = value
                    new.append(value)
                if not last:
                    sw[w, j] = weight * (new[0] + new[1] + new[2])

    def receive(w, t):
        n = w * STEPS + t
        wait_all(w, t, "wait_recv")
        for a in range(5):
            for i in range(3):
                f = fs[w, t, a, i]
                if a == 0:
                    f = f + rxp[n, i]
                if a == 4:
                    f = f + rxm[n, i]
                ft[a, i] = f
        for a in range(5):
            for i in range(3):
                row = a * 12 + i * 4
                low = ryp[n, row : row + 4, :]
                top = rym[n, row : row + 4, :]
                if a == 4:
                    low = low + rdg[n, 1, i * 4 : i * 4 + 4, :]
                    top = top + rdg[n, 0, i * 4 : i * 4 + 4, :]
                if a == 0:
                    low = low + rdg[n, 3, i * 4 : i * 4 + 4, :]
                    top = top + rdg[n, 2, i * 4 : i * 4 + 4, :]
                if w == 1 and i == 1:
                    low = low - frc[a * 4 : a * 4 + 4, :]
                at_low = (a, i, pl.ds(0, 4, stride=5), slice(None))
                at_top = (a, i, pl.ds(4, 4, stride=5), slice(None))
                ft[at_low] = ft[at_low] + low
                ft[at_top] = ft[at_top] + top

    def update(w):
        for a in range(5):
            scale = inv_mass[a]
            for i in range(3):
                v = nd[a, VEL[w] + i] - scale * ft[a, i]
                nd[a, VEL[w] + i] = v
                nd[a, DISP[w] + i] = nd[a, DISP[w] + i] + DT * v

    def sample(t):
        for a in range(5):
            sj[t, a * 4 : a * 4 + 4, :] = nd[a, DISP[0] + 1, pl.ds(0, 4, stride=5), :]

    def forcing(t):
        f = fgn[t * 24 : t * 24 + 24, :]
        for m in range(t + 1):
            f = f + fgn[(4 + m) * 24 : (5 + m) * 24, :] * sj[t - m]
        frc[...] = f

    def fill(g, count):
        slots, _, recv_rows, corner, _ = groups[g]
        first = slots.start
        for a in range(5):
            for k in range(count):
                row = (a * count + k) * 4
                top = corner[k * 4 : k * 4 + 4, :] if a == 4 else recv_rows[row : row + 4, :]
                nd[a, first + k, pl.ds(4, 4, stride=5), :] = top if first + k == RHO else below * top

    halo_wait(0)
    fill(0, 3)
    l_opg.wait()
    l_opf.wait()
    strain_stress_force(0, 0)

    @pl.when(head)
    def _():
        pl.semaphore_wait(ready, 1 + low_n + top_n + far_n)

    send(0, 0)

    @pl.when(head)
    def _():
        far.start()

    forward((2,))
    l_rc.wait()
    relaxed(1)
    halo_wait(1)
    fill(1, 3)
    strain_stress_force(1, 0)
    send(1, 0)
    memory(0, False)
    halo_wait(2)
    fill(2, 7)
    first = (d == 0).astype(F32)
    row_factor = tab_v[1, 0:24] * (1.0 + first * tab_v[2, 0:24] - (1.0 - below) * tab_v[3, 0:24])
    for a in range(5):
        wx = float([0.2, 49.0 / 90.0, 32.0 / 45.0, 49.0 / 90.0, 0.2][a])
        inv_mass[a] = (DT / wx) * row_factor / (nd[a, RHO] + tab_v[4, 0:24])

    @pl.when(d == 0)
    def _():
        for j in range(1, 4):
            remote(fg_own, fgb.at[j, 0:32], g_send.at[1], g_recv.at[j], (s, 0)).wait_recv()
        for j in range(4):
            remote(fg_own.at[0:8], fgb.at[j, 32:40], g_send.at[0], g_recv.at[4 + j], (sm, 0)).wait_recv()
        fgb[0, 0:32, :] = fg_own[...]
        x = jnp.concatenate([fgb[j] for j in range(4)], axis=1)
        y = jnp.dot(jnp.concatenate(split3(x), axis=0), perm_v[...], preferred_element_type=F32)
        y = y[0:40] + y[40:80] + y[80:120]
        for a in range(5):
            for c in range(4):
                fgn[pl.ds(a * 4 + c, 8, stride=24), :] = y[a * 8 : a * 8 + 8, c * 128 : c * 128 + 128]

    far.wait_send()

    @pl.when(d != 0)
    def _():
        remote(fg_own, fgb.at[d, 0:32], g_send.at[1], g_recv.at[d], (s, 0)).wait_send()

    memory(1, False)

    def finish(w):
        for i in range(3):
            for x in range(4):
                row = (i * 4 + x) * 8
                for c in range(4):
                    xr[c, row : row + 4, :] = nd[x, DISP[w] + i, c * 5 : c * 5 + 4, :]
                    xr[c, row + 4 : row + 8, :] = nd[x, VEL[w] + i, c * 5 : c * 5 + 4, :]
        x = jnp.concatenate([xr[c] for c in range(4)], axis=1)
        y = lax.dot_general(
            jnp.concatenate(split3(x), axis=0), perm_v[...], (((1,), (1,)), ((), ())),
            preferred_element_type=F32,
        )
        out_v[w] = (y[0:96] + y[96:192] + y[192:288]).reshape(12, 8, 512)

    for t in range(STEPS):
        receive(0, t)
        update(0)
        if t < STEPS - 1:
            strain_stress_force(0, t + 1)
            send(0, t + 1)
        sample(t)
        forcing(t)
        if t < STEPS - 1:
            if t > 0:
                memory(1, False)
        else:
            memory(1, True)
            finish(0)
        receive(1, t)
        update(1)
        if t < STEPS - 1:
            strain_stress_force(1, t + 1)
            send(1, t + 1)
            memory(0, t == STEPS - 2)
        else:
            finish(1)
    forward_wait((0, 1, 2))
    for w in range(2):
        for t in range(STEPS):
            wait_all(w, t, "wait_send")


def write_kernel(mem, out_v, ug_o, vg_o, rg_o, uc_o, vc_o, rc_o, sem):
    pairs = [
        (mem.at[0, :, 0:25], rg_o.at[:, :, 0]),
        (mem.at[1, :, 0:25], rc_o.at[:, :, 0]),
        (out_v.at[0, :, 0:4], ug_o),
        (out_v.at[0, :, 4:8], vg_o),
        (out_v.at[1, :, 0:4], uc_o),
        (out_v.at[1, :, 4:8], vc_o),
    ]
    copies = [pltpu.make_async_copy(src, dst, sem.at[j]) for j, (src, dst) in enumerate(pairs)]
    for copy in copies:
        copy.start()
    for copy in copies:
        copy.wait()


def body(*args):
    (ug, vg, rg, uc, vc, rc, lam, mu, defect, keep, rho, hist, cells, filt) = args
    gradient, force = operators()
    operands = (
        ug.reshape(12, 4, 512), vg.reshape(12, 4, 512), rg.reshape(75, 25, 1, 128),
        uc.reshape(12, 4, 512), vc.reshape(12, 4, 512), rc.reshape(75, 25, 1, 128),
        lam.reshape(5, 25, 1, 128), mu.reshape(5, 25, 1, 128), defect.reshape(5, 25, 1, 128),
        keep, rho, hist, cells, filt.T,
        jnp.asarray(interleave()), jnp.asarray(gradient), jnp.asarray(force), jnp.asarray(tables()),
    )
    operands = tuple(
        pltpu.with_memory_space_constraint(x, pltpu.HBM) for x in operands
    )
    in_hbm = pl.BlockSpec(memory_space=pltpu.HBM)
    in_vmem = pl.BlockSpec(memory_space=pltpu.VMEM)
    in_specs = [in_hbm] * len(operands)
    nodal = pltpu.HBM((12, 4, 512), F32)
    points = pltpu.HBM((75, 25, 1, 128), F32)
    dma = pltpu.SemaphoreType.DMA
    vm = lambda *shape: pltpu.VMEM(shape, F32)
    waves = 2 * STEPS
    results = pl.pallas_call(
        kernel,
        out_shape=(vm(2, 75, 32, 128), vm(2, 12, 8, 512)),
        in_specs=in_specs,
        out_specs=(in_vmem,) * 2,
        scratch_shapes=[
            vm(12, 8, 512), vm(12, 8, 512), vm(4, 8, 512),
            pltpu.VMEM((512, 512), BF16), pltpu.VMEM((96, 96), BF16), pltpu.VMEM((32, 256), BF16),
            vm(5, 32, 128),
            vm(2, 25, 32, 128), vm(2, 25, 32, 128),
            vm(5, 32, 128), vm(5, 32, 128), vm(5, 32, 128), vm(5, 24, 128),
            vm(5, SLOTS, 24, 128), vm(5, 3, 24, 128), vm(2, STEPS, 5, 3, 24, 128),
            vm(waves, 64, 128), vm(waves, 64, 128),
            vm(waves, 3, 24, 128), vm(waves, 3, 24, 128),
            vm(waves, 64, 128), vm(waves, 64, 128), vm(waves, 4, 16, 128),
            vm(48, 128), vm(48, 128), vm(112, 128), vm(48, 128), vm(48, 128), vm(112, 128),
            vm(16, 128), vm(16, 128), vm(32, 128), vm(SLOTS, 24, 128), vm(16, 128), vm(16, 128), vm(32, 128),
            vm(4, 72, 128), pltpu.VMEM((4, 128), jnp.int32), vm(64, 256),
            vm(32, 128), vm(4, 40, 128), vm(192, 128), vm(STEPS, 24, 128), vm(24, 128),
            vm(4, 96, 128),
            pltpu.SMEM((3,), F32), dma((24,)), pltpu.SemaphoreType.REGULAR,
            dma((3, 3)), dma((3, 3)), dma((3, 2)), dma((3, 2)), dma((waves, 8)), dma((waves, 8)),
            dma((2,)), dma((8,)),
        ],
        compiler_params=pltpu.CompilerParams(
            collective_id=0, has_side_effects=True, vmem_limit_bytes=40 * 1024 * 1024
        ),
    )(*operands)
    outs = pl.pallas_call(
        write_kernel,
        out_shape=(nodal, nodal, points, nodal, nodal, points),
        in_specs=(in_vmem,) * 2,
        out_specs=(in_hbm,) * 6,
        scratch_shapes=[dma((6,))],
        compiler_params=pltpu.CompilerParams(vmem_limit_bytes=1024 * 1024),
    )(*(pltpu.with_memory_space_constraint(x, pltpu.VMEM) for x in results))
    full = (3, 5, 5, 5, 5, 1, 1, 128)
    u = (3, 4, 4, 512)
    return (
        outs[0].reshape(u), outs[1].reshape(u), outs[2].reshape(full),
        outs[3].reshape(u), outs[4].reshape(u), outs[5].reshape(full),
    )


def solution(mesh):
    nodal = P(None, "slab", "depth", None)
    points = P(None, None, None, None, None, "slab", "depth", None)
    material = P(None, None, None, "slab", "depth", None)
    return jax.shard_map(
        body,
        mesh=mesh,
        in_specs=(
            nodal, nodal, points, nodal, nodal, points, material, material, material, P(),
            P("slab", "depth", None), P(None, "slab", "depth"), P("slab", "depth"), P(),
        ),
        out_specs=(nodal, nodal, points, nodal, nodal, points),
        check_vma=False,
    )
```

```python
import functools

import jax
import jax.numpy as jnp
import ml_dtypes
import numpy as np
from jax import lax
from jax.experimental import pallas as pl
from jax.experimental.pallas import tpu as pltpu
from jax.sharding import PartitionSpec as P

STEPS = 4
TAPS = 64
DT = 0.04
F32 = jnp.float32
BF16 = jnp.bfloat16
MESH = pl.DeviceIdType.MESH
ROW = 8

DISP = (0, 3)
VEL = (6, 9)
RHO = 12
SLOTS = 13


def gll_tables():
    points = np.array([-1.0, -np.sqrt(3.0 / 7.0), 0.0, np.sqrt(3.0 / 7.0), 1.0])
    weights = np.array([0.1, 49.0 / 90.0, 32.0 / 45.0, 49.0 / 90.0, 0.1])
    products = np.array([np.prod([points[t] - points[o] for o in range(5) if o != t]) for t in range(5)])
    derivative = np.zeros((5, 5))
    for t in range(5):
        for s in range(5):
            if t == s:
                derivative[t, s] = np.sum([1.0 / (points[t] - points[o]) for o in range(5) if o != t])
            else:
                derivative[t, s] = products[t] / products[s] / (points[t] - points[s])
    return derivative, weights


DMAT, WGLL = gll_tables()


def node_row(b, c):
    return c * 5 + b if c < 4 else 24 + b


def halves(matrix):
    high = matrix.astype(ml_dtypes.bfloat16)
    low = (matrix - high.astype(np.float64)).astype(ml_dtypes.bfloat16)
    return high, low


def operators():
    same = np.zeros((32, 32))
    along_y = np.zeros((32, 32))
    along_z = np.zeros((32, 32))
    for b in range(5):
        for c in range(5):
            row = b * 5 + c
            same[row, node_row(b, c)] = 1.0
            for q in range(5):
                along_y[row, node_row(q, c)] = DMAT[b, q]
                along_z[row, node_row(b, q)] = DMAT[c, q]
    high, low = halves(np.concatenate([same, along_y, along_z], axis=0))
    gradient = np.concatenate([high, high, low], axis=1)
    y_high, y_low = halves(along_y.T)
    z_high, z_low = halves(along_z.T)
    back = same.T.astype(ml_dtypes.bfloat16)
    force = np.concatenate([y_high, z_high, y_high, z_high, y_low, z_low, back, back], axis=1)
    return gradient, force


def tables():
    table = np.zeros((5, 32, 128), np.float32)
    wn = np.array([0.2, 49.0 / 90.0, 32.0 / 45.0, 49.0 / 90.0, 0.2])
    for b in range(5):
        for c in range(5):
            table[0, b * 5 + c] = WGLL[b] * WGLL[c]
        for c in range(4):
            row = node_row(b, c)
            table[1, row] = 1.0 / (wn[b] * wn[c])
            table[2, row] = float(b == 0)
            table[3, row] = float(b == 4)
    table[4, 20:] = 1.0
    return table


def interleave():
    table = np.zeros((512, 512), np.float32)
    for c in range(4):
        for e in range(128):
            table[4 * e + c, c * 128 + e] = 1.0
    return table.astype(ml_dtypes.bfloat16)


def split2(x):
    high = x.astype(BF16)
    return high, (x - high.astype(F32)).astype(BF16)


def split3(x):
    high = x.astype(BF16)
    rest = x - high.astype(F32)
    middle = rest.astype(BF16)
    return high, middle, (rest - middle.astype(F32)).astype(BF16)


def derive(x, matrix):
    even = [x[0] + x[4], x[1] + x[3]]
    odd = [x[0] - x[4], x[1] - x[3]]
    out = [None] * 5
    for p in range(2):
        s = sum(float(0.5 * (matrix[p, q] - matrix[p, 4 - q])) * odd[q] for q in range(2))
        t = sum(float(0.5 * (matrix[p, q] + matrix[p, 4 - q])) * even[q] for q in range(2))
        t = t + float(matrix[p, 2]) * x[2]
        out[p] = s + t
        out[4 - p] = s - t
    out[2] = sum(float(matrix[2, q]) * odd[q] for q in range(2))
    return out


def kernel(
    ug, vg, rg, uc, vc, rc, lam, mu, defect, keep, rho, hist, cells, filt, perm, opg, opf, table,
    mem, out_v,
    pair_u, pair_v, pair_r, perm_v, opg_v, opf_v, tab_v,
    sw, qs, lam_v, mu_v, def_v, inv_mass,
    nd, ft, fs, yp, ym, rxm, rxp, rym, ryp, rdg,
    hy0, hy1, hy2, ry0, ry1, ry2, rc0, rc1, rc2, rlp, rl0, rl1, rl2,
    hist_v, cells_v, filt_v, fg_own, fgb, fgn, sj, frc,
    xr,
    keep_s, lsem, ready, h_send, h_recv, l_send, l_recv, f_send, f_recv, g_send, g_recv,
):
    s = lax.axis_index("slab")
    d = lax.axis_index("depth")
    ns = lax.axis_size("slab")
    nd_ = lax.axis_size("depth")
    sp, sm = lax.rem(s + 1, ns), lax.rem(s + ns - 1, ns)
    dp, dm = d + 1, d - 1

    barrier = pltpu.get_barrier_semaphore()

    def greet(*target):
        pl.semaphore_signal(barrier, inc=1, device_id=target, device_id_type=MESH)

    has_low, has_top = d > 0, d < nd_ - 1

    head, relay, tail = (lax.rem(s, ROW) == k for k in (0, 1, ROW - 1))
    not_head, not_tail = jnp.logical_not(head), jnp.logical_not(tail)
    row_before, row_after = lax.rem(s + ns - ROW + 1, ns), lax.rem(s + ROW - 1, ns)

    @pl.when(relay)
    def _():
        greet(row_after, d)

        @pl.when(has_top)
        def _():
            greet(row_after, dp)

    @pl.when(tail)
    def _():
        greet(s - (ROW - 2), d)

    @pl.when(jnp.logical_and(head, d >= 2))
    def _():
        greet(sm, 0)

    @pl.when(not_tail)
    def _():
        @pl.when(d == 0)
        def _():
            for k in (3, 2):
                greet(sp, k)

        @pl.when(has_low)
        def _():
            greet(sp, dm)

        @pl.when(has_top)
        def _():
            greet(sp, dp)

        greet(sp, d)

    @pl.when(d == 0)
    def _():
        for k in (3, 2):
            greet(s, k)

    @pl.when(has_low)
    def _():
        greet(sm, dm)
        greet(s, dm)

    @pl.when(has_top)
    def _():
        greet(sm, dp)
        greet(s, dp)

    greet(sm, d)
    low_n, top_n, far_n = (flag.astype(jnp.int32) for flag in (has_low, has_top, d >= 2))
    usual = 2 + 3 * low_n + 3 * top_n + 2 * far_n
    peers = jnp.where(
        head, 2 + 3 * low_n + 2 * top_n + far_n, usual + relay.astype(jnp.int32)
        + 2 * jnp.logical_and(tail, d == 0).astype(jnp.int32),
    )

    loads = []

    def load(src, dst):
        copy = pltpu.make_async_copy(src, dst, lsem.at[len(loads)])
        copy.start()
        loads.append(copy)
        return copy

    l_ug = load(ug, pair_u.at[:, 0:4])
    l_uc = load(uc, pair_u.at[:, 4:8])
    l_perm = load(perm, perm_v)
    l_opg = load(opg, opg_v)
    l_tab = load(table, tab_v)
    l_vg = load(vg, pair_v.at[:, 0:4])
    l_vc = load(vc, pair_v.at[:, 4:8])
    l_rho = load(rho, pair_r.at[:, 0:4])
    l_opf = load(opf, opf_v)
    zero7 = jnp.zeros((7, 128), F32)
    for w in range(2):
        for k in range(75):
            mem[w, k, 25:32, :] = zero7
    for a in range(5):
        lam_v[a, 25:32, :] = zero7
        mu_v[a, 25:32, :] = zero7
        def_v[a, 25:32, :] = zero7
    for x in range(4):
        hist_v[x, 64:72, :] = jnp.zeros((8, 128), F32)
    l_lam = load(lam.at[:, :, 0], lam_v.at[:, 0:25])
    l_mu = load(mu.at[:, :, 0], mu_v.at[:, 0:25])
    l_rg = load(rg.at[:, :, 0], mem.at[0, :, 0:25])
    l_def = load(defect.at[:, :, 0], def_v.at[:, 0:25])
    l_keep = load(keep, keep_s)
    l_cells = load(cells, cells_v)
    l_filt = load(filt, filt_v)
    l_hist = [load(hist.at[:, x], hist_v.at[x, 0:64]) for x in range(4)]
    l_rc = load(rc.at[:, :, 0], mem.at[1, :, 0:25])

    @pl.when(tail)
    def _():
        pl.semaphore_wait(barrier, peers)

        def announce(*target):
            pl.semaphore_signal(ready, inc=1, device_id=target, device_id_type=MESH)

        announce(sp, d)

        @pl.when(has_low)
        def _():
            announce(sp, dm)

        @pl.when(has_top)
        def _():
            announce(sp, dp)

        @pl.when(d == 0)
        def _():
            for k in (2, 3):
                announce(sp, k)

    zero24 = jnp.zeros((24, 128), F32)
    for a in range(4):
        for k in range(SLOTS):
            nd[a, k] = zero24
    for q in range(8):
        fgn[pl.ds(q * 24, 24), :] = zero24

    def deinterleave(ref, blocks):
        rows = blocks * 8
        x = ref[...].reshape(rows, 512)
        y = jnp.dot(jnp.concatenate(split3(x), axis=0), perm_v[...], preferred_element_type=F32)
        return y[0:rows] + y[rows : 2 * rows] + y[2 * rows : 3 * rows]

    l_perm.wait()
    l_ug.wait()
    l_uc.wait()
    y = deinterleave(pair_u, 12)
    for k in range(12):
        for c in range(4):
            lanes = slice(c * 128, c * 128 + 128)
            nd[k % 4, DISP[0] + k // 4, c * 5 : c * 5 + 4, :] = y[k * 8 : k * 8 + 4, lanes]
            nd[k % 4, DISP[1] + k // 4, c * 5 : c * 5 + 4, :] = y[k * 8 + 4 : k * 8 + 8, lanes]
    for a in range(4):
        for k in range(3):
            row = a * 12 + k * 4
            hy0[row : row + 4, :] = nd[a, k, pl.ds(0, 4, stride=5), :]
            hy1[row : row + 4, :] = nd[a, 3 + k, pl.ds(0, 4, stride=5), :]

    @pl.when(not_tail)
    def _():
        pl.semaphore_wait(barrier, peers)

    def remote(src, dst, send, recv, target):
        return pltpu.make_async_remote_copy(
            src_ref=src, dst_ref=dst, send_sem=send, recv_sem=recv, device_id=target, device_id_type=MESH
        )

    groups = [
        (slice(0, 3), hy0, ry0, rc0, rl0),
        (slice(3, 6), hy1, ry1, rc1, rl1),
        (slice(6, 13), hy2, ry2, rc2, rl2),
    ]

    def halo(g):
        slots, rows, recv_rows, corner, relay_corner = groups[g]
        size = corner.shape[0]
        side_src, corner_src = nd.at[0, slots], rows.at[0:size]
        below = remote(rows, recv_rows, h_send.at[g, 0], h_recv.at[g, 0], (s, dm))
        side = remote(side_src, nd.at[4, slots], h_send.at[g, 1], h_recv.at[g, 1], (sm, d))
        edge = remote(corner_src, corner, h_send.at[g, 2], h_recv.at[g, 2], (sm, dm))
        to_relay = (
            remote(side_src, rlp.at[slots], h_send.at[g, 1], l_recv.at[g, 0], (row_before, d)),
            remote(corner_src, relay_corner, h_send.at[g, 2], l_recv.at[g, 1], (row_before, dm)),
        )
        end = s + (ROW - 2)
        from_relay = (
            remote(rlp.at[slots], nd.at[4, slots], l_send.at[g, 0], h_recv.at[g, 1], (end, d)),
            remote(relay_corner, corner, l_send.at[g, 1], h_recv.at[g, 2], (end, d)),
        )
        return below, side, edge, to_relay, from_relay

    def halo_start(g):
        below, side, edge, to_relay, _ = halo(g)

        @pl.when(head)
        def _():
            to_relay[0].start()

            @pl.when(has_low)
            def _():
                to_relay[1].start()

        @pl.when(not_head)
        def _():
            side.start()

            @pl.when(has_low)
            def _():
                edge.start()

        @pl.when(has_low)
        def _():
            below.start()

    def forward(gs):
        @pl.when(relay)
        def _():
            for g in gs:
                _, _, _, to_relay, from_relay = halo(g)
                to_relay[0].wait_recv()
                from_relay[0].start()

                @pl.when(has_top)
                def _():
                    to_relay[1].wait_recv()
                    from_relay[1].start()

    def forward_wait(gs):
        @pl.when(relay)
        def _():
            for g in gs:
                from_relay = halo(g)[4]
                from_relay[0].wait_send()

                @pl.when(has_top)
                def _():
                    from_relay[1].wait_send()

    def halo_wait(g):
        below, side, edge, _, _ = halo(g)
        side.wait()

        @pl.when(has_low)
        def _():
            below.wait_send()
            edge.wait_send()

        @pl.when(has_top)
        def _():
            below.wait_recv()
            edge.wait_recv()

    halo_start(0)
    halo_start(1)
    forward((0, 1))

    l_vg.wait()
    l_vc.wait()
    l_rho.wait()
    y = deinterleave(pair_v, 12)
    for k in range(12):
        for c in range(4):
            lanes = slice(c * 128, c * 128 + 128)
            nd[k % 4, VEL[0] + k // 4, c * 5 : c * 5 + 4, :] = y[k * 8 : k * 8 + 4, lanes]
            nd[k % 4, VEL[1] + k // 4, c * 5 : c * 5 + 4, :] = y[k * 8 + 4 : k * 8 + 8, lanes]
    y = deinterleave(pair_r, 4)
    for k in range(4):
        for c in range(4):
            nd[k, RHO, c * 5 : c * 5 + 4, :] = y[k * 8 : k * 8 + 4, c * 128 : c * 128 + 128]
    for a in range(4):
        for k in range(7):
            row = a * 28 + k * 4
            hy2[row : row + 4, :] = nd[a, 6 + k, pl.ds(0, 4, stride=5), :]
    halo_start(2)

    @pl.when(d == nd_ - 1)
    def _():
        for ref in (ry0, ry1, ry2, rc0, rc1, rc2):
            ref[...] = jnp.ones(ref.shape, F32)
        for n in range(2 * STEPS):
            rym[n] = jnp.zeros((64, 128), F32)
            rdg[n, 0] = jnp.zeros((16, 128), F32)
            rdg[n, 2] = jnp.zeros((16, 128), F32)

    @pl.when(d == 0)
    def _():
        for n in range(2 * STEPS):
            ryp[n] = jnp.zeros((64, 128), F32)
            rdg[n, 1] = jnp.zeros((16, 128), F32)
            rdg[n, 3] = jnp.zeros((16, 128), F32)

    l_tab.wait()
    l_lam.wait()
    l_mu.wait()
    l_def.wait()
    weight_bc = tab_v[0]
    for a in range(5):
        weight = weight_bc * float(WGLL[a])
        two_mu = 2.0 * mu_v[a]
        lam_v[a] = weight * lam_v[a]
        mu_v[a] = weight * two_mu
        def_v[a] = two_mu * def_v[a]

    def relaxed(w):
        for a in range(5):
            weight = weight_bc * float(WGLL[a])
            for k in range(5):
                j = k * 5 + a
                sw[w, j] = weight * (mem[w, j] + mem[w, 25 + j] + mem[w, 50 + j])

    l_rg.wait()
    relaxed(0)

    l_cells.wait()
    l_filt.wait()
    for copy in l_hist:
        copy.wait()
    filt3 = jnp.concatenate(split3(filt_v[...]), axis=0)
    ids = lax.broadcasted_iota(jnp.int32, (256, 128), 0)
    for x in range(4):
        one_hot = jnp.where(ids == cells_v[x : x + 1, :], 1.0, 0.0).astype(BF16)
        g = jnp.dot(filt3, one_hot, preferred_element_type=F32)
        g = g[0:64] + g[64:128] + g[128:192]
        for t in range(4):
            fg_own[x * 8 + t : x * 8 + t + 1, :] = jnp.sum(
                g * hist_v[x, t + 1 : t + 65, :], axis=0, keepdims=True
            )
            fg_own[x * 8 + 4 + t : x * 8 + 5 + t, :] = g[63 - t : 64 - t]
    far = remote(fg_own.at[0:8], fgb.at[d, 32:40], g_send.at[0], g_recv.at[4 + d], (sm, 0))
    @pl.when(not_head)
    def _():
        far.start()

    @pl.when(d != 0)
    def _():
        remote(fg_own, fgb.at[d, 0:32], g_send.at[1], g_recv.at[d], (s, 0)).start()

    def strain_stress_force(w, t):
        opg_m = opg_v[...]
        comps = []
        for i in range(3):
            columns = []
            for a in range(5):
                u = nd[a, DISP[w] + i]
                u = jnp.concatenate([u, pltpu.roll(u[0:8], 127, 1)], axis=0)
                high, low = split2(u)
                columns.append(jnp.concatenate([high, low, high], axis=0))
            g = jnp.dot(opg_m, jnp.concatenate(columns, axis=1), preferred_element_type=F32)
            lanes = [slice(a * 128, a * 128 + 128) for a in range(5)]
            gx = derive([g[0:32, l] for l in lanes], DMAT)
            comps.append((gx, [g[32:64, l] for l in lanes], [g[64:96, l] for l in lanes]))
        fluxes = []
        for a in range(5):
            gx = [comps[i][0][a] for i in range(3)]
            gy = [comps[i][1][a] for i in range(3)]
            gz = [comps[i][2][a] for i in range(3)]
            xy = 0.5 * (gy[0] + gx[1])
            xz = 0.5 * (gz[0] + gx[2])
            yz = 0.5 * (gz[1] + gy[2])
            trace = gx[0] + gy[1] + gz[2]
            third = trace * (1.0 / 3.0)
            m, q = mu_v[a], def_v[a]
            for k, e in enumerate((gx[0] - third, gy[1] - third, xy, xz, yz)):
                qs[w, k * 5 + a] = q * e
            pressure = lam_v[a] * trace
            r = [sw[w, k * 5 + a] for k in range(5)]
            sxx = pressure + m * gx[0] - r[0]
            syy = pressure + m * gy[1] - r[1]
            szz = pressure + m * gz[2] + (r[0] + r[1])
            sxy = m * xy - r[2]
            sxz = m * xz - r[3]
            syz = m * yz - r[4]
            fluxes.append(((sxx, sxy, sxz), (sxy, syy, syz), (sxz, syz, szz)))
        opf_m = opf_v[...]
        for i in range(3):
            fx = derive([fluxes[a][0][i] for a in range(5)], DMAT.T)
            columns = []
            for a in range(5):
                y_high, y_low = split2(fluxes[a][1][i])
                z_high, z_low = split2(fluxes[a][2][i])
                x_high, x_low = split2(fx[a])
                columns.append(
                    jnp.concatenate([y_high, z_high, y_low, z_low, y_high, z_high, x_high, x_low], axis=0)
                )
            f = jnp.dot(opf_m, jnp.concatenate(columns, axis=1), preferred_element_type=F32)
            for a in range(5):
                fa = f[:, a * 128 : a * 128 + 128]
                fs[w, t, a, i, 0:8, :] = fa[0:8] + pltpu.roll(fa[24:32], 1, 1)
                fs[w, t, a, i, 8:24, :] = fa[8:24]

    below = (d < nd_ - 1).astype(F32)

    def messages(w, t):
        n = w * STEPS + t
        low = [
            (ym.at[n, 0:16], rdg.at[n, 0], (sm, dm)),
            (ym.at[n, 48:64], rdg.at[n, 2], (sp, dm)),
            (ym.at[n], rym.at[n], (s, dm)),
        ]
        top = [
            (yp.at[n, 0:16], rdg.at[n, 1], (sm, dp)),
            (yp.at[n, 48:64], rdg.at[n, 3], (sp, dp)),
            (yp.at[n], ryp.at[n], (s, dp)),
        ]
        side = [
            (fs.at[w, t, 0], rxm.at[n], (sm, d)),
            (fs.at[w, t, 4], rxp.at[n], (sp, d)),
        ]
        made = []
        for base, group in ((0, low), (3, top), (6, side)):
            made.append(
                [
                    remote(src, dst, f_send.at[n, base + j], f_recv.at[n, base + j], target)
                    for j, (src, dst, target) in enumerate(group)
                ]
            )
        return made

    def start_all(w, t):
        low, top, side = messages(w, t)

        @pl.when(has_low)
        def _():
            for copy in low[:2]:
                copy.start()

        @pl.when(has_top)
        def _():
            for copy in top[:2]:
                copy.start()

        for copy in side:
            copy.start()

        @pl.when(has_low)
        def _():
            low[2].start()

        @pl.when(has_top)
        def _():
            top[2].start()

    def wait_all(w, t, name):
        low, top, side = messages(w, t)
        for copy in side:
            getattr(copy, name)()
        sent = name == "wait_send"

        @pl.when(has_low if sent else has_top)
        def _():
            for copy in low:
                getattr(copy, name)()

        @pl.when(has_top if sent else has_low)
        def _():
            for copy in top:
                getattr(copy, name)()

    def send(w, t):
        n = w * STEPS + t
        for a in range(5):
            for i in range(3):
                row = a * 12 + i * 4
                ym[n, row : row + 4, :] = fs[w, t, a, i, pl.ds(0, 4, stride=5), :]
                yp[n, row : row + 4, :] = fs[w, t, a, i, pl.ds(4, 4, stride=5), :]
        ym[n, 60:64, :] = jnp.zeros((4, 128), F32)
        yp[n, 60:64, :] = jnp.zeros((4, 128), F32)
        start_all(w, t)

    l_keep.wait()
    kept = [keep_s[l] for l in range(3)]

    def memory(w, last):
        for a in range(5):
            weight = weight_bc * float(WGLL[a])
            for k in range(5):
                j = k * 5 + a
                q = qs[w, j]
                new = []
                for l in range(3):
                    value = kept[l] * mem[w, 25 * l + j] + (1.0 - kept[l]) * q
                    mem[w, 25 * l + j] = value
                    new.append(value)
                if not last:
                    sw[w, j] = weight * (new[0] + new[1] + new[2])

    def receive(w, t):
        n = w * STEPS + t
        wait_all(w, t, "wait_recv")
        for a in range(5):
            for i in range(3):
                f = fs[w, t, a, i]
                if a == 0:
                    f = f + rxp[n, i]
                if a == 4:
                    f = f + rxm[n, i]
                ft[a, i] = f
        for a in range(5):
            for i in range(3):
                row = a * 12 + i * 4
                low = ryp[n, row : row + 4, :]
                top = rym[n, row : row + 4, :]
                if a == 4:
                    low = low + rdg[n, 1, i * 4 : i * 4 + 4, :]
                    top = top + rdg[n, 0, i * 4 : i * 4 + 4, :]
                if a == 0:
                    low = low + rdg[n, 3, i * 4 : i * 4 + 4, :]
                    top = top + rdg[n, 2, i * 4 : i * 4 + 4, :]
                if w == 1 and i == 1:
                    low = low - frc[a * 4 : a * 4 + 4, :]
                at_low = (a, i, pl.ds(0, 4, stride=5), slice(None))
                at_top = (a, i, pl.ds(4, 4, stride=5), slice(None))
                ft[at_low] = ft[at_low] + low
                ft[at_top] = ft[at_top] + top

    def update(w):
        for a in range(5):
            scale = inv_mass[a]
            for i in range(3):
                v = nd[a, VEL[w] + i] - scale * ft[a, i]
                nd[a, VEL[w] + i] = v
                nd[a, DISP[w] + i] = nd[a, DISP[w] + i] + DT * v

    def sample(t):
        for a in range(5):
            sj[t, a * 4 : a * 4 + 4, :] = nd[a, DISP[0] + 1, pl.ds(0, 4, stride=5), :]

    def forcing(t):
        f = fgn[t * 24 : t * 24 + 24, :]
        for m in range(t + 1):
            f = f + fgn[(4 + m) * 24 : (5 + m) * 24, :] * sj[t - m]
        frc[...] = f

    def fill(g, count):
        slots, _, recv_rows, corner, _ = groups[g]
        first = slots.start
        for a in range(5):
            for k in range(count):
                row = (a * count + k) * 4
                top = corner[k * 4 : k * 4 + 4, :] if a == 4 else recv_rows[row : row + 4, :]
                nd[a, first + k, pl.ds(4, 4, stride=5), :] = top if first + k == RHO else below * top

    halo_wait(0)
    fill(0, 3)
    l_opg.wait()
    l_opf.wait()
    strain_stress_force(0, 0)

    @pl.when(head)
    def _():
        pl.semaphore_wait(ready, 1 + low_n + top_n + far_n)
        far.start()

    send(0, 0)

    forward((2,))
    l_rc.wait()
    relaxed(1)
    halo_wait(1)
    fill(1, 3)
    strain_stress_force(1, 0)
    send(1, 0)
    memory(0, False)
    halo_wait(2)
    fill(2, 7)
    first = (d == 0).astype(F32)
    row_factor = tab_v[1, 0:24] * (1.0 + first * tab_v[2, 0:24] - (1.0 - below) * tab_v[3, 0:24])
    for a in range(5):
        wx = float([0.2, 49.0 / 90.0, 32.0 / 45.0, 49.0 / 90.0, 0.2][a])
        inv_mass[a] = (DT / wx) * row_factor / (nd[a, RHO] + tab_v[4, 0:24])

    memory(1, False)

    def finish(w):
        for i in range(3):
            for x in range(4):
                row = (i * 4 + x) * 8
                for c in range(4):
                    xr[c, row : row + 4, :] = nd[x, DISP[w] + i, c * 5 : c * 5 + 4, :]
                    xr[c, row + 4 : row + 8, :] = nd[x, VEL[w] + i, c * 5 : c * 5 + 4, :]
        x = jnp.concatenate([xr[c] for c in range(4)], axis=1)
        y = lax.dot_general(
            jnp.concatenate(split3(x), axis=0), perm_v[...], (((1,), (1,)), ((), ())),
            preferred_element_type=F32,
        )
        out_v[w] = (y[0:96] + y[96:192] + y[192:288]).reshape(12, 8, 512)

    def gather():
        for j in range(1, 4):
            remote(fg_own, fgb.at[j, 0:32], g_send.at[1], g_recv.at[j], (s, 0)).wait_recv()
        for j in range(4):
            remote(fg_own.at[0:8], fgb.at[j, 32:40], g_send.at[0], g_recv.at[4 + j], (sm, 0)).wait_recv()
        fgb[0, 0:32, :] = fg_own[...]
        x = jnp.concatenate([fgb[j] for j in range(4)], axis=1)
        y = jnp.dot(jnp.concatenate(split3(x), axis=0), perm_v[...], preferred_element_type=F32)
        y = y[0:40] + y[40:80] + y[80:120]
        for a in range(5):
            for c in range(4):
                fgn[pl.ds(a * 4 + c, 8, stride=24), :] = y[a * 8 : a * 8 + 8, c * 128 : c * 128 + 128]

    for t in range(STEPS):
        receive(0, t)
        update(0)
        if t < STEPS - 1:
            strain_stress_force(0, t + 1)
            send(0, t + 1)
        sample(t)
        if t == 0:
            pl.when(d == 0)(gather)
        forcing(t)
        if t < STEPS - 1:
            if t > 0:
                memory(1, False)
        else:
            memory(1, True)
            finish(0)
        receive(1, t)
        update(1)
        if t < STEPS - 1:
            strain_stress_force(1, t + 1)
            send(1, t + 1)
            memory(0, t == STEPS - 2)
        else:
            finish(1)
    forward_wait((0, 1, 2))
    far.wait_send()

    @pl.when(d != 0)
    def _():
        remote(fg_own, fgb.at[d, 0:32], g_send.at[1], g_recv.at[d], (s, 0)).wait_send()
    for w in range(2):
        for t in range(STEPS):
            wait_all(w, t, "wait_send")


def write_kernel(mem, out_v, ug_o, vg_o, rg_o, uc_o, vc_o, rc_o, sem):
    pairs = [
        (mem.at[0, :, 0:25], rg_o.at[:, :, 0]),
        (mem.at[1, :, 0:25], rc_o.at[:, :, 0]),
        (out_v.at[0, :, 0:4], ug_o),
        (out_v.at[0, :, 4:8], vg_o),
        (out_v.at[1, :, 0:4], uc_o),
        (out_v.at[1, :, 4:8], vc_o),
    ]
    copies = [pltpu.make_async_copy(src, dst, sem.at[j]) for j, (src, dst) in enumerate(pairs)]
    for copy in copies:
        copy.start()
    for copy in copies:
        copy.wait()


def body(*args):
    (ug, vg, rg, uc, vc, rc, lam, mu, defect, keep, rho, hist, cells, filt) = args
    gradient, force = operators()
    operands = (
        ug.reshape(12, 4, 512), vg.reshape(12, 4, 512), rg.reshape(75, 25, 1, 128),
        uc.reshape(12, 4, 512), vc.reshape(12, 4, 512), rc.reshape(75, 25, 1, 128),
        lam.reshape(5, 25, 1, 128), mu.reshape(5, 25, 1, 128), defect.reshape(5, 25, 1, 128),
        keep, rho, hist, cells, filt.T,
        jnp.asarray(interleave()), jnp.asarray(gradient), jnp.asarray(force), jnp.asarray(tables()),
    )
    operands = tuple(
        pltpu.with_memory_space_constraint(x, pltpu.HBM) for x in operands
    )
    in_hbm = pl.BlockSpec(memory_space=pltpu.HBM)
    in_vmem = pl.BlockSpec(memory_space=pltpu.VMEM)
    in_specs = [in_hbm] * len(operands)
    nodal = pltpu.HBM((12, 4, 512), F32)
    points = pltpu.HBM((75, 25, 1, 128), F32)
    dma = pltpu.SemaphoreType.DMA
    vm = lambda *shape: pltpu.VMEM(shape, F32)
    waves = 2 * STEPS
    results = pl.pallas_call(
        kernel,
        out_shape=(vm(2, 75, 32, 128), vm(2, 12, 8, 512)),
        in_specs=in_specs,
        out_specs=(in_vmem,) * 2,
        scratch_shapes=[
            vm(12, 8, 512), vm(12, 8, 512), vm(4, 8, 512),
            pltpu.VMEM((512, 512), BF16), pltpu.VMEM((96, 96), BF16), pltpu.VMEM((32, 256), BF16),
            vm(5, 32, 128),
            vm(2, 25, 32, 128), vm(2, 25, 32, 128),
            vm(5, 32, 128), vm(5, 32, 128), vm(5, 32, 128), vm(5, 24, 128),
            vm(5, SLOTS, 24, 128), vm(5, 3, 24, 128), vm(2, STEPS, 5, 3, 24, 128),
            vm(waves, 64, 128), vm(waves, 64, 128),
            vm(waves, 3, 24, 128), vm(waves, 3, 24, 128),
            vm(waves, 64, 128), vm(waves, 64, 128), vm(waves, 4, 16, 128),
            vm(48, 128), vm(48, 128), vm(112, 128), vm(48, 128), vm(48, 128), vm(112, 128),
            vm(16, 128), vm(16, 128), vm(32, 128), vm(SLOTS, 24, 128), vm(16, 128), vm(16, 128), vm(32, 128),
            vm(4, 72, 128), pltpu.VMEM((4, 128), jnp.int32), vm(64, 256),
            vm(32, 128), vm(4, 40, 128), vm(192, 128), vm(STEPS, 24, 128), vm(24, 128),
            vm(4, 96, 128),
            pltpu.SMEM((3,), F32), dma((24,)), pltpu.SemaphoreType.REGULAR,
            dma((3, 3)), dma((3, 3)), dma((3, 2)), dma((3, 2)), dma((waves, 8)), dma((waves, 8)),
            dma((2,)), dma((8,)),
        ],
        compiler_params=pltpu.CompilerParams(
            collective_id=0, has_side_effects=True, vmem_limit_bytes=40 * 1024 * 1024
        ),
    )(*operands)
    outs = pl.pallas_call(
        write_kernel,
        out_shape=(nodal, nodal, points, nodal, nodal, points),
        in_specs=(in_vmem,) * 2,
        out_specs=(in_hbm,) * 6,
        scratch_shapes=[dma((6,))],
        compiler_params=pltpu.CompilerParams(vmem_limit_bytes=1024 * 1024),
    )(*(pltpu.with_memory_space_constraint(x, pltpu.VMEM) for x in results))
    full = (3, 5, 5, 5, 5, 1, 1, 128)
    u = (3, 4, 4, 512)
    return (
        outs[0].reshape(u), outs[1].reshape(u), outs[2].reshape(full),
        outs[3].reshape(u), outs[4].reshape(u), outs[5].reshape(full),
    )


def solution(mesh):
    nodal = P(None, "slab", "depth", None)
    points = P(None, None, None, None, None, "slab", "depth", None)
    material = P(None, None, None, "slab", "depth", None)
    return jax.shard_map(
        body,
        mesh=mesh,
        in_specs=(
            nodal, nodal, points, nodal, nodal, points, material, material, material, P(),
            P("slab", "depth", None), P(None, "slab", "depth"), P("slab", "depth"), P(),
        ),
        out_specs=(nodal, nodal, points, nodal, nodal, points),
        check_vma=False,
    )
```

```python
import functools

import jax
import jax.numpy as jnp
import ml_dtypes
import numpy as np
from jax import lax
from jax.experimental import pallas as pl
from jax.experimental.pallas import tpu as pltpu
from jax.sharding import PartitionSpec as P

STEPS = 4
TAPS = 64
DT = 0.04
F32 = jnp.float32
BF16 = jnp.bfloat16
MESH = pl.DeviceIdType.MESH
ROW = 8

DISP = (0, 3)
VEL = (6, 9)
RHO = 12
SLOTS = 13


def gll_tables():
    points = np.array([-1.0, -np.sqrt(3.0 / 7.0), 0.0, np.sqrt(3.0 / 7.0), 1.0])
    weights = np.array([0.1, 49.0 / 90.0, 32.0 / 45.0, 49.0 / 90.0, 0.1])
    products = np.array([np.prod([points[t] - points[o] for o in range(5) if o != t]) for t in range(5)])
    derivative = np.zeros((5, 5))
    for t in range(5):
        for s in range(5):
            if t == s:
                derivative[t, s] = np.sum([1.0 / (points[t] - points[o]) for o in range(5) if o != t])
            else:
                derivative[t, s] = products[t] / products[s] / (points[t] - points[s])
    return derivative, weights


DMAT, WGLL = gll_tables()


def node_row(b, c):
    return c * 5 + b if c < 4 else 24 + b


def halves(matrix):
    high = matrix.astype(ml_dtypes.bfloat16)
    low = (matrix - high.astype(np.float64)).astype(ml_dtypes.bfloat16)
    return high, low


def operators():
    same = np.zeros((32, 32))
    along_y = np.zeros((32, 32))
    along_z = np.zeros((32, 32))
    for b in range(5):
        for c in range(5):
            row = b * 5 + c
            same[row, node_row(b, c)] = 1.0
            for q in range(5):
                along_y[row, node_row(q, c)] = DMAT[b, q]
                along_z[row, node_row(b, q)] = DMAT[c, q]
    high, low = halves(np.concatenate([same, along_y, along_z], axis=0))
    gradient = np.concatenate([high, high, low], axis=1)
    y_high, y_low = halves(along_y.T)
    z_high, z_low = halves(along_z.T)
    back = same.T.astype(ml_dtypes.bfloat16)
    force = np.concatenate([y_high, z_high, y_high, z_high, y_low, z_low, back, back], axis=1)
    return gradient, force


def tables():
    table = np.zeros((5, 32, 128), np.float32)
    wn = np.array([0.2, 49.0 / 90.0, 32.0 / 45.0, 49.0 / 90.0, 0.2])
    for b in range(5):
        for c in range(5):
            table[0, b * 5 + c] = WGLL[b] * WGLL[c]
        for c in range(4):
            row = node_row(b, c)
            table[1, row] = 1.0 / (wn[b] * wn[c])
            table[2, row] = float(b == 0)
            table[3, row] = float(b == 4)
    table[4, 20:] = 1.0
    return table


def interleave():
    table = np.zeros((512, 512), np.float32)
    for c in range(4):
        for e in range(128):
            table[4 * e + c, c * 128 + e] = 1.0
    return table.astype(ml_dtypes.bfloat16)


def split2(x):
    high = x.astype(BF16)
    return high, (x - high.astype(F32)).astype(BF16)


def split3(x):
    high = x.astype(BF16)
    rest = x - high.astype(F32)
    middle = rest.astype(BF16)
    return high, middle, (rest - middle.astype(F32)).astype(BF16)


def derive(x, matrix):
    even = [x[0] + x[4], x[1] + x[3]]
    odd = [x[0] - x[4], x[1] - x[3]]
    out = [None] * 5
    for p in range(2):
        s = sum(float(0.5 * (matrix[p, q] - matrix[p, 4 - q])) * odd[q] for q in range(2))
        t = sum(float(0.5 * (matrix[p, q] + matrix[p, 4 - q])) * even[q] for q in range(2))
        t = t + float(matrix[p, 2]) * x[2]
        out[p] = s + t
        out[4 - p] = s - t
    out[2] = sum(float(matrix[2, q]) * odd[q] for q in range(2))
    return out


def kernel(
    ug, vg, rg, uc, vc, rc, lam, mu, defect, keep, rho, hist, cells, filt, perm, opg, opf, table,
    mem, out_v,
    pair_u, pair_v, pair_r, perm_v, opg_v, opf_v, tab_v,
    sw, qs, lam_v, mu_v, def_v, inv_mass,
    nd, ft, fs, cr, yp, ym, rxm, rxp, rym, ryp, rdg,
    hy0, hy1, hy2, ry0, ry1, ry2, rc0, rc1, rc2, rlp, rl0, rl1, rl2, rlf,
    hist_v, cells_v, filt_v, fg_own, fgb, fgn, sj, frc,
    xr,
    keep_s, lsem, ready, r_send, r_recv, h_send, h_recv, l_send, l_recv, f_send, f_recv, g_send, g_recv,
):
    s = lax.axis_index("slab")
    d = lax.axis_index("depth")
    ns = lax.axis_size("slab")
    nd_ = lax.axis_size("depth")
    sp, sm = lax.rem(s + 1, ns), lax.rem(s + ns - 1, ns)
    dp, dm = d + 1, d - 1

    barrier = pltpu.get_barrier_semaphore()

    def greet(*target):
        pl.semaphore_signal(barrier, inc=1, device_id=target, device_id_type=MESH)

    has_low, has_top = d > 0, d < nd_ - 1

    head, relay, tail = (lax.rem(s, ROW) == k for k in (0, 1, ROW - 1))
    not_head, not_tail = jnp.logical_not(head), jnp.logical_not(tail)
    row_before, row_after = lax.rem(s + ns - ROW + 1, ns), lax.rem(s + ROW - 1, ns)

    @pl.when(relay)
    def _():
        greet(row_after, d)

        @pl.when(has_top)
        def _():
            greet(row_after, dp)

    @pl.when(tail)
    def _():
        greet(s - (ROW - 2), d)

        @pl.when(d == 0)
        def _():
            for k in (1, 2, 3):
                greet(s - (ROW - 2), k)

    @pl.when(not_tail)
    def _():
        @pl.when(d == 0)
        def _():
            for k in (3, 2):
                greet(sp, k)

        @pl.when(has_low)
        def _():
            greet(sp, dm)

        @pl.when(has_top)
        def _():
            greet(sp, dp)

        greet(sp, d)

    @pl.when(d == 0)
    def _():
        for k in (3, 2):
            greet(s, k)

    @pl.when(has_low)
    def _():
        greet(sm, dm)
        greet(s, dm)

    @pl.when(has_top)
    def _():
        greet(sm, dp)
        greet(s, dp)

    greet(sm, d)
    low_n, top_n, far_n = (flag.astype(jnp.int32) for flag in (has_low, has_top, d >= 2))
    usual = 2 + 3 * low_n + 3 * top_n + 2 * far_n
    peers = jnp.where(
        head,
        2 + 3 * low_n + 2 * top_n + far_n,
        usual + relay.astype(jnp.int32) * (1 + low_n),
    )

    loads = []

    def load(src, dst):
        copy = pltpu.make_async_copy(src, dst, lsem.at[len(loads)])
        copy.start()
        loads.append(copy)
        return copy

    l_ug = load(ug, pair_u.at[:, 0:4])
    l_uc = load(uc, pair_u.at[:, 4:8])
    l_perm = load(perm, perm_v)
    l_opg = load(opg, opg_v)
    l_tab = load(table, tab_v)
    l_vg = load(vg, pair_v.at[:, 0:4])
    l_vc = load(vc, pair_v.at[:, 4:8])
    l_rho = load(rho, pair_r.at[:, 0:4])
    l_opf = load(opf, opf_v)
    zero7 = jnp.zeros((7, 128), F32)
    for w in range(2):
        for k in range(75):
            mem[w, k, 25:32, :] = zero7
    for a in range(5):
        lam_v[a, 25:32, :] = zero7
        mu_v[a, 25:32, :] = zero7
        def_v[a, 25:32, :] = zero7
    for x in range(4):
        hist_v[x, 64:72, :] = jnp.zeros((8, 128), F32)
    l_lam = load(lam.at[:, :, 0], lam_v.at[:, 0:25])
    l_mu = load(mu.at[:, :, 0], mu_v.at[:, 0:25])
    l_rg = load(rg.at[:, :, 0], mem.at[0, :, 0:25])
    l_def = load(defect.at[:, :, 0], def_v.at[:, 0:25])
    l_keep = load(keep, keep_s)
    l_cells = load(cells, cells_v)
    l_filt = load(filt, filt_v)
    l_hist = [load(hist.at[:, x], hist_v.at[x, 0:64]) for x in range(4)]
    l_rc = load(rc.at[:, :, 0], mem.at[1, :, 0:25])

    @pl.when(tail)
    def _():
        pl.semaphore_wait(barrier, peers)

        def announce(*target):
            pl.semaphore_signal(ready, inc=1, device_id=target, device_id_type=MESH)

        announce(sp, d)

        @pl.when(has_low)
        def _():
            announce(sp, dm)

        @pl.when(has_top)
        def _():
            announce(sp, dp)

    zero24 = jnp.zeros((24, 128), F32)
    for a in range(4):
        for k in range(SLOTS):
            nd[a, k] = zero24
    for q in range(8):
        fgn[pl.ds(q * 24, 24), :] = zero24

    def deinterleave(ref, blocks):
        rows = blocks * 8
        x = ref[...].reshape(rows, 512)
        y = jnp.dot(jnp.concatenate(split3(x), axis=0), perm_v[...], preferred_element_type=F32)
        return y[0:rows] + y[rows : 2 * rows] + y[2 * rows : 3 * rows]

    l_perm.wait()
    l_ug.wait()
    l_uc.wait()
    y = deinterleave(pair_u, 12)
    for k in range(12):
        for c in range(4):
            lanes = slice(c * 128, c * 128 + 128)
            nd[k % 4, DISP[0] + k // 4, c * 5 : c * 5 + 4, :] = y[k * 8 : k * 8 + 4, lanes]
            nd[k % 4, DISP[1] + k // 4, c * 5 : c * 5 + 4, :] = y[k * 8 + 4 : k * 8 + 8, lanes]
    for a in range(4):
        for k in range(3):
            row = a * 12 + k * 4
            hy0[row : row + 4, :] = nd[a, k, pl.ds(0, 4, stride=5), :]
            hy1[row : row + 4, :] = nd[a, 3 + k, pl.ds(0, 4, stride=5), :]

    @pl.when(not_tail)
    def _():
        pl.semaphore_wait(barrier, peers)

    def remote(src, dst, send, recv, target):
        return pltpu.make_async_remote_copy(
            src_ref=src, dst_ref=dst, send_sem=send, recv_sem=recv, device_id=target, device_id_type=MESH
        )

    groups = [
        (slice(0, 3), hy0, ry0, rc0, rl0),
        (slice(3, 6), hy1, ry1, rc1, rl1),
        (slice(6, 13), hy2, ry2, rc2, rl2),
    ]

    def halo(g):
        slots, rows, recv_rows, corner, relay_corner = groups[g]
        size = corner.shape[0]
        side_src, corner_src = nd.at[0, slots], rows.at[0:size]
        below = remote(rows, recv_rows, h_send.at[g, 0], h_recv.at[g, 0], (s, dm))
        side = remote(side_src, nd.at[4, slots], h_send.at[g, 1], h_recv.at[g, 1], (sm, d))
        edge = remote(corner_src, corner, h_send.at[g, 2], h_recv.at[g, 2], (sm, dm))
        to_relay = (
            remote(side_src, rlp.at[slots], h_send.at[g, 1], l_recv.at[g, 0], (row_before, d)),
            remote(corner_src, relay_corner, h_send.at[g, 2], l_recv.at[g, 1], (row_before, dm)),
        )
        end = s + (ROW - 2)
        from_relay = (
            remote(rlp.at[slots], nd.at[4, slots], l_send.at[g, 0], h_recv.at[g, 1], (end, d)),
            remote(relay_corner, corner, l_send.at[g, 1], h_recv.at[g, 2], (end, d)),
        )
        return below, side, edge, to_relay, from_relay

    def halo_start(g):
        below, side, edge, to_relay, _ = halo(g)

        @pl.when(head)
        def _():
            to_relay[0].start()

            @pl.when(has_low)
            def _():
                to_relay[1].start()

        @pl.when(not_head)
        def _():
            side.start()

            @pl.when(has_low)
            def _():
                edge.start()

        @pl.when(has_low)
        def _():
            below.start()

    def forward(gs):
        @pl.when(relay)
        def _():
            for g in gs:
                _, _, _, to_relay, from_relay = halo(g)
                to_relay[0].wait_recv()
                from_relay[0].start()

                @pl.when(has_top)
                def _():
                    to_relay[1].wait_recv()
                    from_relay[1].start()

    def forward_wait(gs):
        @pl.when(relay)
        def _():
            for g in gs:
                from_relay = halo(g)[4]
                from_relay[0].wait_send()

                @pl.when(has_top)
                def _():
                    from_relay[1].wait_send()

    def halo_wait(g):
        below, side, edge, _, _ = halo(g)
        side.wait()

        @pl.when(has_low)
        def _():
            below.wait_send()
            edge.wait_send()

        @pl.when(has_top)
        def _():
            below.wait_recv()
            edge.wait_recv()

    halo_start(0)
    halo_start(1)
    forward((0, 1))

    l_vg.wait()
    l_vc.wait()
    l_rho.wait()
    y = deinterleave(pair_v, 12)
    for k in range(12):
        for c in range(4):
            lanes = slice(c * 128, c * 128 + 128)
            nd[k % 4, VEL[0] + k // 4, c * 5 : c * 5 + 4, :] = y[k * 8 : k * 8 + 4, lanes]
            nd[k % 4, VEL[1] + k // 4, c * 5 : c * 5 + 4, :] = y[k * 8 + 4 : k * 8 + 8, lanes]
    y = deinterleave(pair_r, 4)
    for k in range(4):
        for c in range(4):
            nd[k, RHO, c * 5 : c * 5 + 4, :] = y[k * 8 : k * 8 + 4, c * 128 : c * 128 + 128]
    for a in range(4):
        for k in range(7):
            row = a * 28 + k * 4
            hy2[row : row + 4, :] = nd[a, 6 + k, pl.ds(0, 4, stride=5), :]
    halo_start(2)

    @pl.when(d == nd_ - 1)
    def _():
        for ref in (ry0, ry1, ry2, rc0, rc1, rc2):
            ref[...] = jnp.ones(ref.shape, F32)
        for n in range(2 * STEPS):
            rym[n] = jnp.zeros((64, 128), F32)
            rdg[n, 0] = jnp.zeros((16, 128), F32)
            rdg[n, 2] = jnp.zeros((16, 128), F32)

    @pl.when(d == 0)
    def _():
        for n in range(2 * STEPS):
            ryp[n] = jnp.zeros((64, 128), F32)
            rdg[n, 1] = jnp.zeros((16, 128), F32)
            rdg[n, 3] = jnp.zeros((16, 128), F32)

    l_tab.wait()
    l_lam.wait()
    l_mu.wait()
    l_def.wait()
    weight_bc = tab_v[0]
    for a in range(5):
        weight = weight_bc * float(WGLL[a])
        two_mu = 2.0 * mu_v[a]
        lam_v[a] = weight * lam_v[a]
        mu_v[a] = weight * two_mu
        def_v[a] = two_mu * def_v[a]

    def relaxed(w):
        for a in range(5):
            weight = weight_bc * float(WGLL[a])
            for k in range(5):
                j = k * 5 + a
                sw[w, j] = weight * (mem[w, j] + mem[w, 25 + j] + mem[w, 50 + j])

    l_rg.wait()
    relaxed(0)

    l_cells.wait()
    l_filt.wait()
    for copy in l_hist:
        copy.wait()
    filt3 = jnp.concatenate(split3(filt_v[...]), axis=0)
    ids = lax.broadcasted_iota(jnp.int32, (256, 128), 0)
    for x in range(4):
        one_hot = jnp.where(ids == cells_v[x : x + 1, :], 1.0, 0.0).astype(BF16)
        g = jnp.dot(filt3, one_hot, preferred_element_type=F32)
        g = g[0:64] + g[64:128] + g[128:192]
        for t in range(4):
            fg_own[x * 8 + t : x * 8 + t + 1, :] = jnp.sum(
                g * hist_v[x, t + 1 : t + 65, :], axis=0, keepdims=True
            )
            fg_own[x * 8 + 4 + t : x * 8 + 5 + t, :] = g[63 - t : 64 - t]
    far = remote(fg_own.at[0:8], fgb.at[d, 32:40], g_send.at[0], g_recv.at[4 + d], (sm, 0))
    far_to_relay = remote(fg_own.at[0:8], rlf, g_send.at[0], r_recv.at[0], (row_before, d))
    far_from_relay = remote(rlf, fgb.at[d, 32:40], r_send.at[0], g_recv.at[4 + d], (s + (ROW - 2), 0))

    @pl.when(not_head)
    def _():
        far.start()

    @pl.when(head)
    def _():
        far_to_relay.start()

    @pl.when(d != 0)
    def _():
        remote(fg_own, fgb.at[d, 0:32], g_send.at[1], g_recv.at[d], (s, 0)).start()

    def strain_stress(w, t):
        opg_m = opg_v[...]
        comps = []
        for i in range(3):
            columns = []
            for a in range(5):
                u = nd[a, DISP[w] + i]
                u = jnp.concatenate([u, pltpu.roll(u[0:8], 127, 1)], axis=0)
                high, low = split2(u)
                columns.append(jnp.concatenate([high, low, high], axis=0))
            g = jnp.dot(opg_m, jnp.concatenate(columns, axis=1), preferred_element_type=F32)
            lanes = [slice(a * 128, a * 128 + 128) for a in range(5)]
            gx = derive([g[0:32, l] for l in lanes], DMAT)
            comps.append((gx, [g[32:64, l] for l in lanes], [g[64:96, l] for l in lanes]))
        fluxes = []
        for a in range(5):
            gx = [comps[i][0][a] for i in range(3)]
            gy = [comps[i][1][a] for i in range(3)]
            gz = [comps[i][2][a] for i in range(3)]
            xy = 0.5 * (gy[0] + gx[1])
            xz = 0.5 * (gz[0] + gx[2])
            yz = 0.5 * (gz[1] + gy[2])
            trace = gx[0] + gy[1] + gz[2]
            third = trace * (1.0 / 3.0)
            m, q = mu_v[a], def_v[a]
            for k, e in enumerate((gx[0] - third, gy[1] - third, xy, xz, yz)):
                qs[w, k * 5 + a] = q * e
            pressure = lam_v[a] * trace
            r = [sw[w, k * 5 + a] for k in range(5)]
            sxx = pressure + m * gx[0] - r[0]
            syy = pressure + m * gy[1] - r[1]
            szz = pressure + m * gz[2] + (r[0] + r[1])
            sxy = m * xy - r[2]
            sxz = m * xz - r[3]
            syz = m * yz - r[4]
            fluxes.append(((sxx, sxy, sxz), (sxy, syy, syz), (sxz, syz, szz)))
        flux_x = [derive([fluxes[a][0][i] for a in range(5)], DMAT.T) for i in range(3)]

        def force(planes):
            columns = []
            for a in planes:
                for i in range(3):
                    y_high, y_low = split2(fluxes[a][1][i])
                    z_high, z_low = split2(fluxes[a][2][i])
                    x_high, x_low = split2(flux_x[i][a])
                    columns.append(
                        jnp.concatenate([y_high, z_high, y_low, z_low, y_high, z_high, x_high, x_low], axis=0)
                    )
            f = jnp.dot(opf_v[...], jnp.concatenate(columns, axis=1), preferred_element_type=F32)
            for k, a in enumerate(planes):
                for i in range(3):
                    lane = (k * 3 + i) * 128
                    fa = f[:, lane : lane + 128]
                    fs[w, t, a, i, 0:8, :] = fa[0:8] + pltpu.roll(fa[24:32], 1, 1)
                    fs[w, t, a, i, 8:24, :] = fa[8:24]

        return force

    below = (d < nd_ - 1).astype(F32)

    def messages(w, t):
        n = w * STEPS + t
        low = [
            (cr.at[n, 0, 0:12], rdg.at[n, 0, 0:12], (sm, dm)),
            (cr.at[n, 2, 0:12], rdg.at[n, 2, 0:12], (sp, dm)),
            (ym.at[n, 0:60], rym.at[n, 0:60], (s, dm)),
        ]
        top = [
            (cr.at[n, 1, 0:12], rdg.at[n, 1, 0:12], (sm, dp)),
            (cr.at[n, 3, 0:12], rdg.at[n, 3, 0:12], (sp, dp)),
            (yp.at[n, 0:60], ryp.at[n, 0:60], (s, dp)),
        ]
        side = [
            (fs.at[w, t, 0, :, 0:20], rxm.at[n, :, 0:20], (sm, d)),
            (fs.at[w, t, 4, :, 0:20], rxp.at[n, :, 0:20], (sp, d)),
        ]
        made = []
        for base, group in ((0, low), (3, top), (6, side)):
            made.append(
                [
                    remote(src, dst, f_send.at[n, base + j], f_recv.at[n, base + j], target)
                    for j, (src, dst, target) in enumerate(group)
                ]
            )
        return made

    def start_outer(w, t):
        low, top, side = messages(w, t)

        @pl.when(has_low)
        def _():
            for copy in low[:2]:
                copy.start()

        @pl.when(has_top)
        def _():
            for copy in top[:2]:
                copy.start()

        for copy in side:
            copy.start()

    def start_inner(w, t):
        low, top, _ = messages(w, t)

        @pl.when(has_low)
        def _():
            low[2].start()

        @pl.when(has_top)
        def _():
            top[2].start()

    def wait_all(w, t, name):
        low, top, side = messages(w, t)
        for copy in side:
            getattr(copy, name)()
        sent = name == "wait_send"

        @pl.when(has_low if sent else has_top)
        def _():
            for copy in low:
                getattr(copy, name)()

        @pl.when(has_top if sent else has_low)
        def _():
            for copy in top:
                getattr(copy, name)()

    def step(w, t, gate=None):
        n = w * STEPS + t
        force = strain_stress(w, t)
        force((0, 4))
        for k, a in enumerate((0, 4)):
            for i in range(3):
                for b in range(2):
                    cr[n, 2 * k + b, i * 4 : i * 4 + 4, :] = fs[w, t, a, i, pl.ds(4 * b, 4, stride=5), :]
        if gate is not None:
            gate()
        start_outer(w, t)
        force((1, 2, 3))
        for a in range(5):
            for i in range(3):
                row = a * 12 + i * 4
                ym[n, row : row + 4, :] = fs[w, t, a, i, pl.ds(0, 4, stride=5), :]
                yp[n, row : row + 4, :] = fs[w, t, a, i, pl.ds(4, 4, stride=5), :]
        start_inner(w, t)

    l_keep.wait()
    kept = [keep_s[l] for l in range(3)]

    def memory(w, last):
        for a in range(5):
            weight = weight_bc * float(WGLL[a])
            for k in range(5):
                j = k * 5 + a
                q = qs[w, j]
                new = []
                for l in range(3):
                    value = kept[l] * mem[w, 25 * l + j] + (1.0 - kept[l]) * q
                    mem[w, 25 * l + j] = value
                    new.append(value)
                if not last:
                    sw[w, j] = weight * (new[0] + new[1] + new[2])

    def receive(w, t):
        n = w * STEPS + t
        wait_all(w, t, "wait_recv")
        for a in range(5):
            for i in range(3):
                f = fs[w, t, a, i]
                if a == 0:
                    f = f + rxp[n, i]
                if a == 4:
                    f = f + rxm[n, i]
                ft[a, i] = f
        for a in range(5):
            for i in range(3):
                row = a * 12 + i * 4
                low = ryp[n, row : row + 4, :]
                top = rym[n, row : row + 4, :]
                if a == 4:
                    low = low + rdg[n, 1, i * 4 : i * 4 + 4, :]
                    top = top + rdg[n, 0, i * 4 : i * 4 + 4, :]
                if a == 0:
                    low = low + rdg[n, 3, i * 4 : i * 4 + 4, :]
                    top = top + rdg[n, 2, i * 4 : i * 4 + 4, :]
                if w == 1 and i == 1:
                    low = low - frc[a * 4 : a * 4 + 4, :]
                at_low = (a, i, pl.ds(0, 4, stride=5), slice(None))
                at_top = (a, i, pl.ds(4, 4, stride=5), slice(None))
                ft[at_low] = ft[at_low] + low
                ft[at_top] = ft[at_top] + top

    def update(w):
        for a in range(5):
            scale = inv_mass[a]
            for i in range(3):
                v = nd[a, VEL[w] + i] - scale * ft[a, i]
                nd[a, VEL[w] + i] = v
                nd[a, DISP[w] + i] = nd[a, DISP[w] + i] + DT * v

    def sample(t):
        for a in range(5):
            sj[t, a * 4 : a * 4 + 4, :] = nd[a, DISP[0] + 1, pl.ds(0, 4, stride=5), :]

    def forcing(t):
        f = fgn[t * 24 : t * 24 + 24, :]
        for m in range(t + 1):
            f = f + fgn[(4 + m) * 24 : (5 + m) * 24, :] * sj[t - m]
        frc[...] = f

    def fill(g, count):
        slots, _, recv_rows, corner, _ = groups[g]
        first = slots.start
        for a in range(5):
            for k in range(count):
                row = (a * count + k) * 4
                top = corner[k * 4 : k * 4 + 4, :] if a == 4 else recv_rows[row : row + 4, :]
                nd[a, first + k, pl.ds(4, 4, stride=5), :] = top if first + k == RHO else below * top

    halo_wait(0)
    fill(0, 3)
    l_opg.wait()
    l_opf.wait()

    def gate():
        @pl.when(head)
        def _():
            pl.semaphore_wait(ready, 1 + low_n + top_n)

    step(0, 0, gate)

    forward((2,))

    @pl.when(relay)
    def _():
        far_to_relay.wait_recv()
        far_from_relay.start()

    l_rc.wait()
    relaxed(1)
    halo_wait(1)
    fill(1, 3)
    step(1, 0)
    memory(0, False)
    halo_wait(2)
    fill(2, 7)
    first = (d == 0).astype(F32)
    row_factor = tab_v[1, 0:24] * (1.0 + first * tab_v[2, 0:24] - (1.0 - below) * tab_v[3, 0:24])
    for a in range(5):
        wx = float([0.2, 49.0 / 90.0, 32.0 / 45.0, 49.0 / 90.0, 0.2][a])
        inv_mass[a] = (DT / wx) * row_factor / (nd[a, RHO] + tab_v[4, 0:24])

    memory(1, False)

    def finish(w):
        for i in range(3):
            for x in range(4):
                row = (i * 4 + x) * 8
                for c in range(4):
                    xr[c, row : row + 4, :] = nd[x, DISP[w] + i, c * 5 : c * 5 + 4, :]
                    xr[c, row + 4 : row + 8, :] = nd[x, VEL[w] + i, c * 5 : c * 5 + 4, :]
        x = jnp.concatenate([xr[c] for c in range(4)], axis=1)
        y = lax.dot_general(
            jnp.concatenate(split3(x), axis=0), perm_v[...], (((1,), (1,)), ((), ())),
            preferred_element_type=F32,
        )
        out_v[w] = (y[0:96] + y[96:192] + y[192:288]).reshape(12, 8, 512)

    def gather():
        for j in range(1, 4):
            remote(fg_own, fgb.at[j, 0:32], g_send.at[1], g_recv.at[j], (s, 0)).wait_recv()
        for j in range(4):
            remote(fg_own.at[0:8], fgb.at[j, 32:40], g_send.at[0], g_recv.at[4 + j], (sm, 0)).wait_recv()
        fgb[0, 0:32, :] = fg_own[...]
        x = jnp.concatenate([fgb[j] for j in range(4)], axis=1)
        y = jnp.dot(jnp.concatenate(split3(x), axis=0), perm_v[...], preferred_element_type=F32)
        y = y[0:40] + y[40:80] + y[80:120]
        for a in range(5):
            for c in range(4):
                fgn[pl.ds(a * 4 + c, 8, stride=24), :] = y[a * 8 : a * 8 + 8, c * 128 : c * 128 + 128]

    for t in range(STEPS):
        receive(0, t)
        update(0)
        if t < STEPS - 1:
            step(0, t + 1)
        sample(t)
        if t == 0:
            pl.when(d == 0)(gather)
        forcing(t)
        if t < STEPS - 1:
            if t > 0:
                memory(1, False)
        else:
            memory(1, True)
            finish(0)
        receive(1, t)
        update(1)
        if t < STEPS - 1:
            step(1, t + 1)
            memory(0, t == STEPS - 2)
        else:
            finish(1)
    forward_wait((0, 1, 2))

    @pl.when(relay)
    def _():
        far_from_relay.wait_send()

    far.wait_send()

    @pl.when(d != 0)
    def _():
        remote(fg_own, fgb.at[d, 0:32], g_send.at[1], g_recv.at[d], (s, 0)).wait_send()
    for w in range(2):
        for t in range(STEPS):
            wait_all(w, t, "wait_send")


def write_kernel(mem, out_v, ug_o, vg_o, rg_o, uc_o, vc_o, rc_o, sem):
    pairs = [
        (mem.at[0, :, 0:25], rg_o.at[:, :, 0]),
        (mem.at[1, :, 0:25], rc_o.at[:, :, 0]),
        (out_v.at[0, :, 0:4], ug_o),
        (out_v.at[0, :, 4:8], vg_o),
        (out_v.at[1, :, 0:4], uc_o),
        (out_v.at[1, :, 4:8], vc_o),
    ]
    copies = [pltpu.make_async_copy(src, dst, sem.at[j]) for j, (src, dst) in enumerate(pairs)]
    for copy in copies:
        copy.start()
    for copy in copies:
        copy.wait()


def body(*args):
    (ug, vg, rg, uc, vc, rc, lam, mu, defect, keep, rho, hist, cells, filt) = args
    gradient, force = operators()
    operands = (
        ug.reshape(12, 4, 512), vg.reshape(12, 4, 512), rg.reshape(75, 25, 1, 128),
        uc.reshape(12, 4, 512), vc.reshape(12, 4, 512), rc.reshape(75, 25, 1, 128),
        lam.reshape(5, 25, 1, 128), mu.reshape(5, 25, 1, 128), defect.reshape(5, 25, 1, 128),
        keep, rho, hist, cells, filt.T,
        jnp.asarray(interleave()), jnp.asarray(gradient), jnp.asarray(force), jnp.asarray(tables()),
    )
    operands = tuple(
        pltpu.with_memory_space_constraint(x, pltpu.HBM) for x in operands
    )
    in_hbm = pl.BlockSpec(memory_space=pltpu.HBM)
    in_vmem = pl.BlockSpec(memory_space=pltpu.VMEM)
    in_specs = [in_hbm] * len(operands)
    nodal = pltpu.HBM((12, 4, 512), F32)
    points = pltpu.HBM((75, 25, 1, 128), F32)
    dma = pltpu.SemaphoreType.DMA
    vm = lambda *shape: pltpu.VMEM(shape, F32)
    waves = 2 * STEPS
    results = pl.pallas_call(
        kernel,
        out_shape=(vm(2, 75, 32, 128), vm(2, 12, 8, 512)),
        in_specs=in_specs,
        out_specs=(in_vmem,) * 2,
        scratch_shapes=[
            vm(12, 8, 512), vm(12, 8, 512), vm(4, 8, 512),
            pltpu.VMEM((512, 512), BF16), pltpu.VMEM((96, 96), BF16), pltpu.VMEM((32, 256), BF16),
            vm(5, 32, 128),
            vm(2, 25, 32, 128), vm(2, 25, 32, 128),
            vm(5, 32, 128), vm(5, 32, 128), vm(5, 32, 128), vm(5, 24, 128),
            vm(5, SLOTS, 24, 128), vm(5, 3, 24, 128), vm(2, STEPS, 5, 3, 24, 128),
            vm(waves, 4, 16, 128),
            vm(waves, 64, 128), vm(waves, 64, 128),
            vm(waves, 3, 24, 128), vm(waves, 3, 24, 128),
            vm(waves, 64, 128), vm(waves, 64, 128), vm(waves, 4, 16, 128),
            vm(48, 128), vm(48, 128), vm(112, 128), vm(48, 128), vm(48, 128), vm(112, 128),
            vm(16, 128), vm(16, 128), vm(32, 128), vm(SLOTS, 24, 128), vm(16, 128), vm(16, 128), vm(32, 128),
            vm(8, 128),
            vm(4, 72, 128), pltpu.VMEM((4, 128), jnp.int32), vm(64, 256),
            vm(32, 128), vm(4, 40, 128), vm(192, 128), vm(STEPS, 24, 128), vm(24, 128),
            vm(4, 96, 128),
            pltpu.SMEM((3,), F32), dma((24,)), pltpu.SemaphoreType.REGULAR, dma((1,)), dma((1,)),
            dma((3, 3)), dma((3, 3)), dma((3, 2)), dma((3, 2)), dma((waves, 8)), dma((waves, 8)),
            dma((2,)), dma((8,)),
        ],
        compiler_params=pltpu.CompilerParams(
            collective_id=0, has_side_effects=True, vmem_limit_bytes=40 * 1024 * 1024
        ),
    )(*operands)
    outs = pl.pallas_call(
        write_kernel,
        out_shape=(nodal, nodal, points, nodal, nodal, points),
        in_specs=(in_vmem,) * 2,
        out_specs=(in_hbm,) * 6,
        scratch_shapes=[dma((6,))],
        compiler_params=pltpu.CompilerParams(vmem_limit_bytes=1024 * 1024),
    )(*(pltpu.with_memory_space_constraint(x, pltpu.VMEM) for x in results))
    full = (3, 5, 5, 5, 5, 1, 1, 128)
    u = (3, 4, 4, 512)
    return (
        outs[0].reshape(u), outs[1].reshape(u), outs[2].reshape(full),
        outs[3].reshape(u), outs[4].reshape(u), outs[5].reshape(full),
    )


def solution(mesh):
    nodal = P(None, "slab", "depth", None)
    points = P(None, None, None, None, None, "slab", "depth", None)
    material = P(None, None, None, "slab", "depth", None)
    return jax.shard_map(
        body,
        mesh=mesh,
        in_specs=(
            nodal, nodal, points, nodal, nodal, points, material, material, material, P(),
            P("slab", "depth", None), P(None, "slab", "depth"), P("slab", "depth"), P(),
        ),
        out_specs=(nodal, nodal, points, nodal, nodal, points),
        check_vma=False,
    )
```

```python
import functools

import jax
import jax.numpy as jnp
import ml_dtypes
import numpy as np
from jax import lax
from jax.experimental import pallas as pl
from jax.experimental.pallas import tpu as pltpu
from jax.sharding import PartitionSpec as P

STEPS = 4
TAPS = 64
DT = 0.04
F32 = jnp.float32
BF16 = jnp.bfloat16
MESH = pl.DeviceIdType.MESH
ROW = 8

DISP = (0, 3)
VEL = (6, 9)
RHO = 12
SLOTS = 13


def gll_tables():
    points = np.array([-1.0, -np.sqrt(3.0 / 7.0), 0.0, np.sqrt(3.0 / 7.0), 1.0])
    weights = np.array([0.1, 49.0 / 90.0, 32.0 / 45.0, 49.0 / 90.0, 0.1])
    products = np.array([np.prod([points[t] - points[o] for o in range(5) if o != t]) for t in range(5)])
    derivative = np.zeros((5, 5))
    for t in range(5):
        for s in range(5):
            if t == s:
                derivative[t, s] = np.sum([1.0 / (points[t] - points[o]) for o in range(5) if o != t])
            else:
                derivative[t, s] = products[t] / products[s] / (points[t] - points[s])
    return derivative, weights


DMAT, WGLL = gll_tables()


def node_row(b, c):
    return c * 5 + b if c < 4 else 24 + b


def halves(matrix):
    high = matrix.astype(ml_dtypes.bfloat16)
    low = (matrix - high.astype(np.float64)).astype(ml_dtypes.bfloat16)
    return high, low


def operators():
    same = np.zeros((32, 32))
    along_y = np.zeros((32, 32))
    along_z = np.zeros((32, 32))
    for b in range(5):
        for c in range(5):
            row = b * 5 + c
            same[row, node_row(b, c)] = 1.0
            for q in range(5):
                along_y[row, node_row(q, c)] = DMAT[b, q]
                along_z[row, node_row(b, q)] = DMAT[c, q]
    high, low = halves(np.concatenate([same, along_y, along_z], axis=0))
    gradient = np.concatenate([high, high, low], axis=1)
    y_high, y_low = halves(along_y.T)
    z_high, z_low = halves(along_z.T)
    back = same.T.astype(ml_dtypes.bfloat16)
    force = np.concatenate([y_high, z_high, y_high, z_high, y_low, z_low, back, back], axis=1)
    return gradient, force


def tables():
    table = np.zeros((5, 32, 128), np.float32)
    wn = np.array([0.2, 49.0 / 90.0, 32.0 / 45.0, 49.0 / 90.0, 0.2])
    for b in range(5):
        for c in range(5):
            table[0, b * 5 + c] = WGLL[b] * WGLL[c]
        for c in range(4):
            row = node_row(b, c)
            table[1, row] = 1.0 / (wn[b] * wn[c])
            table[2, row] = float(b == 0)
            table[3, row] = float(b == 4)
    table[4, 20:] = 1.0
    return table


def interleave():
    table = np.zeros((512, 512), np.float32)
    for c in range(4):
        for e in range(128):
            table[4 * e + c, c * 128 + e] = 1.0
    return table.astype(ml_dtypes.bfloat16)


def split2(x):
    high = x.astype(BF16)
    return high, (x - high.astype(F32)).astype(BF16)


def split3(x):
    high = x.astype(BF16)
    rest = x - high.astype(F32)
    middle = rest.astype(BF16)
    return high, middle, (rest - middle.astype(F32)).astype(BF16)


def derive(x, matrix):
    even = [x[0] + x[4], x[1] + x[3]]
    odd = [x[0] - x[4], x[1] - x[3]]
    out = [None] * 5
    for p in range(2):
        s = sum(float(0.5 * (matrix[p, q] - matrix[p, 4 - q])) * odd[q] for q in range(2))
        t = sum(float(0.5 * (matrix[p, q] + matrix[p, 4 - q])) * even[q] for q in range(2))
        t = t + float(matrix[p, 2]) * x[2]
        out[p] = s + t
        out[4 - p] = s - t
    out[2] = sum(float(matrix[2, q]) * odd[q] for q in range(2))
    return out


def to_nodes(xr, perm):
    x = jnp.concatenate([xr[c] for c in range(4)], axis=1)
    y = lax.dot_general(
        jnp.concatenate(split3(x), axis=0), perm[...], (((1,), (1,)), ((), ())), preferred_element_type=F32
    )
    return (y[0:96] + y[96:192] + y[192:288]).reshape(12, 8, 512)


def kernel(
    ug, vg, rg, uc, vc, rc, lam, mu, defect, keep, rho, hist, cells, filt, perm, opg, opf, table,
    mem, out_v, xr, perm_v,
    pair_u, pair_v, pair_r, opg_v, opf_v, tab_v,
    sw, qs, lam_v, mu_v, def_v, inv_mass,
    nd, ft, fs, cr, yp, ym, rxm, rxp, rym, ryp, rdg,
    hy0, hy1, hy2, ry0, ry1, ry2, rc0, rc1, rc2, rlp, rl0, rl1, rl2, rlf,
    hist_v, cells_v, filt_v, fg_own, fgb, fgn, sj, frc,
    keep_s, lsem, ready, r_send, r_recv, h_send, h_recv, l_send, l_recv, f_send, f_recv, g_send, g_recv,
):
    s = lax.axis_index("slab")
    d = lax.axis_index("depth")
    ns = lax.axis_size("slab")
    nd_ = lax.axis_size("depth")
    sp, sm = lax.rem(s + 1, ns), lax.rem(s + ns - 1, ns)
    dp, dm = d + 1, d - 1

    barrier = pltpu.get_barrier_semaphore()

    def greet(*target):
        pl.semaphore_signal(barrier, inc=1, device_id=target, device_id_type=MESH)

    has_low, has_top = d > 0, d < nd_ - 1

    head, relay, tail = (lax.rem(s, ROW) == k for k in (0, 1, ROW - 1))
    not_head, not_tail = jnp.logical_not(head), jnp.logical_not(tail)
    row_before, row_after = lax.rem(s + ns - ROW + 1, ns), lax.rem(s + ROW - 1, ns)

    @pl.when(relay)
    def _():
        greet(row_after, d)

        @pl.when(has_top)
        def _():
            greet(row_after, dp)

    @pl.when(tail)
    def _():
        greet(s - (ROW - 2), d)

        @pl.when(d == 0)
        def _():
            for k in (1, 2, 3):
                greet(s - (ROW - 2), k)

    @pl.when(not_tail)
    def _():
        @pl.when(d == 0)
        def _():
            for k in (3, 2):
                greet(sp, k)

        @pl.when(has_low)
        def _():
            greet(sp, dm)

        @pl.when(has_top)
        def _():
            greet(sp, dp)

        greet(sp, d)

    @pl.when(d == 0)
    def _():
        for k in (3, 2):
            greet(s, k)

    @pl.when(has_low)
    def _():
        greet(sm, dm)
        greet(s, dm)

    @pl.when(has_top)
    def _():
        greet(sm, dp)
        greet(s, dp)

    greet(sm, d)
    low_n, top_n, far_n = (flag.astype(jnp.int32) for flag in (has_low, has_top, d >= 2))
    usual = 2 + 3 * low_n + 3 * top_n + 2 * far_n
    peers = jnp.where(
        head,
        2 + 3 * low_n + 2 * top_n + far_n,
        usual + relay.astype(jnp.int32) * (1 + low_n),
    )

    loads = []

    def load(src, dst):
        copy = pltpu.make_async_copy(src, dst, lsem.at[len(loads)])
        copy.start()
        loads.append(copy)
        return copy

    l_ug = load(ug, pair_u.at[:, 0:4])
    l_uc = load(uc, pair_u.at[:, 4:8])
    l_perm = load(perm, perm_v)
    l_opg = load(opg, opg_v)
    l_tab = load(table, tab_v)
    l_vg = load(vg, pair_v.at[:, 0:4])
    l_vc = load(vc, pair_v.at[:, 4:8])
    l_rho = load(rho, pair_r.at[:, 0:4])
    l_opf = load(opf, opf_v)
    zero7 = jnp.zeros((7, 128), F32)
    for w in range(2):
        for k in range(75):
            mem[w, k, 25:32, :] = zero7
    for a in range(5):
        lam_v[a, 25:32, :] = zero7
        mu_v[a, 25:32, :] = zero7
        def_v[a, 25:32, :] = zero7
    for x in range(4):
        hist_v[x, 64:72, :] = jnp.zeros((8, 128), F32)
    l_lam = load(lam.at[:, :, 0], lam_v.at[:, 0:25])
    l_mu = load(mu.at[:, :, 0], mu_v.at[:, 0:25])
    l_rg = load(rg.at[:, :, 0], mem.at[0, :, 0:25])
    l_def = load(defect.at[:, :, 0], def_v.at[:, 0:25])
    l_keep = load(keep, keep_s)
    l_cells = load(cells, cells_v)
    l_filt = load(filt, filt_v)
    l_hist = [load(hist.at[:, x], hist_v.at[x, 0:64]) for x in range(4)]
    l_rc = load(rc.at[:, :, 0], mem.at[1, :, 0:25])

    @pl.when(tail)
    def _():
        pl.semaphore_wait(barrier, peers)

        def announce(*target):
            pl.semaphore_signal(ready, inc=1, device_id=target, device_id_type=MESH)

        announce(sp, d)

        @pl.when(has_low)
        def _():
            announce(sp, dm)

        @pl.when(has_top)
        def _():
            announce(sp, dp)

    zero24 = jnp.zeros((24, 128), F32)
    for a in range(4):
        for k in range(SLOTS):
            nd[a, k] = zero24
    for q in range(8):
        fgn[pl.ds(q * 24, 24), :] = zero24

    def deinterleave(ref, blocks):
        rows = blocks * 8
        x = ref[...].reshape(rows, 512)
        y = jnp.dot(jnp.concatenate(split3(x), axis=0), perm_v[...], preferred_element_type=F32)
        return y[0:rows] + y[rows : 2 * rows] + y[2 * rows : 3 * rows]

    l_perm.wait()
    l_ug.wait()
    l_uc.wait()
    y = deinterleave(pair_u, 12)
    for k in range(12):
        for c in range(4):
            lanes = slice(c * 128, c * 128 + 128)
            nd[k % 4, DISP[0] + k // 4, c * 5 : c * 5 + 4, :] = y[k * 8 : k * 8 + 4, lanes]
            nd[k % 4, DISP[1] + k // 4, c * 5 : c * 5 + 4, :] = y[k * 8 + 4 : k * 8 + 8, lanes]
    for a in range(4):
        for k in range(3):
            row = a * 12 + k * 4
            hy0[row : row + 4, :] = nd[a, k, pl.ds(0, 4, stride=5), :]
            hy1[row : row + 4, :] = nd[a, 3 + k, pl.ds(0, 4, stride=5), :]

    @pl.when(not_tail)
    def _():
        pl.semaphore_wait(barrier, peers)

    def remote(src, dst, send, recv, target):
        return pltpu.make_async_remote_copy(
            src_ref=src, dst_ref=dst, send_sem=send, recv_sem=recv, device_id=target, device_id_type=MESH
        )

    groups = [
        (slice(0, 3), hy0, ry0, rc0, rl0),
        (slice(3, 6), hy1, ry1, rc1, rl1),
        (slice(6, 13), hy2, ry2, rc2, rl2),
    ]

    def halo(g):
        slots, rows, recv_rows, corner, relay_corner = groups[g]
        size = corner.shape[0]
        side_src, corner_src = nd.at[0, slots], rows.at[0:size]
        below = remote(rows, recv_rows, h_send.at[g, 0], h_recv.at[g, 0], (s, dm))
        side = remote(side_src, nd.at[4, slots], h_send.at[g, 1], h_recv.at[g, 1], (sm, d))
        edge = remote(corner_src, corner, h_send.at[g, 2], h_recv.at[g, 2], (sm, dm))
        to_relay = (
            remote(side_src, rlp.at[slots], h_send.at[g, 1], l_recv.at[g, 0], (row_before, d)),
            remote(corner_src, relay_corner, h_send.at[g, 2], l_recv.at[g, 1], (row_before, dm)),
        )
        end = s + (ROW - 2)
        from_relay = (
            remote(rlp.at[slots], nd.at[4, slots], l_send.at[g, 0], h_recv.at[g, 1], (end, d)),
            remote(relay_corner, corner, l_send.at[g, 1], h_recv.at[g, 2], (end, d)),
        )
        return below, side, edge, to_relay, from_relay

    def halo_start(g):
        below, side, edge, to_relay, _ = halo(g)

        @pl.when(head)
        def _():
            to_relay[0].start()

            @pl.when(has_low)
            def _():
                to_relay[1].start()

        @pl.when(not_head)
        def _():
            side.start()

            @pl.when(has_low)
            def _():
                edge.start()

        @pl.when(has_low)
        def _():
            below.start()

    def forward(gs):
        @pl.when(relay)
        def _():
            for g in gs:
                _, _, _, to_relay, from_relay = halo(g)
                to_relay[0].wait_recv()
                from_relay[0].start()

                @pl.when(has_top)
                def _():
                    to_relay[1].wait_recv()
                    from_relay[1].start()

    def forward_wait(gs):
        @pl.when(relay)
        def _():
            for g in gs:
                from_relay = halo(g)[4]
                from_relay[0].wait_send()

                @pl.when(has_top)
                def _():
                    from_relay[1].wait_send()

    def halo_wait(g):
        below, side, edge, _, _ = halo(g)
        side.wait()

        @pl.when(has_low)
        def _():
            below.wait_send()
            edge.wait_send()

        @pl.when(has_top)
        def _():
            below.wait_recv()
            edge.wait_recv()

    halo_start(0)
    halo_start(1)
    forward((0, 1))

    l_vg.wait()
    l_vc.wait()
    l_rho.wait()
    y = deinterleave(pair_v, 12)
    for k in range(12):
        for c in range(4):
            lanes = slice(c * 128, c * 128 + 128)
            nd[k % 4, VEL[0] + k // 4, c * 5 : c * 5 + 4, :] = y[k * 8 : k * 8 + 4, lanes]
            nd[k % 4, VEL[1] + k // 4, c * 5 : c * 5 + 4, :] = y[k * 8 + 4 : k * 8 + 8, lanes]
    y = deinterleave(pair_r, 4)
    for k in range(4):
        for c in range(4):
            nd[k, RHO, c * 5 : c * 5 + 4, :] = y[k * 8 : k * 8 + 4, c * 128 : c * 128 + 128]
    for a in range(4):
        for k in range(7):
            row = a * 28 + k * 4
            hy2[row : row + 4, :] = nd[a, 6 + k, pl.ds(0, 4, stride=5), :]
    halo_start(2)

    @pl.when(d == nd_ - 1)
    def _():
        for ref in (ry0, ry1, ry2, rc0, rc1, rc2):
            ref[...] = jnp.ones(ref.shape, F32)
        for n in range(2 * STEPS):
            rym[n] = jnp.zeros((64, 128), F32)
            rdg[n, 0] = jnp.zeros((16, 128), F32)
            rdg[n, 2] = jnp.zeros((16, 128), F32)

    @pl.when(d == 0)
    def _():
        for n in range(2 * STEPS):
            ryp[n] = jnp.zeros((64, 128), F32)
            rdg[n, 1] = jnp.zeros((16, 128), F32)
            rdg[n, 3] = jnp.zeros((16, 128), F32)

    l_tab.wait()
    l_lam.wait()
    l_mu.wait()
    l_def.wait()
    weight_bc = tab_v[0]
    for a in range(5):
        weight = weight_bc * float(WGLL[a])
        two_mu = 2.0 * mu_v[a]
        lam_v[a] = weight * lam_v[a]
        mu_v[a] = weight * two_mu
        def_v[a] = two_mu * def_v[a]

    def relaxed(w):
        for a in range(5):
            weight = weight_bc * float(WGLL[a])
            for k in range(5):
                j = k * 5 + a
                sw[w, j] = weight * (mem[w, j] + mem[w, 25 + j] + mem[w, 50 + j])

    l_rg.wait()
    relaxed(0)

    l_cells.wait()
    l_filt.wait()
    for copy in l_hist:
        copy.wait()
    filt3 = jnp.concatenate(split3(filt_v[...]), axis=0)
    ids = lax.broadcasted_iota(jnp.int32, (256, 128), 0)
    for x in range(4):
        one_hot = jnp.where(ids == cells_v[x : x + 1, :], 1.0, 0.0).astype(BF16)
        g = jnp.dot(filt3, one_hot, preferred_element_type=F32)
        g = g[0:64] + g[64:128] + g[128:192]
        for t in range(4):
            fg_own[x * 8 + t : x * 8 + t + 1, :] = jnp.sum(
                g * hist_v[x, t + 1 : t + 65, :], axis=0, keepdims=True
            )
            fg_own[x * 8 + 4 + t : x * 8 + 5 + t, :] = g[63 - t : 64 - t]
    far = remote(fg_own.at[0:8], fgb.at[d, 32:40], g_send.at[0], g_recv.at[4 + d], (sm, 0))
    far_to_relay = remote(fg_own.at[0:8], rlf, g_send.at[0], r_recv.at[0], (row_before, d))
    far_from_relay = remote(rlf, fgb.at[d, 32:40], r_send.at[0], g_recv.at[4 + d], (s + (ROW - 2), 0))

    @pl.when(not_head)
    def _():
        far.start()

    @pl.when(head)
    def _():
        far_to_relay.start()

    @pl.when(d != 0)
    def _():
        remote(fg_own, fgb.at[d, 0:32], g_send.at[1], g_recv.at[d], (s, 0)).start()

    def strain_stress(w, t):
        opg_m = opg_v[...]
        comps = []
        for i in range(3):
            columns = []
            for a in range(5):
                u = nd[a, DISP[w] + i]
                u = jnp.concatenate([u, pltpu.roll(u[0:8], 127, 1)], axis=0)
                high, low = split2(u)
                columns.append(jnp.concatenate([high, low, high], axis=0))
            g = jnp.dot(opg_m, jnp.concatenate(columns, axis=1), preferred_element_type=F32)
            lanes = [slice(a * 128, a * 128 + 128) for a in range(5)]
            gx = derive([g[0:32, l] for l in lanes], DMAT)
            comps.append((gx, [g[32:64, l] for l in lanes], [g[64:96, l] for l in lanes]))
        fluxes = []
        for a in range(5):
            gx = [comps[i][0][a] for i in range(3)]
            gy = [comps[i][1][a] for i in range(3)]
            gz = [comps[i][2][a] for i in range(3)]
            xy = 0.5 * (gy[0] + gx[1])
            xz = 0.5 * (gz[0] + gx[2])
            yz = 0.5 * (gz[1] + gy[2])
            trace = gx[0] + gy[1] + gz[2]
            third = trace * (1.0 / 3.0)
            m, q = mu_v[a], def_v[a]
            for k, e in enumerate((gx[0] - third, gy[1] - third, xy, xz, yz)):
                qs[w, k * 5 + a] = q * e
            pressure = lam_v[a] * trace
            r = [sw[w, k * 5 + a] for k in range(5)]
            sxx = pressure + m * gx[0] - r[0]
            syy = pressure + m * gy[1] - r[1]
            szz = pressure + m * gz[2] + (r[0] + r[1])
            sxy = m * xy - r[2]
            sxz = m * xz - r[3]
            syz = m * yz - r[4]
            fluxes.append(((sxx, sxy, sxz), (sxy, syy, syz), (sxz, syz, szz)))
        flux_x = [derive([fluxes[a][0][i] for a in range(5)], DMAT.T) for i in range(3)]

        def force(planes):
            columns = []
            for a in planes:
                for i in range(3):
                    y_high, y_low = split2(fluxes[a][1][i])
                    z_high, z_low = split2(fluxes[a][2][i])
                    x_high, x_low = split2(flux_x[i][a])
                    columns.append(
                        jnp.concatenate([y_high, z_high, y_low, z_low, y_high, z_high, x_high, x_low], axis=0)
                    )
            f = jnp.dot(opf_v[...], jnp.concatenate(columns, axis=1), preferred_element_type=F32)
            for k, a in enumerate(planes):
                for i in range(3):
                    lane = (k * 3 + i) * 128
                    fa = f[:, lane : lane + 128]
                    fs[w, t, a, i, 0:8, :] = fa[0:8] + pltpu.roll(fa[24:32], 1, 1)
                    fs[w, t, a, i, 8:24, :] = fa[8:24]

        return force

    below = (d < nd_ - 1).astype(F32)

    def messages(w, t):
        n = w * STEPS + t
        low = [
            (cr.at[n, 0, 0:12], rdg.at[n, 0, 0:12], (sm, dm)),
            (cr.at[n, 2, 0:12], rdg.at[n, 2, 0:12], (sp, dm)),
            (ym.at[n, 0:60], rym.at[n, 0:60], (s, dm)),
        ]
        top = [
            (cr.at[n, 1, 0:12], rdg.at[n, 1, 0:12], (sm, dp)),
            (cr.at[n, 3, 0:12], rdg.at[n, 3, 0:12], (sp, dp)),
            (yp.at[n, 0:60], ryp.at[n, 0:60], (s, dp)),
        ]
        side = [
            (fs.at[w, t, 0, :, 0:20], rxm.at[n, :, 0:20], (sm, d)),
            (fs.at[w, t, 4, :, 0:20], rxp.at[n, :, 0:20], (sp, d)),
        ]
        made = []
        for base, group in ((0, low), (3, top), (6, side)):
            made.append(
                [
                    remote(src, dst, f_send.at[n, base + j], f_recv.at[n, base + j], target)
                    for j, (src, dst, target) in enumerate(group)
                ]
            )
        return made

    def start_outer(w, t):
        low, top, side = messages(w, t)

        @pl.when(has_low)
        def _():
            for copy in low[:2]:
                copy.start()

        @pl.when(has_top)
        def _():
            for copy in top[:2]:
                copy.start()

        for copy in side:
            copy.start()

    def start_inner(w, t):
        low, top, _ = messages(w, t)

        @pl.when(has_low)
        def _():
            low[2].start()

        @pl.when(has_top)
        def _():
            top[2].start()

    def wait_all(w, t, name):
        low, top, side = messages(w, t)
        for copy in side:
            getattr(copy, name)()
        sent = name == "wait_send"

        @pl.when(has_low if sent else has_top)
        def _():
            for copy in low:
                getattr(copy, name)()

        @pl.when(has_top if sent else has_low)
        def _():
            for copy in top:
                getattr(copy, name)()

    def step(w, t, gate=None):
        n = w * STEPS + t
        force = strain_stress(w, t)
        force((0, 4))
        for k, a in enumerate((0, 4)):
            for i in range(3):
                for b in range(2):
                    cr[n, 2 * k + b, i * 4 : i * 4 + 4, :] = fs[w, t, a, i, pl.ds(4 * b, 4, stride=5), :]
        if gate is not None:
            gate()
        start_outer(w, t)
        force((1, 2, 3))
        for a in range(5):
            for i in range(3):
                row = a * 12 + i * 4
                ym[n, row : row + 4, :] = fs[w, t, a, i, pl.ds(0, 4, stride=5), :]
                yp[n, row : row + 4, :] = fs[w, t, a, i, pl.ds(4, 4, stride=5), :]
        start_inner(w, t)

    l_keep.wait()
    kept = [keep_s[l] for l in range(3)]

    def memory(w, last):
        for a in range(5):
            weight = weight_bc * float(WGLL[a])
            for k in range(5):
                j = k * 5 + a
                q = qs[w, j]
                new = []
                for l in range(3):
                    value = kept[l] * mem[w, 25 * l + j] + (1.0 - kept[l]) * q
                    mem[w, 25 * l + j] = value
                    new.append(value)
                if not last:
                    sw[w, j] = weight * (new[0] + new[1] + new[2])

    def receive(w, t):
        n = w * STEPS + t
        wait_all(w, t, "wait_recv")
        for a in range(5):
            for i in range(3):
                f = fs[w, t, a, i]
                if a == 0:
                    f = f + rxp[n, i]
                if a == 4:
                    f = f + rxm[n, i]
                ft[a, i] = f
        for a in range(5):
            for i in range(3):
                row = a * 12 + i * 4
                low = ryp[n, row : row + 4, :]
                top = rym[n, row : row + 4, :]
                if a == 4:
                    low = low + rdg[n, 1, i * 4 : i * 4 + 4, :]
                    top = top + rdg[n, 0, i * 4 : i * 4 + 4, :]
                if a == 0:
                    low = low + rdg[n, 3, i * 4 : i * 4 + 4, :]
                    top = top + rdg[n, 2, i * 4 : i * 4 + 4, :]
                if w == 1 and i == 1:
                    low = low - frc[a * 4 : a * 4 + 4, :]
                at_low = (a, i, pl.ds(0, 4, stride=5), slice(None))
                at_top = (a, i, pl.ds(4, 4, stride=5), slice(None))
                ft[at_low] = ft[at_low] + low
                ft[at_top] = ft[at_top] + top

    def update(w):
        for a in range(5):
            scale = inv_mass[a]
            for i in range(3):
                v = nd[a, VEL[w] + i] - scale * ft[a, i]
                nd[a, VEL[w] + i] = v
                nd[a, DISP[w] + i] = nd[a, DISP[w] + i] + DT * v

    def sample(t):
        for a in range(5):
            sj[t, a * 4 : a * 4 + 4, :] = nd[a, DISP[0] + 1, pl.ds(0, 4, stride=5), :]

    def forcing(t):
        f = fgn[t * 24 : t * 24 + 24, :]
        for m in range(t + 1):
            f = f + fgn[(4 + m) * 24 : (5 + m) * 24, :] * sj[t - m]
        frc[...] = f

    def fill(g, count):
        slots, _, recv_rows, corner, _ = groups[g]
        first = slots.start
        for a in range(5):
            for k in range(count):
                row = (a * count + k) * 4
                top = corner[k * 4 : k * 4 + 4, :] if a == 4 else recv_rows[row : row + 4, :]
                nd[a, first + k, pl.ds(4, 4, stride=5), :] = top if first + k == RHO else below * top

    halo_wait(0)
    fill(0, 3)
    l_opg.wait()
    l_opf.wait()

    def gate():
        @pl.when(head)
        def _():
            pl.semaphore_wait(ready, 1 + low_n + top_n)

    step(0, 0, gate)

    forward((2,))

    @pl.when(relay)
    def _():
        far_to_relay.wait_recv()
        far_from_relay.start()

    l_rc.wait()
    relaxed(1)
    halo_wait(1)
    fill(1, 3)
    step(1, 0)
    memory(0, False)
    halo_wait(2)
    fill(2, 7)
    first = (d == 0).astype(F32)
    row_factor = tab_v[1, 0:24] * (1.0 + first * tab_v[2, 0:24] - (1.0 - below) * tab_v[3, 0:24])
    for a in range(5):
        wx = float([0.2, 49.0 / 90.0, 32.0 / 45.0, 49.0 / 90.0, 0.2][a])
        inv_mass[a] = (DT / wx) * row_factor / (nd[a, RHO] + tab_v[4, 0:24])

    memory(1, False)

    def finish(w):
        for i in range(3):
            for x in range(4):
                row = (i * 4 + x) * 8
                for c in range(4):
                    xr[c, row : row + 4, :] = nd[x, DISP[w] + i, c * 5 : c * 5 + 4, :]
                    xr[c, row + 4 : row + 8, :] = nd[x, VEL[w] + i, c * 5 : c * 5 + 4, :]
        if w == 0:
            out_v[...] = to_nodes(xr, perm_v)

    def gather():
        for j in range(1, 4):
            remote(fg_own, fgb.at[j, 0:32], g_send.at[1], g_recv.at[j], (s, 0)).wait_recv()
        for j in range(4):
            remote(fg_own.at[0:8], fgb.at[j, 32:40], g_send.at[0], g_recv.at[4 + j], (sm, 0)).wait_recv()
        fgb[0, 0:32, :] = fg_own[...]
        x = jnp.concatenate([fgb[j] for j in range(4)], axis=1)
        y = jnp.dot(jnp.concatenate(split3(x), axis=0), perm_v[...], preferred_element_type=F32)
        y = y[0:40] + y[40:80] + y[80:120]
        for a in range(5):
            for c in range(4):
                fgn[pl.ds(a * 4 + c, 8, stride=24), :] = y[a * 8 : a * 8 + 8, c * 128 : c * 128 + 128]

    for t in range(STEPS):
        receive(0, t)
        update(0)
        if t < STEPS - 1:
            step(0, t + 1)
        sample(t)
        if t == 0:
            pl.when(d == 0)(gather)
        forcing(t)
        if t < STEPS - 1:
            if t > 0:
                memory(1, False)
        else:
            memory(1, True)
            finish(0)
        receive(1, t)
        update(1)
        if t < STEPS - 1:
            step(1, t + 1)
            memory(0, t == STEPS - 2)
        else:
            finish(1)
    forward_wait((0, 1, 2))

    @pl.when(relay)
    def _():
        far_from_relay.wait_send()

    far.wait_send()

    @pl.when(d != 0)
    def _():
        remote(fg_own, fgb.at[d, 0:32], g_send.at[1], g_recv.at[d], (s, 0)).wait_send()
    for w in range(2):
        for t in range(STEPS):
            wait_all(w, t, "wait_send")


def write_kernel(mem, out_v, xr, perm_v, ug_o, vg_o, rg_o, uc_o, vc_o, rc_o, last_v, sem):
    pairs = [
        (mem.at[0, :, 0:25], rg_o.at[:, :, 0]),
        (mem.at[1, :, 0:25], rc_o.at[:, :, 0]),
        (out_v.at[:, 0:4], ug_o),
        (out_v.at[:, 4:8], vg_o),
        (last_v.at[:, 0:4], uc_o),
        (last_v.at[:, 4:8], vc_o),
    ]
    copies = [pltpu.make_async_copy(src, dst, sem.at[j]) for j, (src, dst) in enumerate(pairs)]
    for copy in copies[:4]:
        copy.start()
    last_v[...] = to_nodes(xr, perm_v)
    for copy in copies[4:]:
        copy.start()
    for copy in copies:
        copy.wait()


def body(*args):
    (ug, vg, rg, uc, vc, rc, lam, mu, defect, keep, rho, hist, cells, filt) = args
    gradient, force = operators()
    operands = (
        ug.reshape(12, 4, 512), vg.reshape(12, 4, 512), rg.reshape(75, 25, 1, 128),
        uc.reshape(12, 4, 512), vc.reshape(12, 4, 512), rc.reshape(75, 25, 1, 128),
        lam.reshape(5, 25, 1, 128), mu.reshape(5, 25, 1, 128), defect.reshape(5, 25, 1, 128),
        keep, rho, hist, cells, filt.T,
        jnp.asarray(interleave()), jnp.asarray(gradient), jnp.asarray(force), jnp.asarray(tables()),
    )
    operands = tuple(
        pltpu.with_memory_space_constraint(x, pltpu.HBM) for x in operands
    )
    in_hbm = pl.BlockSpec(memory_space=pltpu.HBM)
    in_vmem = pl.BlockSpec(memory_space=pltpu.VMEM)
    in_specs = [in_hbm] * len(operands)
    nodal = pltpu.HBM((12, 4, 512), F32)
    points = pltpu.HBM((75, 25, 1, 128), F32)
    dma = pltpu.SemaphoreType.DMA
    vm = lambda *shape: pltpu.VMEM(shape, F32)
    waves = 2 * STEPS
    results = pl.pallas_call(
        kernel,
        out_shape=(vm(2, 75, 32, 128), vm(12, 8, 512), vm(4, 96, 128), pltpu.VMEM((512, 512), BF16)),
        in_specs=in_specs,
        out_specs=(in_vmem,) * 4,
        scratch_shapes=[
            vm(12, 8, 512), vm(12, 8, 512), vm(4, 8, 512),
            pltpu.VMEM((96, 96), BF16), pltpu.VMEM((32, 256), BF16),
            vm(5, 32, 128),
            vm(2, 25, 32, 128), vm(2, 25, 32, 128),
            vm(5, 32, 128), vm(5, 32, 128), vm(5, 32, 128), vm(5, 24, 128),
            vm(5, SLOTS, 24, 128), vm(5, 3, 24, 128), vm(2, STEPS, 5, 3, 24, 128),
            vm(waves, 4, 16, 128),
            vm(waves, 64, 128), vm(waves, 64, 128),
            vm(waves, 3, 24, 128), vm(waves, 3, 24, 128),
            vm(waves, 64, 128), vm(waves, 64, 128), vm(waves, 4, 16, 128),
            vm(48, 128), vm(48, 128), vm(112, 128), vm(48, 128), vm(48, 128), vm(112, 128),
            vm(16, 128), vm(16, 128), vm(32, 128), vm(SLOTS, 24, 128), vm(16, 128), vm(16, 128), vm(32, 128),
            vm(8, 128),
            vm(4, 72, 128), pltpu.VMEM((4, 128), jnp.int32), vm(64, 256),
            vm(32, 128), vm(4, 40, 128), vm(192, 128), vm(STEPS, 24, 128), vm(24, 128),
            pltpu.SMEM((3,), F32), dma((24,)), pltpu.SemaphoreType.REGULAR, dma((1,)), dma((1,)),
            dma((3, 3)), dma((3, 3)), dma((3, 2)), dma((3, 2)), dma((waves, 8)), dma((waves, 8)),
            dma((2,)), dma((8,)),
        ],
        compiler_params=pltpu.CompilerParams(
            collective_id=0, has_side_effects=True, vmem_limit_bytes=40 * 1024 * 1024
        ),
    )(*operands)
    outs = pl.pallas_call(
        write_kernel,
        out_shape=(nodal, nodal, points, nodal, nodal, points),
        in_specs=(in_vmem,) * 4,
        out_specs=(in_hbm,) * 6,
        scratch_shapes=[vm(12, 8, 512), dma((6,))],
        compiler_params=pltpu.CompilerParams(vmem_limit_bytes=8 * 1024 * 1024),
    )(*(pltpu.with_memory_space_constraint(x, pltpu.VMEM) for x in results))
    full = (3, 5, 5, 5, 5, 1, 1, 128)
    u = (3, 4, 4, 512)
    return (
        outs[0].reshape(u), outs[1].reshape(u), outs[2].reshape(full),
        outs[3].reshape(u), outs[4].reshape(u), outs[5].reshape(full),
    )


def solution(mesh):
    nodal = P(None, "slab", "depth", None)
    points = P(None, None, None, None, None, "slab", "depth", None)
    material = P(None, None, None, "slab", "depth", None)
    return jax.shard_map(
        body,
        mesh=mesh,
        in_specs=(
            nodal, nodal, points, nodal, nodal, points, material, material, material, P(),
            P("slab", "depth", None), P(None, "slab", "depth"), P("slab", "depth"), P(),
        ),
        out_specs=(nodal, nodal, points, nodal, nodal, points),
        check_vma=False,
    )
```
